512 devices in a mesh: tower: 4 (over y_lo), dp: 128 (over y_hi, z, x, core).
Axes of the slice: x: 4, y: 8 (y_hi: 2, y_lo: 4; y = y_hi * 4 + y_lo), z: 8, core: 2. Of those that a mesh axis runs over, the one named last changes fastest.
Arguments:
- image_in: bfloat16 [1536, 48, 1664], P('dp')
- text_in: bfloat16 [1536, 64, 1280], P('dp')
- proj_img: bfloat16 [1664, 1280], P('dp')
- proj_txt: bfloat16 [1280, 1280], P('dp')
- img_gain: float32 [1664], replicated, may hold values from 0.5 to 1.5
- txt_gain: float32 [1280], replicated, may hold values from 0.5 to 1.5
- logit_scale: float32 [1], replicated, may hold values from 60 to 100
- positive: int32 [1536], P('dp'), may hold values from 0 to 1535, each once
Outputs:
- mean_loss: float32 [1], replicated
- grad_image: bfloat16 [4, 384, 48, 1664], P('tower', 'dp')
- grad_text: bfloat16 [4, 384, 64, 1280], P('tower', 'dp')
The draws below stay inside these ranges and needn't reach their ends.
Inputs may be any that keep to these rules, and one draw needn't show every extreme that they name: positive is a permutation: every text index appears once.
All inputs are finite; a program needn't handle non-finite values.
Results may differ from the reference program's by a relative error of at most 0.0095.
Values may be sent and summed in bfloat16 or wider, within the bound.
No kernel may reach another device: no remote copies, remote signals or barrier semaphores. Data moves between devices by JAX's collectives and lax.ppermute only.
A program may use at most 128 MiB of HBM per device.

```python
import math
import jax
import jax.numpy as jnp
from jax import lax

DI = 1664
DT = 1280
EMB = 1280
IMG_TOK = 48
TXT_TOK = 64
QUARTER = 3
PAIRS = 1536
N_DP = 128


def rows_with_pattern(key, count, width):
    noise_key = jax.random.fold_in(key, 0)
    base = jax.random.normal(noise_key, (PAIRS, count, width), jnp.float32)
    return base


def draw_image_in(key, part):
    key = jax.random.fold_in(key, 11)
    return rows_with_pattern(key, IMG_TOK, DI).astype(jnp.bfloat16)


def draw_text_in(key, part):
    key = jax.random.fold_in(key, 12)
    return rows_with_pattern(key, TXT_TOK, DT).astype(jnp.bfloat16)


def draw_proj_img(key, part):
    key = jax.random.fold_in(key, 13)
    base = jax.random.normal(key, (DI, EMB), jnp.float32) / math.sqrt(DI)
    return base.astype(jnp.bfloat16)


def draw_proj_txt(key, part):
    key = jax.random.fold_in(key, 14)
    base = jax.random.normal(key, (DT, EMB), jnp.float32) / math.sqrt(DT)
    return base.astype(jnp.bfloat16)


def setup_inputs(seed: int = 0) -> dict:
    seeds = jax.random.split(jax.random.key(seed), 9)
    image_in = draw_image_in(jax.random.fold_in(seeds[8], 71), 0)
    text_in = draw_text_in(jax.random.fold_in(seeds[8], 71), 0)
    proj_img = draw_proj_img(jax.random.fold_in(seeds[8], 71), 0)
    proj_txt = draw_proj_txt(jax.random.fold_in(seeds[8], 71), 0)
    img_gain = jnp.clip(1.0 + 0.1 * jax.random.normal(seeds[4], (DI,), jnp.float32), 0.5, 1.5)
    txt_gain = jnp.clip(1.0 + 0.1 * jax.random.normal(seeds[5], (DT,), jnp.float32), 0.5, 1.5)
    logit_scale = jnp.clip(jax.random.uniform(seeds[6], (1,), jnp.float32, 60.0, 100.0), 60.0, 100.0)
    positive = jax.random.permutation(seeds[7], PAIRS).astype(jnp.int32)
    return dict(image_in=image_in, text_in=text_in, proj_img=proj_img, proj_txt=proj_txt, img_gain=img_gain, txt_gain=txt_gain, logit_scale=logit_scale, positive=positive)


def norm_tokens(token_block, gain_vector):
    values = token_block.astype(jnp.float32)
    center = values - lax.optimization_barrier(jnp.mean(values, axis=-1, keepdims=True))
    spread = lax.optimization_barrier(jnp.mean(center * center, axis=-1, keepdims=True))
    return center * lax.rsqrt(spread + 1e-05) * gain_vector

def project_rows(token_block, gain_vector, weight):
    pooled = lax.optimization_barrier(jnp.mean(norm_tokens(token_block, gain_vector), axis=1)).astype(jnp.bfloat16)
    return jnp.dot(pooled, weight, preferred_element_type=jnp.float32)

def unit_rows(projected):
    return projected * lax.rsqrt(lax.optimization_barrier(jnp.sum(projected * projected, axis=-1, keepdims=True)) + 1e-06)

def pooled_back(projected, weight, cotangent):
    _, pull_back = jax.vjp(unit_rows, projected)
    proj_cot = pull_back(cotangent)[0].astype(jnp.bfloat16)
    return lax.dot_general(proj_cot, weight, (((1,), (1,)), ((), ())), preferred_element_type=jnp.float32)

def token_back(token_block, gain_vector, pool_cot):
    spread_cot = jnp.broadcast_to(pool_cot[:, None, :], token_block.shape)
    _, pull_back = jax.vjp(lambda token_piece: norm_tokens(token_piece, gain_vector), token_block)
    return pull_back(spread_cot)[0].astype(jnp.bfloat16)

def log_total(scores, along):
    largest = lax.optimization_barrier(jnp.max(scores, axis=along, keepdims=True))
    summed = lax.optimization_barrier(jnp.sum(jnp.exp(scores - largest), axis=along, keepdims=True))
    return jnp.squeeze(largest + jnp.log(summed), axis=along)

def by_device(gradients):
    count = gradients.shape[1]
    width = gradients.shape[2]
    arranged = gradients.reshape(N_DP, 4, QUARTER, count, width).transpose(1, 0, 2, 3, 4)
    return arranged.reshape(4, N_DP * QUARTER, count, width)

def reference(image_in, text_in, proj_img, proj_txt, img_gain, txt_gain, logit_scale, positive):
    img_projected = project_rows(image_in, img_gain, proj_img)
    txt_projected = project_rows(text_in, txt_gain, proj_txt)
    img_emb = unit_rows(img_projected).astype(jnp.bfloat16)
    txt_emb = unit_rows(txt_projected).astype(jnp.bfloat16)
    logit = logit_scale[0]
    scores = logit * jnp.dot(img_emb, txt_emb.T, preferred_element_type=jnp.float32)
    row_lse = log_total(scores, 1)
    col_lse = log_total(scores, 0)
    matched = (positive[:, None] == jnp.arange(PAIRS, dtype=jnp.int32)[None, :]).astype(jnp.float32)
    pos_total = jnp.sum(matched * scores)
    mean_loss = ((jnp.sum(row_lse) + jnp.sum(col_lse) - 2.0 * pos_total) / (2.0 * PAIRS)).reshape(1)
    coef = (0.5 * logit * (jnp.exp(scores - row_lse[:, None]) + jnp.exp(scores - col_lse[None, :]) - 2.0 * matched)).astype(jnp.bfloat16)
    img_cot = jnp.dot(coef, txt_emb, preferred_element_type=jnp.float32)
    txt_cot = jnp.dot(coef.T, img_emb, preferred_element_type=jnp.float32)
    img_grads = token_back(image_in, img_gain, pooled_back(img_projected, proj_img, img_cot))
    txt_grads = token_back(text_in, txt_gain, pooled_back(txt_projected, proj_txt, txt_cot))
    return (mean_loss, by_device(img_grads), by_device(txt_grads))
```

```python
import jax
import jax.numpy as jnp
from jax import lax
from jax.sharding import Mesh, PartitionSpec as P

BF = jnp.bfloat16
F32 = jnp.float32
Y = ("h", "t")
ZX = ("z", "x")
ZXC = ("z", "x", "c")
DP = ("h", "z", "x", "c")


def norm_tokens(token_block, gain_vector):
    values = token_block.astype(F32)
    center = values - jnp.mean(values, axis=-1, keepdims=True)
    spread = jnp.mean(center * center, axis=-1, keepdims=True)
    return center * lax.rsqrt(spread + 1e-05) * gain_vector


def token_back(token_block, gain_vector, pool_cot):
    spread_cot = jnp.broadcast_to(pool_cot[:, None, :], token_block.shape)
    _, pull_back = jax.vjp(lambda token_piece: norm_tokens(token_piece, gain_vector), token_block)
    return pull_back(spread_cot)[0]


def exchange(blocks, axes):
    return lax.all_to_all(blocks, axes, 0, 0, tiled=True)


def spread_to(block, axes, count):
    return exchange(jnp.broadcast_to(block[None], (count,) + block.shape), axes)


def both_cores(blocks):
    half = blocks.shape[0] // 2
    parts = [lax.all_gather(part, "c", axis=0) for part in (blocks[:half], blocks[half:])]
    return jnp.concatenate(parts, axis=1)


def per_device(image_in, text_in, proj_img, proj_txt, img_gain, txt_gain, logit_scale, positive):
    t_index = lax.axis_index("t")
    h_index = lax.axis_index("h")
    g_index = (lax.axis_index("z") * 4 + lax.axis_index("x")) * 2 + lax.axis_index("c")
    logit = logit_scale[0]
    emb = proj_img.shape[1]
    slab_i, slab_t = proj_img.shape[0], proj_txt.shape[0]
    half_i, half_t = slab_i * 64, slab_t * 64
    own = h_index * 12 + t_index * 3

    w = jnp.pad(jnp.concatenate([proj_img, proj_txt], 0), ((0, 1), (0, 256)))
    w = lax.dynamic_slice(w, (0, 384 * t_index), (24, 384))
    w = both_cores(spread_to(w, ZX, 32)).transpose(1, 0, 2, 3)
    w_img = w[:, :, :slab_i].reshape(half_i, 384)
    w_txt = w[:, :, slab_i : slab_i + slab_t].reshape(half_t, 384)

    pooled_i = jnp.mean(norm_tokens(image_in, img_gain), axis=1).astype(BF)
    pooled_t = jnp.mean(norm_tokens(text_in, txt_gain), axis=1).astype(BF)

    def feature_half(which):
        return jnp.concatenate(
            [
                lax.dynamic_slice(pooled_i, (0, half_i * which), (12, half_i)),
                lax.dynamic_slice(pooled_t, (0, half_t * which), (12, half_t)),
            ],
            1,
        )

    mine = feature_half(h_index)
    theirs = lax.ppermute(feature_half(1 - h_index), "h", [(0, 1), (1, 0)])
    first = h_index == 0
    pooled = jnp.concatenate([jnp.where(first, mine, theirs), jnp.where(first, theirs, mine)], 0)

    part = jnp.concatenate(
        [
            jnp.dot(pooled[:, :half_i], w_img, preferred_element_type=F32),
            jnp.dot(pooled[:, half_i:], w_txt, preferred_element_type=F32),
        ],
        0,
    ).astype(BF)
    parts = spread_to(part, Y, 8).astype(F32)
    parts = parts[:4] + parts[4:]
    projected = jnp.concatenate([parts[k] for k in range(4)], 1)
    inv = lax.rsqrt(jnp.sum(projected * projected, axis=-1, keepdims=True) + 1e-06)
    unit = projected * inv
    rows = unit[:, :emb].astype(BF)

    blank = jnp.zeros((1, emb), BF)
    block = jnp.concatenate(
        [
            lax.dynamic_slice(rows, (own, 0), (3, emb)),
            blank,
            lax.dynamic_slice(rows, (24 + own, 0), (3, emb)),
            blank,
        ],
        0,
    )
    items = both_cores(spread_to(block, ZX, 32)).reshape(512, emb)
    scores = logit * lax.dot_general(
        rows, items, (((1,), (1,)), ((), ())), preferred_element_type=F32
    )

    place = lax.iota(jnp.int32, 512)
    item_g = ((place // 8) % 32) * 2 + place // 256
    item_pair = (h_index * 64 + item_g) * 12 + 3 * t_index + place % 4
    item_txt = (place % 8) // 4 == 1
    item_real = place % 4 < 3
    row = lax.iota(jnp.int32, 48)
    row_txt = row >= 24
    row_pair = (((row // 12) % 2) * 64 + g_index) * 12 + row % 12
    valid = (row_txt[:, None] != item_txt[None, :]) & item_real[None, :]
    valid_scores = jnp.where(valid, scores, -1e30)
    top = jnp.max(valid_scores, axis=1)
    total = jnp.sum(jnp.exp(valid_scores - top[:, None]), axis=1)

    seen = spread_to(
        jnp.stack([top, total, jnp.pad(positive.astype(F32), (0, 36))]), Y, 8
    )
    every_top = jnp.max(seen[:, 0], axis=0)
    row_lse = every_top + jnp.log(
        jnp.sum(seen[:, 1] * jnp.exp(seen[:, 0] - every_top[None]), axis=0)
    )
    row_pos = jnp.concatenate([seen[0, 2, :12], seen[4, 2, :12], jnp.full((24,), -1.0)])
    img_match = valid & (row_pos[:, None] == item_pair[None, :].astype(F32))
    img_lse = lax.dynamic_slice(row_lse, (own,), (3,))
    txt_lse = lax.dynamic_slice(row_lse, (24 + own,), (3,))
    part_value = (
        jnp.sum(img_lse) + jnp.sum(txt_lse) - 2.0 * jnp.sum(jnp.where(img_match, scores, 0.0))
    )
    zero = jnp.zeros((1,), F32)
    own_pos = lax.dynamic_slice(positive, (3 * t_index,), (3,)).astype(F32)
    told = spread_to(
        jnp.concatenate(
            [img_lse, zero, txt_lse, zero, own_pos, zero, part_value[None], jnp.zeros((115,), F32)]
        )[None],
        ZXC,
        64,
    )[:, 0]
    item_lse = told[:, :8].reshape(32, 2, 8).transpose(1, 0, 2).reshape(512)
    item_pos = jnp.pad(told[:, 8:12], ((0, 0), (0, 4)), constant_values=-1.0)
    item_pos = item_pos.reshape(32, 2, 8).transpose(1, 0, 2).reshape(512)
    y_value = jnp.sum(told[:, 12])

    match = img_match | (
        valid
        & row_txt[:, None]
        & (item_pos[None, :] == row_pair[:, None].astype(F32))
    )
    coef = (
        0.5
        * logit
        * (
            jnp.exp(valid_scores - row_lse[:, None])
            + jnp.exp(jnp.where(valid, scores - item_lse[None, :], -1e30))
            - 2.0 * match.astype(F32)
        )
    ).astype(BF)
    along = jnp.sum(coef.astype(F32) * scores, axis=1) / logit
    cot = jnp.dot(coef, items, preferred_element_type=F32).astype(BF)
    cot = jnp.pad(cot, ((0, 0), (0, 256)))

    def two_parts(values):
        high = values.astype(BF)
        return high, (values - high.astype(F32)).astype(BF)

    along_high, along_low = two_parts(along)
    value_high, value_low = two_parts(jnp.broadcast_to(y_value[None], (48,)))
    extra = jnp.pad(
        jnp.stack([along_high, along_low, value_high, value_low]), ((0, 4), (0, 336))
    )
    sent = jnp.stack(
        [jnp.concatenate([cot[:, 384 * k : 384 * k + 384], extra], 0) for k in (0, 1, 2, 3)] * 2
    )
    summed = jnp.sum(exchange(sent, Y).astype(F32), axis=0)
    along = summed[48, :48] + summed[49, :48]
    mean_loss = ((summed[50, :1] + summed[51, :1]) / (2.0 * 1536)).reshape(1)

    unit_part = lax.dynamic_slice(unit, (0, 384 * t_index), (48, 384))
    proj_cot = (inv * (summed[:48] - unit_part * along[:, None])).astype(BF)
    back = (((1,), (1,)), ((), ()))
    pool = jnp.concatenate(
        [
            lax.dot_general(proj_cot[:24], w_img, back, preferred_element_type=F32),
            lax.dot_general(proj_cot[24:], w_txt, back, preferred_element_type=F32),
        ],
        1,
    ).astype(BF)
    pool = exchange(pool.reshape(8, 3, half_i + half_t), Y).astype(F32)
    pool = jnp.sum(pool.reshape(2, 4, 3, half_i + half_t), axis=1)
    img_pool_cot = jnp.concatenate([pool[0, :, :half_i], pool[1, :, :half_i]], 1)
    txt_pool_cot = jnp.concatenate([pool[0, :, half_i:], pool[1, :, half_i:]], 1)
    img_own = lax.dynamic_slice_in_dim(image_in, 3 * t_index, 3, 0)
    txt_own = lax.dynamic_slice_in_dim(text_in, 3 * t_index, 3, 0)
    img_grads = token_back(img_own, img_gain, img_pool_cot)
    txt_grads = token_back(txt_own, txt_gain, txt_pool_cot)
    return (mean_loss, img_grads[None], txt_grads[None])


def solution(mesh):
    fine = Mesh(mesh.devices.reshape(4, 2, 8, 4, 2), ("t", "h", "z", "x", "c"))
    in_specs = (
        P(DP, None, None),
        P(DP, None, None),
        P(DP, None),
        P(DP, None),
        P(),
        P(),
        P(),
        P(DP),
    )
    out_specs = (P(), P("t", DP, None, None), P("t", DP, None, None))
    return jax.shard_map(
        per_device, mesh=fine, in_specs=in_specs, out_specs=out_specs, check_vma=False
    )
```

```python
import jax
import jax.numpy as jnp
from jax import lax
from jax.sharding import Mesh, PartitionSpec as P

BF = jnp.bfloat16
F32 = jnp.float32
Y = ("h", "t")
ZX = ("z", "x")
ZXC = ("z", "x", "c")
DP = ("h", "z", "x", "c")


def norm_tokens(token_block, gain_vector):
    values = token_block.astype(F32)
    center = values - jnp.mean(values, axis=-1, keepdims=True)
    spread = jnp.mean(center * center, axis=-1, keepdims=True)
    return center * lax.rsqrt(spread + 1e-05) * gain_vector


def token_back(token_block, gain_vector, pool_cot):
    spread_cot = jnp.broadcast_to(pool_cot[:, None, :], token_block.shape)
    _, pull_back = jax.vjp(lambda token_piece: norm_tokens(token_piece, gain_vector), token_block)
    return pull_back(spread_cot)[0]


def exchange(blocks, axes):
    return lax.all_to_all(blocks, axes, 0, 0, tiled=True)


def spread_to(block, axes, count):
    return exchange(jnp.broadcast_to(block[None], (count,) + block.shape), axes)


def both_cores(blocks):
    half = blocks.shape[0] // 2
    parts = [lax.all_gather(part, "c", axis=0) for part in (blocks[:half], blocks[half:])]
    return jnp.concatenate(parts, axis=1)


def per_device(image_in, text_in, proj_img, proj_txt, img_gain, txt_gain, logit_scale, positive):
    t_index = lax.axis_index("t")
    h_index = lax.axis_index("h")
    g_index = (lax.axis_index("z") * 4 + lax.axis_index("x")) * 2 + lax.axis_index("c")
    logit = logit_scale[0]
    emb = proj_img.shape[1]
    slab_i, slab_t = proj_img.shape[0], proj_txt.shape[0]
    half_i, half_t = slab_i * 64, slab_t * 64

    w = jnp.pad(jnp.concatenate([proj_img, proj_txt], 0), ((0, 1), (0, 256)))
    w = lax.dynamic_slice(w, (0, 384 * t_index), (24, 384))
    w = both_cores(spread_to(w, ZX, 32)).transpose(1, 0, 2, 3)
    w_img = w[:, :, :slab_i].reshape(half_i, 384)
    w_txt = w[:, :, slab_i : slab_i + slab_t].reshape(half_t, 384)

    pooled_i = jnp.mean(norm_tokens(image_in, img_gain), axis=1).astype(BF)
    pooled_t = jnp.mean(norm_tokens(text_in, txt_gain), axis=1).astype(BF)

    def feature_half(which):
        return jnp.concatenate(
            [
                lax.dynamic_slice(pooled_i, (0, half_i * which), (12, half_i)),
                lax.dynamic_slice(pooled_t, (0, half_t * which), (12, half_t)),
            ],
            1,
        )

    mine = feature_half(h_index)
    theirs = lax.ppermute(feature_half(1 - h_index), "h", [(0, 1), (1, 0)])
    first = h_index == 0
    pooled = jnp.concatenate([jnp.where(first, mine, theirs), jnp.where(first, theirs, mine)], 0)

    def in_blocks(img_rows, txt_rows):
        quad = lambda x: jnp.pad(x.reshape(8, 3, x.shape[1]), ((0, 0), (0, 1), (0, 0)))
        return jnp.concatenate([quad(img_rows), quad(txt_rows)], 1)

    part = in_blocks(
        jnp.dot(pooled[:, :half_i], w_img, preferred_element_type=F32).astype(BF),
        jnp.dot(pooled[:, half_i:], w_txt, preferred_element_type=F32).astype(BF),
    )
    parts = exchange(part, Y).astype(F32)
    parts = parts[:4] + parts[4:]
    projected = jnp.concatenate([parts[k] for k in range(4)], 1)[:, :emb]
    inv = lax.rsqrt(jnp.sum(projected * projected, axis=-1, keepdims=True) + 1e-06)
    unit = (projected * inv).astype(BF)

    own_pos = lax.dynamic_slice(positive, (3 * t_index,), (3,))
    digits = jnp.pad(jnp.concatenate([own_pos // 32, own_pos % 32]).astype(BF), (0, emb - 6))
    in_block = lax.iota(jnp.int32, 8)[:, None]
    block = jnp.where(in_block == 3, digits[None], unit)
    near = spread_to(block, Y, 8)
    far = both_cores(spread_to(block, ZX, 32))
    rows = near.reshape(64, emb)
    items = far.reshape(512, emb)

    def positions(blocks):
        count = blocks.shape[0]
        found = blocks[:, 3, :6].astype(F32)
        found = found[:, :3] * 32.0 + found[:, 3:]
        return jnp.pad(found, ((0, 0), (0, 5)), constant_values=-1.0).reshape(count * 8)

    row_pos = positions(near)
    item_pos = positions(far.reshape(64, 8, emb))
    scores = logit * lax.dot_general(
        rows, items, (((1,), (1,)), ((), ())), preferred_element_type=F32
    )

    place = lax.iota(jnp.int32, 512)
    item_g = ((place // 8) % 32) * 2 + place // 256
    item_pair = ((h_index * 64 + item_g) * 12 + 3 * t_index + place % 4).astype(F32)
    item_txt = (place % 8) // 4 == 1
    item_real = place % 4 < 3
    row = lax.iota(jnp.int32, 64)
    row_txt = (row % 8) // 4 == 1
    row_real = row % 4 < 3
    row_pair = ((row // 32) * 64 + g_index) * 12 + ((row // 8) % 4) * 3 + row % 4
    row_pair = row_pair.astype(F32)
    real = row_real[:, None] & item_real[None, :]
    valid = (row_txt[:, None] != item_txt[None, :]) & real
    img_match = valid & (row_pos[:, None] == item_pair[None, :])
    match = img_match | (valid & (item_pos[None, :] == row_pair[:, None]))
    valid_scores = jnp.where(valid, scores, -1e30)

    def log_total(values, axis):
        largest = jnp.max(values, axis=axis, keepdims=True)
        summed = jnp.sum(jnp.exp(values - largest), axis=axis, keepdims=True)
        return jnp.squeeze(largest + jnp.log(summed), axis)

    row_part = jnp.where(row_real, log_total(valid_scores, 1), 0.0)
    item_part = jnp.where(item_real, log_total(valid_scores, 0), 0.0)
    matched_part = jnp.sum(jnp.where(img_match, scores, 0.0))
    item_part = jnp.where(place == 3, matched_part, item_part)
    row_seen = spread_to(row_part[None], Y, 8)[:, 0]
    item_seen = spread_to(item_part[None], ZXC, 64)[:, 0]
    row_lse = log_total(row_seen, 0)
    item_lse = log_total(item_seen, 0)
    y_value = jnp.sum(jnp.where(item_real, item_lse, 0.0)) - 2.0 * jnp.sum(item_seen[:, 3])

    coef = jnp.where(
        valid,
        0.5
        * logit
        * (
            jnp.exp(valid_scores - row_lse[:, None])
            + jnp.exp(valid_scores - item_lse[None, :])
            - 2.0 * match.astype(F32)
        ),
        0.0,
    ).astype(BF)
    along = jnp.sum(coef.astype(F32) * scores, axis=1) / logit
    cot = jnp.dot(coef, items, preferred_element_type=F32).astype(BF)
    cot = jnp.pad(cot, ((0, 0), (0, 256)))

    def two_parts(values):
        high = values.astype(BF)
        return high, (values - high.astype(F32)).astype(BF)

    along_high, along_low = two_parts(along)
    value_high, value_low = two_parts(jnp.broadcast_to(y_value[None], (64,)))
    riders = jnp.pad(
        jnp.stack([along_high, along_low, value_high, value_low]), ((0, 0), (0, 320))
    )
    at = lax.iota(jnp.int32, 64)[:, None]
    extra = jnp.zeros((64, 384), BF)
    for k in range(4):
        extra = jnp.where(at == 4 * k + 3, riders[k][None], extra)
    ways = jnp.stack([cot[:, 384 * k : 384 * k + 384] + extra for k in range(4)])
    summed = jnp.sum(exchange(jnp.concatenate([ways, ways], 0), Y).astype(F32), axis=0)
    along = summed[3, :64] + summed[7, :64]
    mean_loss = ((summed[11, :1] + summed[15, :1]) / (2.0 * 1536)).reshape(1)

    rows_part = lax.dynamic_slice(
        jnp.pad(rows, ((0, 0), (0, 256))), (0, 384 * t_index), (64, 384)
    ).astype(F32)
    proj_cot = (summed - rows_part * along[:, None]).astype(BF)
    back = (((1,), (1,)), ((), ()))
    pool_i = lax.dot_general(proj_cot, w_img, back, preferred_element_type=F32).astype(BF)
    pool_t = lax.dot_general(proj_cot, w_txt, back, preferred_element_type=F32).astype(BF)
    pool = jnp.concatenate(
        [pool_i.reshape(8, 8, half_i)[:, :4], pool_t.reshape(8, 8, half_t)[:, 4:]], 2
    )
    pool = exchange(pool, Y).astype(F32)
    pool = jnp.sum(pool.reshape(2, 4, 4, half_i + half_t), axis=1)
    img_pool_cot = jnp.concatenate([pool[0, :3, :half_i], pool[1, :3, :half_i]], 1) * inv[:3]
    txt_pool_cot = jnp.concatenate([pool[0, :3, half_i:], pool[1, :3, half_i:]], 1) * inv[4:7]
    img_own = lax.dynamic_slice_in_dim(image_in, 3 * t_index, 3, 0)
    txt_own = lax.dynamic_slice_in_dim(text_in, 3 * t_index, 3, 0)
    img_grads = token_back(img_own, img_gain, img_pool_cot)
    txt_grads = token_back(txt_own, txt_gain, txt_pool_cot)
    return (mean_loss, img_grads[None], txt_grads[None])


def solution(mesh):
    fine = Mesh(mesh.devices.reshape(4, 2, 8, 4, 2), ("t", "h", "z", "x", "c"))
    in_specs = (
        P(DP, None, None),
        P(DP, None, None),
        P(DP, None),
        P(DP, None),
        P(),
        P(),
        P(),
        P(DP),
    )
    out_specs = (P(), P("t", DP, None, None), P("t", DP, None, None))
    return jax.shard_map(
        per_device, mesh=fine, in_specs=in_specs, out_specs=out_specs, check_vma=False
    )
```

```python
import jax
import jax.numpy as jnp
from jax import lax
from jax.experimental import pallas as pl
from jax.experimental.pallas import tpu as pltpu
from jax.sharding import Mesh, PartitionSpec as P

BF = jnp.bfloat16
F32 = jnp.float32
Y = ("h", "t")
ZX = ("z", "x")
ZXC = ("z", "x", "c")
DP = ("h", "z", "x", "c")
LOW = -1e30
ROWS_DOT = (((1,), (1,)), ((), ()))


def norm_tokens(token_block, gain_vector):
    values = token_block.astype(F32)
    center = values - jnp.mean(values, axis=-1, keepdims=True)
    spread = jnp.mean(center * center, axis=-1, keepdims=True)
    return center * lax.rsqrt(spread + 1e-05) * gain_vector


def token_back(token_block, gain_vector, pool_cot):
    spread_cot = jnp.broadcast_to(pool_cot[:, None, :], token_block.shape)
    _, pull_back = jax.vjp(lambda token_piece: norm_tokens(token_piece, gain_vector), token_block)
    return pull_back(spread_cot)[0]


def exchange(blocks, axes):
    return lax.all_to_all(blocks, axes, 0, 0, tiled=True)


def both_cores(blocks):
    half = blocks.shape[0] // 2
    parts = [lax.all_gather(part, "c", axis=0) for part in (blocks[:half], blocks[half:])]
    return [part.reshape(-1, blocks.shape[2]) for part in parts]


def kernel_call(body, outs, args, scratch=(), smem=()):
    vmem = pl.BlockSpec(memory_space=pltpu.VMEM)
    return pl.pallas_call(
        body,
        out_shape=[jax.ShapeDtypeStruct(shape, kind) for shape, kind in outs],
        in_specs=[
            pl.BlockSpec(memory_space=pltpu.SMEM) if k in smem else vmem for k in range(len(args))
        ],
        out_specs=[vmem] * len(outs),
        scratch_shapes=list(scratch),
        compiler_params=pltpu.CompilerParams(vmem_limit_bytes=40 * 1024 * 1024),
    )(*args)


def project_kernel(left_ref, wa_ref, wb_ref, out_ref):
    half = wa_ref.shape[0]
    part = jnp.dot(left_ref[:, :half], wa_ref[...], preferred_element_type=F32)
    part += jnp.dot(left_ref[:, half:], wb_ref[...], preferred_element_type=F32)
    part = part.astype(BF)
    for k in range(8):
        out_ref[48 * k : 48 * k + 48, :] = part


def unit_kernel(place_ref, parts_ref, digits_ref, rows_ref, far_ref, inv_ref, held, held_inv):
    spread = parts_ref[...].astype(F32)
    emb = rows_ref.shape[1]
    blocks = [spread[48 * k : 48 * k + 48] + spread[192 + 48 * k : 240 + 48 * k] for k in range(4)]
    projected = jnp.concatenate(blocks, 1)[:, :emb]
    inv = lax.rsqrt(jnp.sum(projected * projected, axis=1, keepdims=True) + 1e-06)

    def in_blocks(values):
        blank = jnp.zeros((1, values.shape[1]), F32)
        pieces = []
        for k in range(8):
            pieces += [values[6 * k : 6 * k + 3], blank, values[6 * k + 3 : 6 * k + 6], blank]
        return jnp.concatenate(pieces, 0)

    unit = in_blocks(projected * inv)
    rows_ref[...] = unit.astype(BF)
    held[...] = unit
    held_inv[...] = in_blocks(jnp.broadcast_to(inv, (48, 128)))
    own = pl.ds(pl.multiple_of(8 * place_ref[0], 8), 8)
    inv_ref[...] = held_inv[own, :]
    block = held[own, :]
    at = lax.broadcasted_iota(jnp.int32, (8, 128), 0)
    start = jnp.where(at == 3, digits_ref[...], block[:, :128])
    block = jnp.concatenate([start, block[:, 128:]], 1)
    block = jnp.concatenate([block, block], 0).astype(BF)
    for k in range(16):
        far_ref[16 * k : 16 * k + 16, :] = block


def tile_masks(place_ref):
    h, t, g = place_ref[1], place_ref[2], place_ref[3]
    row = lax.broadcasted_iota(jnp.int32, (64, 512), 0)
    item = lax.broadcasted_iota(jnp.int32, (64, 512), 1)
    item_g = ((item // 256) * 16 + (item % 128) // 8) * 2 + (item // 128) % 2
    item_pair = (h * 64 + item_g) * 12 + 3 * t + item % 4
    row_pair = ((row // 32) * 64 + g) * 12 + ((row // 8) % 4) * 3 + row % 4
    row_txt, item_txt = (row % 8) // 4, (item % 8) // 4
    valid = (row_txt != item_txt) & (row % 4 < 3) & (item % 4 < 3)
    return valid, row_pair, item_pair, row_txt, item


def square_mask():
    down = lax.broadcasted_iota(jnp.int32, (64, 128), 0)
    along = lax.broadcasted_iota(jnp.int32, (64, 128), 1)
    return down == along


def as_lanes(column):
    return jnp.sum(jnp.where(square_mask(), column, 0.0), axis=0, keepdims=True)


def as_column(lanes):
    return jnp.sum(jnp.where(square_mask(), lanes, 0.0), axis=1, keepdims=True)


def log_total(values, axis):
    largest = jnp.max(values, axis=axis, keepdims=True)
    return largest + jnp.log(jnp.sum(jnp.exp(values - largest), axis=axis, keepdims=True))


def score_kernel(
    place_ref, logit_ref, rows_ref, fa_ref, fb_ref, row_pos_ref, scores_ref, near_ref, far_ref
):
    rows = rows_ref[...]
    scores = jnp.concatenate(
        [
            lax.dot_general(rows, ref[...], ROWS_DOT, preferred_element_type=F32)
            for ref in (fa_ref, fb_ref)
        ],
        1,
    )
    scores = logit_ref[0] * scores
    scores_ref[...] = scores
    valid, _, item_pair, row_txt, _ = tile_masks(place_ref)
    masked = jnp.where(valid, scores, LOW)
    row_part = as_lanes(log_total(masked, 1))
    near_ref[...] = jnp.broadcast_to(row_part, (8, 128))
    item_part = log_total(masked, 0)
    hit = valid & (row_txt == 0) & (row_pos_ref[...] == item_pair)
    matched = jnp.sum(
        jnp.sum(jnp.where(hit, scores, 0.0), axis=1, keepdims=True), axis=0, keepdims=True
    )
    lane = lax.broadcasted_iota(jnp.int32, (1, 512), 1)
    item_part = jnp.where(lane == 3, matched, item_part)
    lines = jnp.concatenate([item_part[:, 128 * k : 128 * k + 128] for k in range(4)] * 2, 0)
    for k in range(32):
        far_ref[8 * k : 8 * k + 8, :] = lines


def coef_kernel(
    place_ref,
    logit_ref,
    scores_ref,
    near_ref,
    far_ref,
    row_pos_ref,
    item_pos_ref,
    fa_ref,
    fb_ref,
    out_ref,
):
    logit = logit_ref[0]
    scores = scores_ref[...]
    row_lse = as_column(log_total(near_ref[...], 0))
    seen = far_ref[...].reshape(32, 8, 128)
    largest = jnp.max(seen, axis=0)
    largest = jnp.maximum(largest[:4], largest[4:])
    both = jnp.concatenate([largest, largest], 0)
    total = jnp.sum(jnp.exp(seen - both[None]), axis=0)
    lines = largest + jnp.log(total[:4] + total[4:])
    item_lse = jnp.concatenate([lines[k : k + 1] for k in range(4)], 1)
    summed = jnp.sum(seen, axis=0)
    summed = summed[:1] + summed[4:5]
    valid, row_pair, item_pair, row_txt, item = tile_masks(place_ref)
    from_img = row_txt == 0
    hit = valid & (
        jnp.where(from_img, row_pos_ref[...], row_pair)
        == jnp.where(from_img, item_pair, item_pos_ref[...])
    )
    real = item[:1] % 4 < 3
    lse_total = jnp.sum(jnp.where(real, item_lse, 0.0), axis=1, keepdims=True)
    lane = lax.broadcasted_iota(jnp.int32, (1, 128), 1)
    matched = jnp.sum(jnp.where(lane == 3, summed, 0.0), axis=1, keepdims=True)
    value = lse_total - 2.0 * matched
    masked = jnp.where(valid, scores, LOW)
    coef = (0.5 * logit) * (
        jnp.exp(masked - row_lse) + jnp.exp(masked - item_lse) - jnp.where(hit, 2.0, 0.0)
    )
    coef = jnp.where(valid, coef, 0.0).astype(BF)
    along = jnp.sum(coef.astype(F32) * scores, axis=1, keepdims=True) / logit
    cot = jnp.dot(coef[:, :256], fa_ref[...], preferred_element_type=F32)
    cot += jnp.dot(coef[:, 256:], fb_ref[...], preferred_element_type=F32)

    riders = []
    for lanes in (as_lanes(along), jnp.broadcast_to(value, (1, 128))):
        high = lanes.astype(BF).astype(F32)
        riders += [high, lanes - high]
    at = lax.broadcasted_iota(jnp.int32, (64, 128), 0)
    extra = jnp.zeros((64, 128), F32)
    for k in range(4):
        extra = jnp.where(at == 4 * k + 3, riders[k], extra)
    blank = jnp.zeros((64, 256), F32)
    extra = jnp.concatenate([extra, blank], 1)
    cot = jnp.concatenate([cot, blank], 1)
    for k in range(4):
        way = (cot[:, 384 * k : 384 * k + 384] + extra).astype(BF)
        out_ref[64 * k : 64 * k + 64, :] = way
        out_ref[256 + 64 * k : 320 + 64 * k, :] = way


def back_kernel(got_ref, unit_ref, wa_ref, wb_ref, out_ref, loss_ref):
    summed = got_ref[:64, :].astype(F32)
    for k in range(1, 8):
        summed += got_ref[64 * k : 64 * k + 64, :].astype(F32)
    along = as_column(summed[3:4, :128] + summed[7:8, :128])
    loss_ref[...] = jnp.broadcast_to(
        (summed[11:12, :128] + summed[15:16, :128]) / (2.0 * 1536), (8, 128)
    )
    proj_cot = (summed - unit_ref[...].astype(F32) * along).astype(BF)
    a, b = [
        lax.dot_general(proj_cot, ref[...], ROWS_DOT, preferred_element_type=F32)
        for ref in (wa_ref, wb_ref)
    ]
    is_img = lax.broadcasted_iota(jnp.int32, a.shape, 1) % 24 < 13
    first = lax.broadcasted_iota(jnp.int32, a.shape, 0) % 8 < 4
    a = jnp.where(is_img, a, pltpu.roll(a, 60, 0))
    b = jnp.where(is_img, pltpu.roll(b, 4, 0), b)
    out_ref[...] = jnp.where(first, a, b).astype(BF)


def per_device(image_in, text_in, proj_img, proj_txt, img_gain, txt_gain, logit_scale, positive):
    t_index = lax.axis_index("t")
    h_index = lax.axis_index("h")
    g_index = (lax.axis_index("z") * 4 + lax.axis_index("x")) * 2 + lax.axis_index("c")
    y_index = h_index * 4 + t_index
    place = jnp.stack([y_index, h_index, t_index, g_index]).astype(jnp.int32)
    emb = proj_img.shape[1]

    w = jnp.pad(jnp.concatenate([proj_img, proj_txt], 0), ((0, 1), (0, 256)))
    w = lax.dynamic_slice(w, (0, 384 * t_index), (24, 384))
    wa, wb = both_cores(exchange(jnp.broadcast_to(w[None], (32, 24, 384)), ZX))

    pooled_i = jnp.mean(norm_tokens(image_in, img_gain), axis=1).astype(BF)
    pooled_t = jnp.mean(norm_tokens(text_in, txt_gain), axis=1).astype(BF)
    slabs = jnp.concatenate(
        [
            pooled_i.reshape(12, 128, 13),
            pooled_t.reshape(12, 128, 10),
            jnp.zeros((12, 128, 1), BF),
        ],
        2,
    )
    slabs = slabs.reshape(12, 2, 2, 16, 2, 24).transpose(0, 1, 2, 4, 3, 5).reshape(12, 2, 1536)
    first = h_index == 0
    mine = jnp.where(first, slabs[:, 0], slabs[:, 1])
    theirs = jnp.where(first, slabs[:, 1], slabs[:, 0])
    digits = jnp.stack([positive // 32, positive % 32], 1).astype(BF)
    spot = lax.iota(jnp.int32, 1536)[None, :]
    theirs = jnp.where(spot == 23, digits[:, :1], jnp.where(spot == 47, digits[:, 1:], theirs))
    theirs = lax.ppermute(theirs, "h", [(0, 1), (1, 0)])
    pooled = jnp.concatenate([jnp.where(first, mine, theirs), jnp.where(first, theirs, mine)], 0)
    own_pos = positive.astype(F32)
    their_pos = theirs[:, 23].astype(F32) * 32.0 + theirs[:, 47].astype(F32)
    row_pos = jnp.concatenate(
        [jnp.where(first, own_pos, their_pos), jnp.where(first, their_pos, own_pos)]
    )
    row_pos = jnp.pad(row_pos.reshape(8, 3), ((0, 0), (0, 5)), constant_values=-1.0)
    row_pos = row_pos.reshape(64, 1).astype(jnp.int32)
    is_img = spot % 24 < 13
    is_txt = (spot % 24 >= 13) & (spot % 24 < 23)
    left = jnp.stack(
        [
            jnp.where(is_img, pooled, 0).reshape(8, 3, 1536),
            jnp.where(is_txt, pooled, 0).reshape(8, 3, 1536),
        ],
        1,
    ).reshape(48, 1536)

    (part,) = kernel_call(project_kernel, [((384, 384), BF)], [left, wa, wb])
    parts = exchange(part.reshape(8, 48, 384), Y).reshape(384, 384)

    own_digits = lax.dynamic_slice(positive, (3 * t_index,), (3,))
    own_digits = jnp.concatenate([own_digits // 32, own_digits % 32]).astype(F32)
    own_digits = jnp.pad(own_digits, (0, 122))[None]
    rows, far, inv = kernel_call(
        unit_kernel,
        [((64, emb), BF), ((256, emb), BF), ((8, 128), F32)],
        [place, parts, own_digits],
        scratch=[pltpu.VMEM((64, emb), F32), pltpu.VMEM((64, 128), F32)],
        smem=(0,),
    )
    fa, fb = both_cores(exchange(far.reshape(32, 8, emb), ZX))

    scores, near, far = kernel_call(
        score_kernel,
        [((64, 512), F32), ((8, 128), F32), ((256, 128), F32)],
        [place, logit_scale, rows, fa, fb, row_pos],
        smem=(0, 1),
    )
    near = exchange(near.reshape(8, 1, 128), Y).reshape(8, 128)
    far = exchange(far.reshape(64, 4, 128), ZXC).reshape(256, 128)

    item_pos = jnp.concatenate([fa.reshape(32, 8, emb)[:, 3, :6], fb.reshape(32, 8, emb)[:, 3, :6]])
    item_pos = item_pos.astype(F32)
    item_pos = item_pos[:, :3] * 32.0 + item_pos[:, 3:]
    item_pos = jnp.pad(item_pos, ((0, 0), (0, 5)), constant_values=-1.0).reshape(1, 512)
    item_pos = item_pos.astype(jnp.int32)
    (ways,) = kernel_call(
        coef_kernel,
        [((512, 384), BF)],
        [place, logit_scale, scores, near, far, row_pos, item_pos, fa, fb],
        smem=(0, 1),
    )
    got = exchange(ways.reshape(8, 64, 384), Y).reshape(512, 384)
    unit_part = lax.dynamic_slice(
        jnp.pad(rows, ((0, 0), (0, 256))), (0, 384 * t_index), (64, 384)
    )
    pool, loss = kernel_call(
        back_kernel, [((64, 768), BF), ((8, 128), F32)], [got, unit_part, wa, wb]
    )
    mean_loss = loss[0, :1]
    pool = exchange(pool.reshape(8, 8, 768), Y).astype(F32)
    pool = jnp.sum(pool.reshape(2, 4, 2, 4, 2, 16, 24), axis=1)
    pool = pool.transpose(2, 0, 1, 4, 3, 5)[:3].reshape(3, 128, 24)
    img_pool_cot = pool[:, :, :13].reshape(3, -1) * inv[:3, :1]
    txt_pool_cot = pool[:, :, 13:23].reshape(3, -1) * inv[4:7, :1]
    img_own = lax.dynamic_slice_in_dim(image_in, 3 * t_index, 3, 0)
    txt_own = lax.dynamic_slice_in_dim(text_in, 3 * t_index, 3, 0)
    img_grads = token_back(img_own, img_gain, img_pool_cot)
    txt_grads = token_back(txt_own, txt_gain, txt_pool_cot)
    return (mean_loss, img_grads[None], txt_grads[None])


def solution(mesh):
    fine = Mesh(mesh.devices.reshape(4, 2, 8, 4, 2), ("t", "h", "z", "x", "c"))
    in_specs = (
        P(DP, None, None),
        P(DP, None, None),
        P(DP, None),
        P(DP, None),
        P(),
        P(),
        P(),
        P(DP),
    )
    out_specs = (P(), P("t", DP, None, None), P("t", DP, None, None))
    return jax.shard_map(
        per_device, mesh=fine, in_specs=in_specs, out_specs=out_specs, check_vma=False
    )
```

```python
import jax
import jax.numpy as jnp
from jax import lax
from jax.experimental import pallas as pl
from jax.experimental.pallas import tpu as pltpu
from jax.sharding import Mesh, PartitionSpec as P

BF = jnp.bfloat16
F32 = jnp.float32
Y = ("h", "t")
ZX = ("z", "x")
ZXC = ("z", "x", "c")
DP = ("h", "z", "x", "c")
LOW = -1e30
ROWS_DOT = (((1,), (1,)), ((), ()))


def norm_tokens(token_block, gain_vector):
    values = token_block.astype(F32)
    center = values - jnp.mean(values, axis=-1, keepdims=True)
    spread = jnp.mean(center * center, axis=-1, keepdims=True)
    return center * lax.rsqrt(spread + 1e-05) * gain_vector


def exchange(blocks, axes):
    return lax.all_to_all(blocks, axes, 0, 0, tiled=True)


def both_cores(blocks):
    half = blocks.shape[0] // 2
    parts = [lax.all_gather(part, "c", axis=0) for part in (blocks[:half], blocks[half:])]
    return [part.reshape(-1, blocks.shape[2]) for part in parts]


def kernel_call(body, outs, args, scratch=(), smem=()):
    vmem = pl.BlockSpec(memory_space=pltpu.VMEM)
    return pl.pallas_call(
        body,
        out_shape=[jax.ShapeDtypeStruct(shape, kind) for shape, kind in outs],
        in_specs=[
            pl.BlockSpec(memory_space=pltpu.SMEM) if k in smem else vmem for k in range(len(args))
        ],
        out_specs=[vmem] * len(outs),
        scratch_shapes=list(scratch),
        compiler_params=pltpu.CompilerParams(vmem_limit_bytes=40 * 1024 * 1024),
    )(*args)


def project_kernel(left_ref, wa_ref, wb_ref, out_ref):
    half = wa_ref.shape[0]
    part = jnp.dot(left_ref[:, :half], wa_ref[...], preferred_element_type=F32)
    part += jnp.dot(left_ref[:, half:], wb_ref[...], preferred_element_type=F32)
    part = part.astype(BF)
    for k in range(8):
        out_ref[48 * k : 48 * k + 48, :] = part


def unit_kernel(place_ref, parts_ref, digits_ref, rows_ref, far_ref, inv_ref, held, held_inv):
    spread = parts_ref[...].astype(F32)
    emb = rows_ref.shape[1]
    blocks = [spread[48 * k : 48 * k + 48] + spread[192 + 48 * k : 240 + 48 * k] for k in range(4)]
    projected = jnp.concatenate(blocks, 1)[:, :emb]
    inv = lax.rsqrt(jnp.sum(projected * projected, axis=1, keepdims=True) + 1e-06)

    def in_blocks(values):
        blank = jnp.zeros((1, values.shape[1]), F32)
        pieces = []
        for k in range(8):
            pieces += [values[6 * k : 6 * k + 3], blank, values[6 * k + 3 : 6 * k + 6], blank]
        return jnp.concatenate(pieces, 0)

    unit = in_blocks(projected * inv)
    rows_ref[...] = unit.astype(BF)
    held[...] = unit
    held_inv[...] = in_blocks(jnp.broadcast_to(inv, (48, 128)))
    own = pl.ds(pl.multiple_of(8 * place_ref[0], 8), 8)
    inv_ref[...] = held_inv[own, :]
    block = held[own, :]
    at = lax.broadcasted_iota(jnp.int32, (8, 128), 0)
    start = jnp.where(at == 3, digits_ref[...], block[:, :128])
    block = jnp.concatenate([start, block[:, 128:]], 1)
    block = jnp.concatenate([block, block], 0).astype(BF)
    for k in range(16):
        far_ref[16 * k : 16 * k + 16, :] = block


def tile_masks(place_ref):
    h, t, g = place_ref[1], place_ref[2], place_ref[3]
    row = lax.broadcasted_iota(jnp.int32, (64, 512), 0)
    item = lax.broadcasted_iota(jnp.int32, (64, 512), 1)
    item_g = ((item // 256) * 16 + (item % 128) // 8) * 2 + (item // 128) % 2
    item_pair = (h * 64 + item_g) * 12 + 3 * t + item % 4
    row_pair = ((row // 32) * 64 + g) * 12 + ((row // 8) % 4) * 3 + row % 4
    row_txt, item_txt = (row % 8) // 4, (item % 8) // 4
    valid = (row_txt != item_txt) & (row % 4 < 3) & (item % 4 < 3)
    return valid, row_pair, item_pair, row_txt, item


def square_mask():
    down = lax.broadcasted_iota(jnp.int32, (64, 128), 0)
    along = lax.broadcasted_iota(jnp.int32, (64, 128), 1)
    return down == along


def as_lanes(column):
    return jnp.sum(jnp.where(square_mask(), column, 0.0), axis=0, keepdims=True)


def as_column(lanes):
    return jnp.sum(jnp.where(square_mask(), lanes, 0.0), axis=1, keepdims=True)


def log_total(values, axis):
    largest = jnp.max(values, axis=axis, keepdims=True)
    return largest + jnp.log(jnp.sum(jnp.exp(values - largest), axis=axis, keepdims=True))


def score_kernel(
    place_ref, logit_ref, rows_ref, fa_ref, fb_ref, row_pos_ref, scores_ref, near_ref, far_ref
):
    rows = rows_ref[...]
    scores = jnp.concatenate(
        [
            lax.dot_general(rows, ref[...], ROWS_DOT, preferred_element_type=F32)
            for ref in (fa_ref, fb_ref)
        ],
        1,
    )
    scores = logit_ref[0] * scores
    scores_ref[...] = scores
    valid, _, item_pair, row_txt, _ = tile_masks(place_ref)
    masked = jnp.where(valid, scores, LOW)
    row_part = as_lanes(log_total(masked, 1))
    near_ref[...] = jnp.broadcast_to(row_part, (8, 128))
    item_part = log_total(masked, 0)
    hit = valid & (row_txt == 0) & (row_pos_ref[...] == item_pair)
    matched = jnp.sum(
        jnp.sum(jnp.where(hit, scores, 0.0), axis=1, keepdims=True), axis=0, keepdims=True
    )
    lane = lax.broadcasted_iota(jnp.int32, (1, 512), 1)
    item_part = jnp.where(lane == 3, matched, item_part)
    lines = jnp.concatenate([item_part[:, 128 * k : 128 * k + 128] for k in range(4)] * 2, 0)
    for k in range(32):
        far_ref[8 * k : 8 * k + 8, :] = lines


def coef_kernel(
    place_ref,
    logit_ref,
    scores_ref,
    near_ref,
    far_ref,
    row_pos_ref,
    item_pos_ref,
    fa_ref,
    fb_ref,
    out_ref,
):
    logit = logit_ref[0]
    scores = scores_ref[...]
    row_lse = as_column(log_total(near_ref[...], 0))
    seen = far_ref[...].reshape(32, 8, 128)
    largest = jnp.max(seen, axis=0)
    largest = jnp.maximum(largest[:4], largest[4:])
    both = jnp.concatenate([largest, largest], 0)
    total = jnp.sum(jnp.exp(seen - both[None]), axis=0)
    lines = largest + jnp.log(total[:4] + total[4:])
    item_lse = jnp.concatenate([lines[k : k + 1] for k in range(4)], 1)
    summed = jnp.sum(seen, axis=0)
    summed = summed[:1] + summed[4:5]
    valid, row_pair, item_pair, row_txt, item = tile_masks(place_ref)
    from_img = row_txt == 0
    hit = valid & (
        jnp.where(from_img, row_pos_ref[...], row_pair)
        == jnp.where(from_img, item_pair, item_pos_ref[...])
    )
    real = item[:1] % 4 < 3
    lse_total = jnp.sum(jnp.where(real, item_lse, 0.0), axis=1, keepdims=True)
    lane = lax.broadcasted_iota(jnp.int32, (1, 128), 1)
    matched = jnp.sum(jnp.where(lane == 3, summed, 0.0), axis=1, keepdims=True)
    value = lse_total - 2.0 * matched
    masked = jnp.where(valid, scores, LOW)
    coef = (0.5 * logit) * (
        jnp.exp(masked - row_lse) + jnp.exp(masked - item_lse) - jnp.where(hit, 2.0, 0.0)
    )
    coef = jnp.where(valid, coef, 0.0).astype(BF)
    along = jnp.sum(coef.astype(F32) * scores, axis=1, keepdims=True) / logit
    cot = jnp.dot(coef[:, :256], fa_ref[...], preferred_element_type=F32)
    cot += jnp.dot(coef[:, 256:], fb_ref[...], preferred_element_type=F32)

    riders = []
    for lanes in (as_lanes(along), jnp.broadcast_to(value, (1, 128))):
        high = lanes.astype(BF).astype(F32)
        riders += [high, lanes - high]
    at = lax.broadcasted_iota(jnp.int32, (64, 128), 0)
    extra = jnp.zeros((64, 128), F32)
    for k in range(4):
        extra = jnp.where(at == 4 * k + 3, riders[k], extra)
    blank = jnp.zeros((64, 256), F32)
    extra = jnp.concatenate([extra, blank], 1)
    cot = jnp.concatenate([cot, blank], 1)
    for k in range(4):
        way = (cot[:, 384 * k : 384 * k + 384] + extra).astype(BF)
        out_ref[64 * k : 64 * k + 64, :] = way
        out_ref[256 + 64 * k : 320 + 64 * k, :] = way


def back_kernel(got_ref, unit_ref, wa_ref, wb_ref, out_ref, loss_ref):
    summed = got_ref[:64, :].astype(F32)
    for k in range(1, 8):
        summed += got_ref[64 * k : 64 * k + 64, :].astype(F32)
    along = as_column(summed[3:4, :128] + summed[7:8, :128])
    loss_ref[...] = jnp.broadcast_to(
        (summed[11:12, :128] + summed[15:16, :128]) / (2.0 * 1536), (8, 128)
    )
    proj_cot = (summed - unit_ref[...].astype(F32) * along).astype(BF)
    a, b = [
        lax.dot_general(proj_cot, ref[...], ROWS_DOT, preferred_element_type=F32)
        for ref in (wa_ref, wb_ref)
    ]
    is_img = lax.broadcasted_iota(jnp.int32, a.shape, 1) % 24 < 13
    first = lax.broadcasted_iota(jnp.int32, a.shape, 0) % 8 < 4
    a = jnp.where(is_img, a, pltpu.roll(a, 60, 0))
    b = jnp.where(is_img, pltpu.roll(b, 4, 0), b)
    out_ref[...] = jnp.where(first, a, b).astype(BF)


def token_kernel(pool_ref, inv_ref, img_ref, txt_ref, ig_ref, tg_ref, img_out, txt_out):
    pool = pool_ref[...]
    inv = inv_ref[...][:, :1]
    for x_ref, gain_ref, out_ref, wide, skip, at in (
        (img_ref, ig_ref, img_out, 13, 0, 0),
        (txt_ref, tg_ref, txt_out, 10, 13, 4),
    ):
        dense = lax.broadcasted_iota(jnp.int32, (1, 32 * wide), 1)
        place = ((dense // wide) % 2) * 384 + (dense // (2 * wide)) * 24 + skip + dense % wide
        lane = lax.broadcasted_iota(jnp.int32, (768, 32 * wide), 0)
        pick = jnp.where(lane == place, 1.0, 0.0).astype(BF)
        found = jnp.dot(pool, pick, preferred_element_type=F32)
        halves = [
            found[32 * k : 32 * k + 8]
            + found[32 * k + 8 : 32 * k + 16]
            + found[32 * k + 16 : 32 * k + 24]
            + found[32 * k + 24 : 32 * k + 32]
            for k in range(2)
        ]
        cot = jnp.concatenate([halves[0][:4], halves[0][4:], halves[1][:4], halves[1][4:]], 1)
        cot = cot * inv[at : at + 4] * gain_ref[...]
        mean_cot = jnp.mean(cot, axis=1, keepdims=True)
        count = x_ref.shape[0] // 3
        for q in range(3):
            span = slice(count * q, count * q + count)
            values = x_ref[span, :].astype(F32)
            center = values - jnp.mean(values, axis=1, keepdims=True)
            inner = lax.rsqrt(jnp.mean(center * center, axis=1, keepdims=True) + 1e-05)
            mine = cot[q : q + 1]
            along = jnp.mean(center * mine, axis=1, keepdims=True)
            out = inner * (mine - mean_cot[q : q + 1]) - center * (inner * inner * inner * along)
            out_ref[span, :] = out.astype(BF)


def per_device(image_in, text_in, proj_img, proj_txt, img_gain, txt_gain, logit_scale, positive):
    t_index = lax.axis_index("t")
    h_index = lax.axis_index("h")
    g_index = (lax.axis_index("z") * 4 + lax.axis_index("x")) * 2 + lax.axis_index("c")
    y_index = h_index * 4 + t_index
    place = jnp.stack([y_index, h_index, t_index, g_index]).astype(jnp.int32)
    emb = proj_img.shape[1]

    w = jnp.pad(jnp.concatenate([proj_img, proj_txt], 0), ((0, 1), (0, 256)))
    w = lax.dynamic_slice(w, (0, 384 * t_index), (24, 384))
    wa, wb = both_cores(exchange(jnp.broadcast_to(w[None], (32, 24, 384)), ZX))

    pooled_i = jnp.mean(norm_tokens(image_in, img_gain), axis=1).astype(BF)
    pooled_t = jnp.mean(norm_tokens(text_in, txt_gain), axis=1).astype(BF)
    slabs = jnp.concatenate(
        [
            pooled_i.reshape(12, 128, 13),
            pooled_t.reshape(12, 128, 10),
            jnp.zeros((12, 128, 1), BF),
        ],
        2,
    )
    slabs = slabs.reshape(12, 2, 2, 16, 2, 24).transpose(0, 1, 2, 4, 3, 5).reshape(12, 2, 1536)
    digits = jnp.stack([positive // 32, positive % 32], 1).astype(BF)[:, :, None]
    spot = lax.iota(jnp.int32, 1536)[None, :]
    slabs = jnp.where(spot == 23, digits[:, :1], jnp.where(spot == 47, digits[:, 1:], slabs))
    both = lax.all_gather(slabs.transpose(1, 0, 2), "h", axis=0)
    pooled = lax.dynamic_index_in_dim(both, h_index, 1, keepdims=False).reshape(24, 1536)
    row_pos = pooled[:, 23].astype(F32) * 32.0 + pooled[:, 47].astype(F32)
    row_pos = jnp.pad(row_pos.reshape(8, 3), ((0, 0), (0, 5)), constant_values=-1.0)
    row_pos = row_pos.reshape(64, 1).astype(jnp.int32)
    is_img = spot % 24 < 13
    is_txt = (spot % 24 >= 13) & (spot % 24 < 23)
    left = jnp.stack(
        [
            jnp.where(is_img, pooled, 0).reshape(8, 3, 1536),
            jnp.where(is_txt, pooled, 0).reshape(8, 3, 1536),
        ],
        1,
    ).reshape(48, 1536)

    (part,) = kernel_call(project_kernel, [((384, 384), BF)], [left, wa, wb])
    parts = exchange(part.reshape(8, 48, 384), Y).reshape(384, 384)

    own_digits = lax.dynamic_slice(positive, (3 * t_index,), (3,))
    own_digits = jnp.concatenate([own_digits // 32, own_digits % 32]).astype(F32)
    own_digits = jnp.pad(own_digits, (0, 122))[None]
    rows, far, inv = kernel_call(
        unit_kernel,
        [((64, emb), BF), ((256, emb), BF), ((8, 128), F32)],
        [place, parts, own_digits],
        scratch=[pltpu.VMEM((64, emb), F32), pltpu.VMEM((64, 128), F32)],
        smem=(0,),
    )
    fa, fb = both_cores(exchange(far.reshape(32, 8, emb), ZX))

    scores, near, far = kernel_call(
        score_kernel,
        [((64, 512), F32), ((8, 128), F32), ((256, 128), F32)],
        [place, logit_scale, rows, fa, fb, row_pos],
        smem=(0, 1),
    )
    near = exchange(near.reshape(8, 1, 128), Y).reshape(8, 128)
    far = exchange(far.reshape(64, 4, 128), ZXC).reshape(256, 128)

    item_pos = jnp.concatenate([fa.reshape(32, 8, emb)[:, 3, :6], fb.reshape(32, 8, emb)[:, 3, :6]])
    item_pos = item_pos.astype(F32)
    item_pos = item_pos[:, :3] * 32.0 + item_pos[:, 3:]
    item_pos = jnp.pad(item_pos, ((0, 0), (0, 5)), constant_values=-1.0).reshape(1, 512)
    item_pos = item_pos.astype(jnp.int32)
    (ways,) = kernel_call(
        coef_kernel,
        [((512, 384), BF)],
        [place, logit_scale, scores, near, far, row_pos, item_pos, fa, fb],
        smem=(0, 1),
    )
    got = exchange(ways.reshape(8, 64, 384), Y).reshape(512, 384)
    unit_part = lax.dynamic_slice(
        jnp.pad(rows, ((0, 0), (0, 256))), (0, 384 * t_index), (64, 384)
    )
    pool, loss = kernel_call(
        back_kernel, [((64, 768), BF), ((8, 128), F32)], [got, unit_part, wa, wb]
    )
    mean_loss = loss[0, :1]
    pool = exchange(pool.reshape(8, 8, 768), Y).reshape(64, 768)
    count_i, width_i = image_in.shape[1:]
    count_t, width_t = text_in.shape[1:]
    img_own = lax.dynamic_slice_in_dim(image_in, 3 * t_index, 3, 0).reshape(-1, width_i)
    txt_own = lax.dynamic_slice_in_dim(text_in, 3 * t_index, 3, 0).reshape(-1, width_t)
    img_grads, txt_grads = kernel_call(
        token_kernel,
        [(img_own.shape, BF), (txt_own.shape, BF)],
        [pool, inv, img_own, txt_own, img_gain[None], txt_gain[None]],
    )
    img_grads = img_grads.reshape(3, count_i, width_i)
    txt_grads = txt_grads.reshape(3, count_t, width_t)
    return (mean_loss, img_grads[None], txt_grads[None])


def solution(mesh):
    fine = Mesh(mesh.devices.reshape(4, 2, 8, 4, 2), ("t", "h", "z", "x", "c"))
    in_specs = (
        P(DP, None, None),
        P(DP, None, None),
        P(DP, None),
        P(DP, None),
        P(),
        P(),
        P(),
        P(DP),
    )
    out_specs = (P(), P("t", DP, None, None), P("t", DP, None, None))
    return jax.shard_map(
        per_device, mesh=fine, in_specs=in_specs, out_specs=out_specs, check_vma=False
    )
```

```python
import jax
import jax.numpy as jnp
from jax import lax
from jax.experimental import pallas as pl
from jax.experimental.pallas import tpu as pltpu
from jax.sharding import Mesh, PartitionSpec as P

BF = jnp.bfloat16
F32 = jnp.float32
Y = ("h", "t")
ZX = ("z", "x")
ZXC = ("z", "x", "c")
DP = ("h", "z", "x", "c")
LOW = -1e30
ROWS_DOT = (((1,), (1,)), ((), ()))


def norm_tokens(token_block, gain_vector):
    values = token_block.astype(F32)
    center = values - jnp.mean(values, axis=-1, keepdims=True)
    spread = jnp.mean(center * center, axis=-1, keepdims=True)
    return center * lax.rsqrt(spread + 1e-05) * gain_vector


def exchange(blocks, axes):
    return lax.all_to_all(blocks, axes, 0, 0, tiled=True)


def both_cores(blocks):
    half = blocks.shape[0] // 2
    parts = [lax.all_gather(part, "c", axis=0) for part in (blocks[:half], blocks[half:])]
    return [part.reshape(-1, blocks.shape[2]) for part in parts]


def kernel_call(body, outs, args, scratch=(), smem=()):
    vmem = pl.BlockSpec(memory_space=pltpu.VMEM)
    return pl.pallas_call(
        body,
        out_shape=[jax.ShapeDtypeStruct(shape, kind) for shape, kind in outs],
        in_specs=[
            pl.BlockSpec(memory_space=pltpu.SMEM) if k in smem else vmem for k in range(len(args))
        ],
        out_specs=[vmem] * len(outs),
        scratch_shapes=list(scratch),
        compiler_params=pltpu.CompilerParams(vmem_limit_bytes=40 * 1024 * 1024),
    )(*args)


def project_kernel(left_ref, wa_ref, wb_ref, out_ref):
    half = wa_ref.shape[0]
    part = jnp.dot(left_ref[:, :half], wa_ref[...], preferred_element_type=F32)
    part += jnp.dot(left_ref[:, half:], wb_ref[...], preferred_element_type=F32)
    part = part.astype(BF)
    for k in range(8):
        out_ref[48 * k : 48 * k + 48, :] = part


def in_blocks(values):
    blank = jnp.zeros((1, values.shape[1]), F32)
    pieces = []
    for k in range(8):
        pieces += [values[6 * k : 6 * k + 3], blank, values[6 * k + 3 : 6 * k + 6], blank]
    return jnp.concatenate(pieces, 0)


def unit_kernel(place_ref, parts_ref, digits_ref, rows_ref, far_ref, inv_ref, held, held_inv):
    spread = parts_ref[...].astype(F32)
    emb = rows_ref.shape[1]
    blocks = [spread[48 * k : 48 * k + 48] + spread[192 + 48 * k : 240 + 48 * k] for k in range(4)]
    projected = jnp.concatenate(blocks, 1)[:, :emb]
    inv = lax.rsqrt(jnp.sum(projected * projected, axis=1, keepdims=True) + 1e-06)
    unit = projected * inv
    rows_ref[...] = unit.astype(BF)
    held[...] = in_blocks(unit)
    held_inv[...] = in_blocks(jnp.broadcast_to(inv, (48, 128)))
    own = pl.ds(pl.multiple_of(8 * place_ref[0], 8), 8)
    inv_ref[...] = held_inv[own, :]
    block = held[own, :]
    at = lax.broadcasted_iota(jnp.int32, (8, 128), 0)
    start = jnp.where(at == 3, digits_ref[...], block[:, :128])
    block = jnp.concatenate([start, block[:, 128:]], 1)
    block = jnp.concatenate([block, block], 0).astype(BF)
    for k in range(16):
        far_ref[16 * k : 16 * k + 16, :] = block


def tile_masks(place_ref):
    h, t, g = place_ref[1], place_ref[2], place_ref[3]
    row = lax.broadcasted_iota(jnp.int32, (48, 512), 0)
    item = lax.broadcasted_iota(jnp.int32, (48, 512), 1)
    item_g = ((item // 256) * 16 + (item % 128) // 8) * 2 + (item // 128) % 2
    item_pair = (h * 64 + item_g) * 12 + 3 * t + item % 4
    row_pair = ((row // 24) * 64 + g) * 12 + ((row // 6) % 4) * 3 + row % 3
    row_txt, item_txt = (row % 6) // 3, (item % 8) // 4
    valid = (row_txt != item_txt) & (item % 4 < 3)
    return valid, row_pair, item_pair, row_txt, item


def square_mask():
    down = lax.broadcasted_iota(jnp.int32, (48, 128), 0)
    along = lax.broadcasted_iota(jnp.int32, (48, 128), 1)
    return down == along


def as_lanes(column):
    return jnp.sum(jnp.where(square_mask(), column, 0.0), axis=0, keepdims=True)


def as_column(lanes):
    return jnp.sum(jnp.where(square_mask(), lanes, 0.0), axis=1, keepdims=True)


def log_total(values, axis):
    largest = jnp.max(values, axis=axis, keepdims=True)
    return largest + jnp.log(jnp.sum(jnp.exp(values - largest), axis=axis, keepdims=True))


def score_kernel(place_ref, logit_ref, rows_ref, fa_ref, fb_ref, row_pos_ref, scores_ref, far_ref):
    rows = rows_ref[...]
    scores = jnp.concatenate(
        [
            lax.dot_general(rows, ref[...], ROWS_DOT, preferred_element_type=F32)
            for ref in (fa_ref, fb_ref)
        ],
        1,
    )
    scores = logit_ref[0] * scores
    scores_ref[...] = scores
    valid, _, item_pair, row_txt, _ = tile_masks(place_ref)
    masked = jnp.where(valid, scores, LOW)
    item_part = log_total(masked, 0)
    hit = valid & (row_txt == 0) & (row_pos_ref[...] == item_pair)
    matched = jnp.sum(
        jnp.sum(jnp.where(hit, scores, 0.0), axis=1, keepdims=True), axis=0, keepdims=True
    )
    lane = lax.broadcasted_iota(jnp.int32, (1, 512), 1)
    item_part = jnp.where(lane == 3, matched, item_part)
    lines = jnp.concatenate([item_part[:, 128 * k : 128 * k + 128] for k in range(4)] * 2, 0)
    for k in range(32):
        far_ref[8 * k : 8 * k + 8, :] = lines


def in_parts(values, count):
    parts = []
    for _ in range(count):
        part = values.astype(BF).astype(F32)
        parts.append(part)
        values = values - part
    return parts


def coef_kernel(
    place_ref, logit_ref, scores_ref, far_ref, row_pos_ref, item_pos_ref, fa_ref, fb_ref, out_ref
):
    logit = logit_ref[0]
    scores = scores_ref[...]
    seen = far_ref[...].reshape(32, 8, 128)
    largest = jnp.max(seen, axis=0)
    largest = jnp.maximum(largest[:4], largest[4:])
    both = jnp.concatenate([largest, largest], 0)
    total = jnp.sum(jnp.exp(seen - both[None]), axis=0)
    lines = largest + jnp.log(total[:4] + total[4:])
    item_lse = jnp.concatenate([lines[k : k + 1] for k in range(4)], 1)
    summed = jnp.sum(seen, axis=0)
    summed = summed[:1] + summed[4:5]
    valid, row_pair, item_pair, row_txt, item = tile_masks(place_ref)
    from_img = row_txt == 0
    hit = valid & (
        jnp.where(from_img, row_pos_ref[...], row_pair)
        == jnp.where(from_img, item_pair, item_pos_ref[...])
    )
    real = item[:1] % 4 < 3
    lse_total = jnp.sum(jnp.where(real, item_lse, 0.0), axis=1, keepdims=True)
    lane = lax.broadcasted_iota(jnp.int32, (1, 128), 1)
    matched = jnp.sum(jnp.where(lane == 3, summed, 0.0), axis=1, keepdims=True)
    value = lse_total - 2.0 * matched
    masked = jnp.where(valid, scores, LOW)
    row_part = log_total(masked, 1)
    by_row = (0.5 * logit) * jnp.exp(masked - row_part)
    by_item = (0.5 * logit) * (jnp.exp(masked - item_lse) - jnp.where(hit, 2.0, 0.0))
    coefs = [jnp.where(valid, part, 0.0).astype(BF) for part in (by_row, by_item)]
    along = [
        as_lanes(jnp.sum(part.astype(F32) * scores, axis=1, keepdims=True) / logit)
        for part in coefs
    ]
    coef = jnp.concatenate(coefs, 0)
    cot = jnp.dot(coef[:, :256], fa_ref[...], preferred_element_type=F32)
    cot += jnp.dot(coef[:, 256:], fb_ref[...], preferred_element_type=F32)

    riders = (
        in_parts(as_lanes(row_part), 3)
        + in_parts(along[0], 2)
        + in_parts(along[1], 2)
        + in_parts(jnp.broadcast_to(value, (1, 128)), 2)
        + [jnp.zeros((7, 128), F32)]
    )
    riders = jnp.concatenate([jnp.concatenate(riders, 0), jnp.zeros((16, 256), F32)], 1).astype(BF)
    cot = jnp.concatenate([cot, jnp.zeros((96, 256), F32)], 1).astype(BF)
    for k in range(8):
        way = k % 4
        out_ref[112 * k : 112 * k + 96, :] = cot[:, 384 * way : 384 * way + 384]
        out_ref[112 * k + 96 : 112 * k + 112, :] = riders


def back_kernel(got_ref, unit_ref, wa_ref, wb_ref, out_ref, loss_ref):
    riders = [got_ref[112 * k + 96 : 112 * k + 112, :128].astype(F32) for k in range(8)]
    parts = jnp.concatenate([r[0:1] + r[1:2] + r[2:3] for r in riders], 0)
    weights = jnp.exp(parts - log_total(parts, 0))
    along = jnp.zeros((1, 128), F32)
    value = jnp.zeros((1, 128), F32)
    summed = jnp.zeros((48, 384), F32)
    for k, r in enumerate(riders):
        weight = weights[k : k + 1]
        along += weight * (r[3:4] + r[4:5]) + (r[5:6] + r[6:7])
        value += r[7:8] + r[8:9]
        summed += as_column(weight) * got_ref[112 * k : 112 * k + 48, :].astype(F32)
        summed += got_ref[112 * k + 48 : 112 * k + 96, :].astype(F32)
    loss_ref[...] = jnp.broadcast_to(value / (2.0 * 1536), (8, 128))
    proj_cot = (summed - unit_ref[...].astype(F32) * as_column(along)).astype(BF)
    mixed = []
    for ref in (wa_ref, wb_ref):
        pool = lax.dot_general(proj_cot, ref[...], ROWS_DOT, preferred_element_type=F32)
        is_img = lax.broadcasted_iota(jnp.int32, pool.shape, 1) % 24 < 13
        mixed.append(jnp.where(is_img, pool, pltpu.roll(pool, 45, 0)))
    blank = jnp.zeros((1, pool.shape[1]), F32)
    pieces = []
    for k in range(8):
        for pool in mixed:
            pieces += [pool[6 * k : 6 * k + 3], blank]
    out_ref[...] = jnp.concatenate(pieces, 0).astype(BF)


def token_kernel(pool_ref, inv_ref, img_ref, txt_ref, ig_ref, tg_ref, img_out, txt_out):
    pool = pool_ref[...]
    inv = inv_ref[...][:, :1]
    for x_ref, gain_ref, out_ref, wide, skip, at in (
        (img_ref, ig_ref, img_out, 13, 0, 0),
        (txt_ref, tg_ref, txt_out, 10, 13, 4),
    ):
        dense = lax.broadcasted_iota(jnp.int32, (1, 32 * wide), 1)
        place = ((dense // wide) % 2) * 384 + (dense // (2 * wide)) * 24 + skip + dense % wide
        lane = lax.broadcasted_iota(jnp.int32, (768, 32 * wide), 0)
        pick = jnp.where(lane == place, 1.0, 0.0).astype(BF)
        found = jnp.dot(pool, pick, preferred_element_type=F32)
        halves = [
            found[32 * k : 32 * k + 8]
            + found[32 * k + 8 : 32 * k + 16]
            + found[32 * k + 16 : 32 * k + 24]
            + found[32 * k + 24 : 32 * k + 32]
            for k in range(2)
        ]
        cot = jnp.concatenate([halves[0][:4], halves[0][4:], halves[1][:4], halves[1][4:]], 1)
        cot = cot * inv[at : at + 4] * gain_ref[...]
        mean_cot = jnp.mean(cot, axis=1, keepdims=True)
        count = x_ref.shape[0] // 3
        for q in range(3):
            span = slice(count * q, count * q + count)
            values = x_ref[span, :].astype(F32)
            center = values - jnp.mean(values, axis=1, keepdims=True)
            inner = lax.rsqrt(jnp.mean(center * center, axis=1, keepdims=True) + 1e-05)
            mine = cot[q : q + 1]
            along = jnp.mean(center * mine, axis=1, keepdims=True)
            out = inner * (mine - mean_cot[q : q + 1]) - center * (inner * inner * inner * along)
            out_ref[span, :] = out.astype(BF)


def per_device(image_in, text_in, proj_img, proj_txt, img_gain, txt_gain, logit_scale, positive):
    t_index = lax.axis_index("t")
    h_index = lax.axis_index("h")
    g_index = (lax.axis_index("z") * 4 + lax.axis_index("x")) * 2 + lax.axis_index("c")
    y_index = h_index * 4 + t_index
    place = jnp.stack([y_index, h_index, t_index, g_index]).astype(jnp.int32)
    emb = proj_img.shape[1]

    w = jnp.pad(jnp.concatenate([proj_img, proj_txt], 0), ((0, 1), (0, 256)))
    w = lax.dynamic_slice(w, (0, 384 * t_index), (24, 384))
    wa, wb = both_cores(exchange(jnp.broadcast_to(w[None], (32, 24, 384)), ZX))

    pooled_i = jnp.mean(norm_tokens(image_in, img_gain), axis=1).astype(BF)
    pooled_t = jnp.mean(norm_tokens(text_in, txt_gain), axis=1).astype(BF)
    slabs = jnp.concatenate(
        [
            pooled_i.reshape(12, 128, 13),
            pooled_t.reshape(12, 128, 10),
            jnp.zeros((12, 128, 1), BF),
        ],
        2,
    )
    slabs = slabs.reshape(12, 2, 2, 16, 2, 24).transpose(0, 1, 2, 4, 3, 5).reshape(12, 2, 1536)
    digits = jnp.stack([positive // 32, positive % 32], 1).astype(BF)[:, :, None]
    spot = lax.iota(jnp.int32, 1536)[None, :]
    slabs = jnp.where(spot == 23, digits[:, :1], jnp.where(spot == 47, digits[:, 1:], slabs))
    both = lax.all_gather(slabs.transpose(1, 0, 2), "h", axis=0)
    pooled = lax.dynamic_index_in_dim(both, h_index, 1, keepdims=False).reshape(24, 1536)
    row_pos = pooled[:, 23].astype(F32) * 32.0 + pooled[:, 47].astype(F32)
    row_pos = jnp.pad(row_pos.reshape(8, 3), ((0, 0), (0, 3)), constant_values=-1.0)
    row_pos = row_pos.reshape(48, 1).astype(jnp.int32)
    is_img = spot % 24 < 13
    is_txt = (spot % 24 >= 13) & (spot % 24 < 23)
    left = jnp.stack(
        [
            jnp.where(is_img, pooled, 0).reshape(8, 3, 1536),
            jnp.where(is_txt, pooled, 0).reshape(8, 3, 1536),
        ],
        1,
    ).reshape(48, 1536)

    (part,) = kernel_call(project_kernel, [((384, 384), BF)], [left, wa, wb])
    parts = exchange(part.reshape(8, 48, 384), Y).reshape(384, 384)

    own_digits = lax.dynamic_slice(positive, (3 * t_index,), (3,))
    own_digits = jnp.concatenate([own_digits // 32, own_digits % 32]).astype(F32)
    own_digits = jnp.pad(own_digits, (0, 122))[None]
    rows, far, inv = kernel_call(
        unit_kernel,
        [((48, emb), BF), ((256, emb), BF), ((8, 128), F32)],
        [place, parts, own_digits],
        scratch=[pltpu.VMEM((64, emb), F32), pltpu.VMEM((64, 128), F32)],
        smem=(0,),
    )
    fa, fb = both_cores(exchange(far.reshape(32, 8, emb), ZX))

    scores, far = kernel_call(
        score_kernel,
        [((48, 512), F32), ((256, 128), F32)],
        [place, logit_scale, rows, fa, fb, row_pos],
        smem=(0, 1),
    )
    far = exchange(far.reshape(64, 4, 128), ZXC).reshape(256, 128)

    item_pos = jnp.concatenate([fa.reshape(32, 8, emb)[:, 3, :6], fb.reshape(32, 8, emb)[:, 3, :6]])
    item_pos = item_pos.astype(F32)
    item_pos = item_pos[:, :3] * 32.0 + item_pos[:, 3:]
    item_pos = jnp.pad(item_pos, ((0, 0), (0, 5)), constant_values=-1.0).reshape(1, 512)
    item_pos = item_pos.astype(jnp.int32)
    (ways,) = kernel_call(
        coef_kernel,
        [((896, 384), BF)],
        [place, logit_scale, scores, far, row_pos, item_pos, fa, fb],
        smem=(0, 1),
    )
    got = exchange(ways.reshape(8, 112, 384), Y).reshape(896, 384)
    unit_part = lax.dynamic_slice(
        jnp.pad(rows, ((0, 0), (0, 256))), (0, 384 * t_index), (48, 384)
    )
    pool, loss = kernel_call(
        back_kernel, [((64, 768), BF), ((8, 128), F32)], [got, unit_part, wa, wb]
    )
    mean_loss = loss[0, :1]
    pool = exchange(pool.reshape(8, 8, 768), Y).reshape(64, 768)
    count_i, width_i = image_in.shape[1:]
    count_t, width_t = text_in.shape[1:]
    img_own = lax.dynamic_slice_in_dim(image_in, 3 * t_index, 3, 0).reshape(-1, width_i)
    txt_own = lax.dynamic_slice_in_dim(text_in, 3 * t_index, 3, 0).reshape(-1, width_t)
    img_grads, txt_grads = kernel_call(
        token_kernel,
        [(img_own.shape, BF), (txt_own.shape, BF)],
        [pool, inv, img_own, txt_own, img_gain[None], txt_gain[None]],
    )
    img_grads = img_grads.reshape(3, count_i, width_i)
    txt_grads = txt_grads.reshape(3, count_t, width_t)
    return (mean_loss, img_grads[None], txt_grads[None])


def solution(mesh):
    fine = Mesh(mesh.devices.reshape(4, 2, 8, 4, 2), ("t", "h", "z", "x", "c"))
    in_specs = (
        P(DP, None, None),
        P(DP, None, None),
        P(DP, None),
        P(DP, None),
        P(),
        P(),
        P(),
        P(DP),
    )
    out_specs = (P(), P("t", DP, None, None), P("t", DP, None, None))
    return jax.shard_map(
        per_device, mesh=fine, in_specs=in_specs, out_specs=out_specs, check_vma=False
    )
```

```python
import jax
import jax.numpy as jnp
from jax import lax
from jax.experimental import pallas as pl
from jax.experimental.pallas import tpu as pltpu
from jax.sharding import Mesh, PartitionSpec as P

BF = jnp.bfloat16
F32 = jnp.float32
Y = ("h", "t")
ZX = ("z", "x")
ZXC = ("z", "x", "c")
DP = ("h", "z", "x", "c")
LOW = -1e30
ROWS_DOT = (((1,), (1,)), ((), ()))


def exchange(blocks, axes):
    return lax.all_to_all(blocks, axes, 0, 0, tiled=True)


def both_cores(blocks):
    half = blocks.shape[0] // 2
    parts = [lax.all_gather(part, "c", axis=0) for part in (blocks[:half], blocks[half:])]
    return [part.reshape(-1, blocks.shape[2]) for part in parts]


def kernel_call(body, outs, args, scratch=(), smem=()):
    vmem = pl.BlockSpec(memory_space=pltpu.VMEM)
    return pl.pallas_call(
        body,
        out_shape=[jax.ShapeDtypeStruct(shape, kind) for shape, kind in outs],
        in_specs=[
            pl.BlockSpec(memory_space=pltpu.SMEM) if k in smem else vmem for k in range(len(args))
        ],
        out_specs=[vmem] * len(outs),
        scratch_shapes=list(scratch),
        compiler_params=pltpu.CompilerParams(vmem_limit_bytes=40 * 1024 * 1024),
    )(*args)


def slab_place(dense, wide, skip):
    return ((dense // wide) % 2) * 384 + (dense // (2 * wide)) * 24 + skip + dense % wide


def pool_kernel(img_ref, txt_ref, ig_ref, tg_ref, digits_ref, out_ref, img_rows, txt_rows):
    step = pl.program_id(0)

    @pl.when(step == 0)
    def _():
        img_rows[...] = jnp.zeros_like(img_rows)
        txt_rows[...] = jnp.zeros_like(txt_rows)

    for x_ref, gain_ref, rows in ((img_ref, ig_ref, img_rows), (txt_ref, tg_ref, txt_rows)):
        values = x_ref[0].astype(F32)
        center = values - jnp.mean(values, axis=1, keepdims=True)
        spread = jnp.mean(center * center, axis=1, keepdims=True)
        mean = jnp.mean(center * lax.rsqrt(spread + 1e-05), axis=0, keepdims=True)
        rows[pl.ds(step, 1), :] = mean * gain_ref[...]

    @pl.when(step == 11)
    def _():
        found = jnp.zeros((64, 768), F32)
        for rows, wide, skip in ((img_rows, 13, 0), (txt_rows, 10, 13)):
            width = 32 * wide
            dense = lax.broadcasted_iota(jnp.int32, (width, 768), 0)
            lane = lax.broadcasted_iota(jnp.int32, (width, 768), 1)
            pick = jnp.where(lane == slab_place(dense, wide, skip), 1.0, 0.0).astype(BF)
            held = rows[...]
            quarters = [held[:, width * k : width * k + width] for k in range(4)]
            quarters = jnp.concatenate(quarters, 0).astype(BF)
            found += jnp.dot(quarters, pick, preferred_element_type=F32)
        digits = digits_ref[...]
        blank = jnp.zeros_like(digits)
        digits = jnp.concatenate([digits, blank, digits, blank], 0)
        found = jnp.concatenate([found[:, :128] + digits, found[:, 128:]], 1)
        out_ref[...] = found.astype(BF)


def pool_call(image_in, text_in, img_gain, txt_gain, digits):
    pairs, count_i, width_i = image_in.shape
    _, count_t, width_t = text_in.shape
    whole = lambda shape: pl.BlockSpec(shape, lambda k: (0, 0))
    return pl.pallas_call(
        pool_kernel,
        grid=(pairs,),
        out_shape=jax.ShapeDtypeStruct((64, 768), BF),
        in_specs=[
            pl.BlockSpec((1, count_i, width_i), lambda k: (k, 0, 0)),
            pl.BlockSpec((1, count_t, width_t), lambda k: (k, 0, 0)),
            whole((1, width_i)),
            whole((1, width_t)),
            whole((16, 128)),
        ],
        out_specs=whole((64, 768)),
        scratch_shapes=[pltpu.VMEM((16, width_i), F32), pltpu.VMEM((16, width_t), F32)],
        cost_estimate=pl.CostEstimate(
            flops=10 * (image_in.size + text_in.size),
            bytes_accessed=2 * (image_in.size + text_in.size),
            transcendentals=0,
        ),
        compiler_params=pltpu.CompilerParams(vmem_limit_bytes=40 * 1024 * 1024),
    )(image_in, text_in, img_gain[None], txt_gain[None], digits)


def project_kernel(place_ref, pooled_ref, wa_ref, wb_ref, out_ref):
    part = jnp.zeros((48, wa_ref.shape[1]), F32)
    inside = lax.broadcasted_iota(jnp.int32, (12, 768), 1) % 24
    for a, w_ref in enumerate((wa_ref, wb_ref)):
        pieces = []
        for h in range(2):
            start = pl.multiple_of(64 * h + 32 * place_ref[1] + 16 * a, 16)
            rows = pooled_ref[pl.ds(start, 16), :].astype(F32)[:12]
            img_rows = jnp.where(inside < 13, rows, 0.0)
            txt_rows = jnp.where((inside >= 13) & (inside < 23), rows, 0.0)
            for t in range(4):
                pieces += [img_rows[3 * t : 3 * t + 3], txt_rows[3 * t : 3 * t + 3]]
        left = jnp.concatenate(pieces, 0).astype(BF)
        part += jnp.dot(left, w_ref[...], preferred_element_type=F32)
    part = part.astype(BF)
    for k in range(8):
        out_ref[48 * k : 48 * k + 48, :] = part


def in_blocks(values):
    blank = jnp.zeros((1, values.shape[1]), F32)
    pieces = []
    for k in range(8):
        pieces += [values[6 * k : 6 * k + 3], blank, values[6 * k + 3 : 6 * k + 6], blank]
    return jnp.concatenate(pieces, 0)


def unit_kernel(place_ref, parts_ref, digits_ref, rows_ref, far_ref, inv_ref, held, held_inv):
    spread = parts_ref[...].astype(F32)
    emb = rows_ref.shape[1]
    blocks = [spread[48 * k : 48 * k + 48] + spread[192 + 48 * k : 240 + 48 * k] for k in range(4)]
    projected = jnp.concatenate(blocks, 1)[:, :emb]
    inv = lax.rsqrt(jnp.sum(projected * projected, axis=1, keepdims=True) + 1e-06)
    unit = projected * inv
    rows_ref[...] = unit.astype(BF)
    held[...] = in_blocks(unit)
    held_inv[...] = in_blocks(jnp.broadcast_to(inv, (48, 128)))
    own = pl.ds(pl.multiple_of(8 * place_ref[0], 8), 8)
    inv_ref[...] = held_inv[own, :]
    block = held[own, :]
    at = lax.broadcasted_iota(jnp.int32, (8, 128), 0)
    start = jnp.where(at == 3, digits_ref[...], block[:, :128])
    block = jnp.concatenate([start, block[:, 128:]], 1)
    block = jnp.concatenate([block, block], 0).astype(BF)
    for k in range(16):
        far_ref[16 * k : 16 * k + 16, :] = block


def tile_masks(place_ref):
    h, t, g = place_ref[1], place_ref[2], place_ref[3]
    row = lax.broadcasted_iota(jnp.int32, (48, 512), 0)
    item = lax.broadcasted_iota(jnp.int32, (48, 512), 1)
    item_g = ((item // 256) * 16 + (item % 128) // 8) * 2 + (item // 128) % 2
    item_pair = (h * 64 + item_g) * 12 + 3 * t + item % 4
    row_pair = ((row // 24) * 64 + g) * 12 + ((row // 6) % 4) * 3 + row % 3
    row_txt, item_txt = (row % 6) // 3, (item % 8) // 4
    valid = (row_txt != item_txt) & (item % 4 < 3)
    return valid, row_pair, item_pair, row_txt, item


def square_mask():
    down = lax.broadcasted_iota(jnp.int32, (48, 128), 0)
    along = lax.broadcasted_iota(jnp.int32, (48, 128), 1)
    return down == along


def as_lanes(column):
    return jnp.sum(jnp.where(square_mask(), column, 0.0), axis=0, keepdims=True)


def as_column(lanes):
    return jnp.sum(jnp.where(square_mask(), lanes, 0.0), axis=1, keepdims=True)


def log_total(values, axis):
    largest = jnp.max(values, axis=axis, keepdims=True)
    return largest + jnp.log(jnp.sum(jnp.exp(values - largest), axis=axis, keepdims=True))


def score_kernel(place_ref, logit_ref, rows_ref, fa_ref, fb_ref, row_pos_ref, scores_ref, far_ref):
    rows = rows_ref[...]
    scores = jnp.concatenate(
        [
            lax.dot_general(rows, ref[...], ROWS_DOT, preferred_element_type=F32)
            for ref in (fa_ref, fb_ref)
        ],
        1,
    )
    scores = logit_ref[0] * scores
    scores_ref[...] = scores
    valid, _, item_pair, row_txt, _ = tile_masks(place_ref)
    masked = jnp.where(valid, scores, LOW)
    item_part = log_total(masked, 0)
    hit = valid & (row_txt == 0) & (row_pos_ref[...] == item_pair)
    matched = jnp.sum(
        jnp.sum(jnp.where(hit, scores, 0.0), axis=1, keepdims=True), axis=0, keepdims=True
    )
    lane = lax.broadcasted_iota(jnp.int32, (1, 512), 1)
    item_part = jnp.where(lane == 3, matched, item_part)
    lines = jnp.concatenate([item_part[:, 128 * k : 128 * k + 128] for k in range(4)] * 2, 0)
    for k in range(32):
        far_ref[8 * k : 8 * k + 8, :] = lines


def in_parts(values, count):
    parts = []
    for _ in range(count):
        part = values.astype(BF).astype(F32)
        parts.append(part)
        values = values - part
    return parts


def coef_kernel(
    place_ref, logit_ref, scores_ref, far_ref, row_pos_ref, item_pos_ref, fa_ref, fb_ref, out_ref
):
    logit = logit_ref[0]
    scores = scores_ref[...]
    seen = far_ref[...].reshape(32, 8, 128)
    largest = jnp.max(seen, axis=0)
    largest = jnp.maximum(largest[:4], largest[4:])
    both = jnp.concatenate([largest, largest], 0)
    total = jnp.sum(jnp.exp(seen - both[None]), axis=0)
    lines = largest + jnp.log(total[:4] + total[4:])
    item_lse = jnp.concatenate([lines[k : k + 1] for k in range(4)], 1)
    summed = jnp.sum(seen, axis=0)
    summed = summed[:1] + summed[4:5]
    valid, row_pair, item_pair, row_txt, item = tile_masks(place_ref)
    from_img = row_txt == 0
    hit = valid & (
        jnp.where(from_img, row_pos_ref[...], row_pair)
        == jnp.where(from_img, item_pair, item_pos_ref[...])
    )
    real = item[:1] % 4 < 3
    lse_total = jnp.sum(jnp.where(real, item_lse, 0.0), axis=1, keepdims=True)
    lane = lax.broadcasted_iota(jnp.int32, (1, 128), 1)
    matched = jnp.sum(jnp.where(lane == 3, summed, 0.0), axis=1, keepdims=True)
    value = lse_total - 2.0 * matched
    masked = jnp.where(valid, scores, LOW)
    row_part = log_total(masked, 1)
    by_row = (0.5 * logit) * jnp.exp(masked - row_part)
    by_item = (0.5 * logit) * (jnp.exp(masked - item_lse) - jnp.where(hit, 2.0, 0.0))
    coefs = [jnp.where(valid, part, 0.0).astype(BF) for part in (by_row, by_item)]
    along = [
        as_lanes(jnp.sum(part.astype(F32) * scores, axis=1, keepdims=True) / logit)
        for part in coefs
    ]
    coef = jnp.concatenate(coefs, 0)
    cot = jnp.dot(coef[:, :256], fa_ref[...], preferred_element_type=F32)
    cot += jnp.dot(coef[:, 256:], fb_ref[...], preferred_element_type=F32)

    riders = (
        in_parts(as_lanes(row_part), 3)
        + in_parts(along[0], 2)
        + in_parts(along[1], 2)
        + in_parts(jnp.broadcast_to(value, (1, 128)), 2)
        + [jnp.zeros((7, 128), F32)]
    )
    riders = jnp.concatenate([jnp.concatenate(riders, 0), jnp.zeros((16, 256), F32)], 1).astype(BF)
    cot = jnp.concatenate([cot, jnp.zeros((96, 256), F32)], 1).astype(BF)
    for k in range(8):
        way = k % 4
        out_ref[112 * k : 112 * k + 96, :] = cot[:, 384 * way : 384 * way + 384]
        out_ref[112 * k + 96 : 112 * k + 112, :] = riders


def back_kernel(got_ref, unit_ref, wa_ref, wb_ref, out_ref, loss_ref):
    riders = [got_ref[112 * k + 96 : 112 * k + 112, :128].astype(F32) for k in range(8)]
    parts = jnp.concatenate([r[0:1] + r[1:2] + r[2:3] for r in riders], 0)
    weights = jnp.exp(parts - log_total(parts, 0))
    along = jnp.zeros((1, 128), F32)
    value = jnp.zeros((1, 128), F32)
    summed = jnp.zeros((48, 384), F32)
    for k, r in enumerate(riders):
        weight = weights[k : k + 1]
        along += weight * (r[3:4] + r[4:5]) + (r[5:6] + r[6:7])
        value += r[7:8] + r[8:9]
        summed += as_column(weight) * got_ref[112 * k : 112 * k + 48, :].astype(F32)
        summed += got_ref[112 * k + 48 : 112 * k + 96, :].astype(F32)
    loss_ref[...] = jnp.broadcast_to(value / (2.0 * 1536), (8, 128))
    proj_cot = (summed - unit_ref[...].astype(F32) * as_column(along)).astype(BF)
    mixed = []
    for ref in (wa_ref, wb_ref):
        pool = lax.dot_general(proj_cot, ref[...], ROWS_DOT, preferred_element_type=F32)
        is_img = lax.broadcasted_iota(jnp.int32, pool.shape, 1) % 24 < 13
        mixed.append(jnp.where(is_img, pool, pltpu.roll(pool, 45, 0)))
    blank = jnp.zeros((1, pool.shape[1]), F32)
    pieces = []
    for k in range(8):
        for pool in mixed:
            pieces += [pool[6 * k : 6 * k + 3], blank]
    out_ref[...] = jnp.concatenate(pieces, 0).astype(BF)


def token_kernel(pool_ref, inv_ref, img_ref, txt_ref, ig_ref, tg_ref, img_out, txt_out):
    pool = pool_ref[...]
    inv = inv_ref[...][:, :1]
    for x_ref, gain_ref, out_ref, wide, skip, at in (
        (img_ref, ig_ref, img_out, 13, 0, 0),
        (txt_ref, tg_ref, txt_out, 10, 13, 4),
    ):
        dense = lax.broadcasted_iota(jnp.int32, (1, 32 * wide), 1)
        lane = lax.broadcasted_iota(jnp.int32, (768, 32 * wide), 0)
        pick = jnp.where(lane == slab_place(dense, wide, skip), 1.0, 0.0).astype(BF)
        found = jnp.dot(pool, pick, preferred_element_type=F32)
        halves = [
            found[32 * k : 32 * k + 8]
            + found[32 * k + 8 : 32 * k + 16]
            + found[32 * k + 16 : 32 * k + 24]
            + found[32 * k + 24 : 32 * k + 32]
            for k in range(2)
        ]
        cot = jnp.concatenate([halves[0][:4], halves[0][4:], halves[1][:4], halves[1][4:]], 1)
        cot = cot * inv[at : at + 4] * gain_ref[...]
        mean_cot = jnp.mean(cot, axis=1, keepdims=True)
        count = x_ref.shape[0] // 3
        for q in range(3):
            span = slice(count * q, count * q + count)
            values = x_ref[span, :].astype(F32)
            center = values - jnp.mean(values, axis=1, keepdims=True)
            inner = lax.rsqrt(jnp.mean(center * center, axis=1, keepdims=True) + 1e-05)
            mine = cot[q : q + 1]
            along = jnp.mean(center * mine, axis=1, keepdims=True)
            out = inner * (mine - mean_cot[q : q + 1]) - center * (inner * inner * inner * along)
            out_ref[span, :] = out.astype(BF)


def per_device(image_in, text_in, proj_img, proj_txt, img_gain, txt_gain, logit_scale, positive):
    t_index = lax.axis_index("t")
    h_index = lax.axis_index("h")
    g_index = (lax.axis_index("z") * 4 + lax.axis_index("x")) * 2 + lax.axis_index("c")
    y_index = h_index * 4 + t_index
    place = jnp.stack([y_index, h_index, t_index, g_index]).astype(jnp.int32)
    emb = proj_img.shape[1]

    w = jnp.pad(jnp.concatenate([proj_img, proj_txt], 0), ((0, 1), (0, 256)))
    w = lax.dynamic_slice(w, (0, 384 * t_index), (24, 384))
    wa, wb = both_cores(exchange(jnp.broadcast_to(w[None], (32, 24, 384)), ZX))

    spot = lax.iota(jnp.int32, 128)[None, :]
    digits = jnp.where(spot == 23, positive[:, None] // 32, 0)
    digits = jnp.where(spot == 47, positive[:, None] % 32, digits).astype(F32)
    digits = jnp.pad(digits, ((0, 4), (0, 0)))
    pooled = pool_call(image_in, text_in, img_gain, txt_gain, digits)
    pooled = lax.all_gather(pooled, "h", axis=0)
    row_pos = pooled[:, :12, 23].astype(F32) * 32.0 + pooled[:, :12, 47].astype(F32)
    row_pos = jnp.pad(row_pos.reshape(8, 3), ((0, 0), (0, 3)), constant_values=-1.0)
    row_pos = row_pos.reshape(48, 1).astype(jnp.int32)

    (part,) = kernel_call(
        project_kernel,
        [((384, 384), BF)],
        [place, pooled.reshape(128, 768), wa, wb],
        smem=(0,),
    )
    parts = exchange(part.reshape(8, 48, 384), Y).reshape(384, 384)

    own_digits = lax.dynamic_slice(positive, (3 * t_index,), (3,))
    own_digits = jnp.concatenate([own_digits // 32, own_digits % 32]).astype(F32)
    own_digits = jnp.pad(own_digits, (0, 122))[None]
    rows, far, inv = kernel_call(
        unit_kernel,
        [((48, emb), BF), ((256, emb), BF), ((8, 128), F32)],
        [place, parts, own_digits],
        scratch=[pltpu.VMEM((64, emb), F32), pltpu.VMEM((64, 128), F32)],
        smem=(0,),
    )
    fa, fb = both_cores(exchange(far.reshape(32, 8, emb), ZX))

    scores, far = kernel_call(
        score_kernel,
        [((48, 512), F32), ((256, 128), F32)],
        [place, logit_scale, rows, fa, fb, row_pos],
        smem=(0, 1),
    )
    far = exchange(far.reshape(64, 4, 128), ZXC).reshape(256, 128)

    item_pos = jnp.concatenate([fa.reshape(32, 8, emb)[:, 3, :6], fb.reshape(32, 8, emb)[:, 3, :6]])
    item_pos = item_pos.astype(F32)
    item_pos = item_pos[:, :3] * 32.0 + item_pos[:, 3:]
    item_pos = jnp.pad(item_pos, ((0, 0), (0, 5)), constant_values=-1.0).reshape(1, 512)
    item_pos = item_pos.astype(jnp.int32)
    (ways,) = kernel_call(
        coef_kernel,
        [((896, 384), BF)],
        [place, logit_scale, scores, far, row_pos, item_pos, fa, fb],
        smem=(0, 1),
    )
    got = exchange(ways.reshape(8, 112, 384), Y).reshape(896, 384)
    unit_part = lax.dynamic_slice(
        jnp.pad(rows, ((0, 0), (0, 256))), (0, 384 * t_index), (48, 384)
    )
    pool, loss = kernel_call(
        back_kernel, [((64, 768), BF), ((8, 128), F32)], [got, unit_part, wa, wb]
    )
    mean_loss = loss[0, :1]
    pool = exchange(pool.reshape(8, 8, 768), Y).reshape(64, 768)
    count_i, width_i = image_in.shape[1:]
    count_t, width_t = text_in.shape[1:]
    img_own = lax.dynamic_slice_in_dim(image_in, 3 * t_index, 3, 0).reshape(-1, width_i)
    txt_own = lax.dynamic_slice_in_dim(text_in, 3 * t_index, 3, 0).reshape(-1, width_t)
    img_grads, txt_grads = kernel_call(
        token_kernel,
        [(img_own.shape, BF), (txt_own.shape, BF)],
        [pool, inv, img_own, txt_own, img_gain[None], txt_gain[None]],
    )
    img_grads = img_grads.reshape(3, count_i, width_i)
    txt_grads = txt_grads.reshape(3, count_t, width_t)
    return (mean_loss, img_grads[None], txt_grads[None])


def solution(mesh):
    fine = Mesh(mesh.devices.reshape(4, 2, 8, 4, 2), ("t", "h", "z", "x", "c"))
    in_specs = (
        P(DP, None, None),
        P(DP, None, None),
        P(DP, None),
        P(DP, None),
        P(),
        P(),
        P(),
        P(DP),
    )
    out_specs = (P(), P("t", DP, None, None), P("t", DP, None, None))
    return jax.shard_map(
        per_device, mesh=fine, in_specs=in_specs, out_specs=out_specs, check_vma=False
    )
```

```python
import functools

import jax
import jax.numpy as jnp
from jax import lax
from jax.experimental import pallas as pl
from jax.experimental.pallas import tpu as pltpu
from jax.sharding import Mesh, PartitionSpec as P

BF = jnp.bfloat16
F32 = jnp.float32
Y = ("h", "t")
ZX = ("z", "x")
ZXC = ("z", "x", "c")
DP = ("h", "z", "x", "c")
LOW = -1e30
ROWS_DOT = (((1,), (1,)), ((), ()))


def exchange(blocks, axes):
    return lax.all_to_all(blocks, axes, 0, 0, tiled=True)


def both_cores(blocks):
    half = blocks.shape[0] // 2
    parts = [lax.all_gather(part, "c", axis=0) for part in (blocks[:half], blocks[half:])]
    return [part.reshape(-1, blocks.shape[2]) for part in parts]


def kernel_call(body, outs, args, scratch=(), smem=()):
    vmem = pl.BlockSpec(memory_space=pltpu.VMEM)
    return pl.pallas_call(
        body,
        out_shape=[jax.ShapeDtypeStruct(shape, kind) for shape, kind in outs],
        in_specs=[
            pl.BlockSpec(memory_space=pltpu.SMEM) if k in smem else vmem for k in range(len(args))
        ],
        out_specs=[vmem] * len(outs),
        scratch_shapes=list(scratch),
        compiler_params=pltpu.CompilerParams(vmem_limit_bytes=40 * 1024 * 1024),
    )(*args)


def slab_place(dense, wide, skip):
    return ((dense // wide) % 2) * 384 + (dense // (2 * wide)) * 24 + skip + dense % wide


def pool_kernel(img_ref, txt_ref, ig_ref, tg_ref, digits_ref, out_ref, img_rows, txt_rows):
    step = pl.program_id(0)

    @pl.when(step == 0)
    def _():
        img_rows[...] = jnp.zeros_like(img_rows)
        txt_rows[...] = jnp.zeros_like(txt_rows)

    for x_ref, gain_ref, rows in ((img_ref, ig_ref, img_rows), (txt_ref, tg_ref, txt_rows)):
        values = x_ref[0].astype(F32)
        center = values - jnp.mean(values, axis=1, keepdims=True)
        spread = jnp.mean(center * center, axis=1, keepdims=True)
        mean = jnp.mean(center * lax.rsqrt(spread + 1e-05), axis=0, keepdims=True)
        rows[pl.ds(step, 1), :] = mean * gain_ref[...][None]

    @pl.when(step == 11)
    def _():
        found = jnp.zeros((64, 768), F32)
        for rows, wide, skip in ((img_rows, 13, 0), (txt_rows, 10, 13)):
            width = 32 * wide
            dense = lax.broadcasted_iota(jnp.int32, (width, 768), 0)
            lane = lax.broadcasted_iota(jnp.int32, (width, 768), 1)
            pick = jnp.where(lane == slab_place(dense, wide, skip), 1.0, 0.0).astype(BF)
            held = rows[...]
            quarters = [held[:, width * k : width * k + width] for k in range(4)]
            quarters = jnp.concatenate(quarters, 0).astype(BF)
            found += jnp.dot(quarters, pick, preferred_element_type=F32)
        digits = digits_ref[...]
        blank = jnp.zeros_like(digits)
        digits = jnp.concatenate([digits, blank, digits, blank], 0)
        found = jnp.concatenate([found[:, :128] + digits, found[:, 128:]], 1)
        out_ref[...] = found.astype(BF)


def pool_call(image_in, text_in, img_gain, txt_gain, digits):
    pairs, count_i, width_i = image_in.shape
    _, count_t, width_t = text_in.shape
    whole = lambda shape: pl.BlockSpec(shape, lambda k: (0,) * len(shape))
    return pl.pallas_call(
        pool_kernel,
        grid=(pairs,),
        out_shape=jax.ShapeDtypeStruct((64, 768), BF),
        in_specs=[
            pl.BlockSpec((1, count_i, width_i), lambda k: (k, 0, 0)),
            pl.BlockSpec((1, count_t, width_t), lambda k: (k, 0, 0)),
            whole((width_i,)),
            whole((width_t,)),
            whole((16, 128)),
        ],
        out_specs=whole((64, 768)),
        scratch_shapes=[pltpu.VMEM((16, width_i), F32), pltpu.VMEM((16, width_t), F32)],
        cost_estimate=pl.CostEstimate(
            flops=10 * (image_in.size + text_in.size),
            bytes_accessed=2 * (image_in.size + text_in.size),
            transcendentals=0,
        ),
        compiler_params=pltpu.CompilerParams(vmem_limit_bytes=60 * 1024 * 1024),
    )(image_in, text_in, img_gain, txt_gain, digits)


def weight_kernel(place_ref, img_ref, txt_ref, out_ref):
    width = out_ref.shape[1]
    rows = jnp.concatenate(
        [
            img_ref[...].astype(F32),
            txt_ref[...].astype(F32),
            jnp.zeros((1, img_ref.shape[1]), F32),
        ],
        0,
    )
    mine = rows[:, :width]
    for k in range(1, 4):
        mine = jnp.where(place_ref[2] == k, rows[:, width * k : width * k + width], mine)
    mine = jnp.concatenate([mine, mine], 0).astype(BF)
    for k in range(16):
        out_ref[48 * k : 48 * k + 48, :] = mine


def project_kernel(place_ref, pooled_ref, wa_ref, wb_ref, out_ref):
    part = jnp.zeros((48, wa_ref.shape[1]), F32)
    inside = lax.broadcasted_iota(jnp.int32, (12, 768), 1) % 24
    for a, w_ref in enumerate((wa_ref, wb_ref)):
        pieces = []
        for h in range(2):
            start = pl.multiple_of(64 * h + 32 * place_ref[1] + 16 * a, 16)
            rows = pooled_ref[pl.ds(start, 16), :].astype(F32)[:12]
            img_rows = jnp.where(inside < 13, rows, 0.0)
            txt_rows = jnp.where((inside >= 13) & (inside < 23), rows, 0.0)
            for t in range(4):
                pieces += [img_rows[3 * t : 3 * t + 3], txt_rows[3 * t : 3 * t + 3]]
        left = jnp.concatenate(pieces, 0).astype(BF)
        part += jnp.dot(left, w_ref[...], preferred_element_type=F32)
    packed = jnp.concatenate([part[:24], part[24:]], 1)
    out_ref[...] = jnp.concatenate([packed] * 8, 0).astype(BF)


def in_blocks(values):
    blank = jnp.zeros((1, values.shape[1]), F32)
    pieces = []
    for k in range(8):
        pieces += [values[6 * k : 6 * k + 3], blank, values[6 * k + 3 : 6 * k + 6], blank]
    return jnp.concatenate(pieces, 0)


def unit_kernel(place_ref, parts_ref, digits_ref, rows_ref, far_ref, inv_ref, held, held_inv):
    spread = parts_ref[...].astype(F32)
    width = spread.shape[1] // 2
    blocks = [spread[24 * k : 24 * k + 24] + spread[96 + 24 * k : 120 + 24 * k] for k in range(4)]
    blocks = [jnp.concatenate([part[:, :width], part[:, width:]], 0) for part in blocks]
    projected = jnp.concatenate(blocks, 1)
    inv = lax.rsqrt(jnp.sum(projected * projected, axis=1, keepdims=True) + 1e-06)
    unit = projected * inv
    rows_ref[...] = unit.astype(BF)
    held[...] = in_blocks(unit)
    held_inv[...] = in_blocks(jnp.broadcast_to(inv, (48, 128)))
    own = pl.ds(pl.multiple_of(8 * place_ref[0], 8), 8)
    inv_ref[...] = held_inv[own, :]
    block = held[own, :]
    free = jnp.concatenate([digits_ref[...], jnp.zeros((1, 128), F32)], 1)
    pieces = []
    for k in (0, 4):
        ends = [block[k + q : k + q + 1, 1024:] for q in range(3)]
        pieces += [block[k : k + 3, :1024], jnp.concatenate(ends + [free], 1)]
    block = jnp.concatenate(pieces, 0)
    block = jnp.concatenate([block, block], 0).astype(BF)
    for k in range(16):
        far_ref[16 * k : 16 * k + 16, :] = block


def tile_masks(place_ref):
    h, t, g = place_ref[1], place_ref[2], place_ref[3]
    row = lax.broadcasted_iota(jnp.int32, (48, 512), 0)
    item = lax.broadcasted_iota(jnp.int32, (48, 512), 1)
    item_g = ((item // 256) * 16 + (item % 128) // 8) * 2 + (item // 128) % 2
    item_pair = (h * 64 + item_g) * 12 + 3 * t + item % 4
    row_pair = ((row // 24) * 64 + g) * 12 + ((row // 6) % 4) * 3 + row % 3
    row_txt, item_txt = (row % 6) // 3, (item % 8) // 4
    valid = (row_txt != item_txt) & (item % 4 < 3)
    return valid, row_pair, item_pair, row_txt, item


def log_total(values, axis):
    largest = jnp.max(values, axis=axis, keepdims=True)
    return largest + jnp.log(jnp.sum(jnp.exp(values - largest), axis=axis, keepdims=True))


def score_kernel(place_ref, logit_ref, rows_ref, fa_ref, fb_ref, row_pos_ref, scores_ref, far_ref):
    rows = rows_ref[...]
    ends = rows[:, 1024:]
    blank = jnp.zeros_like(ends)
    ends = [[ends if k == q else blank for k in range(3)] for q in range(3)]
    ends = jnp.concatenate([jnp.concatenate(line, 1) for line in ends], 0)

    def dots(left, width):
        return jnp.concatenate(
            [
                lax.dot_general(left, ref[:, :width], ROWS_DOT, preferred_element_type=F32)
                for ref in (fa_ref, fb_ref)
            ],
            1,
        )

    scores = dots(rows[:, :1024], 1024)
    ends = dots(ends, 768)
    lane = lax.broadcasted_iota(jnp.int32, (48, 512), 1) % 4
    for q in range(3):
        moved = pltpu.roll(ends[48 * q : 48 * q + 48], 512 - (3 - q), 1)
        scores += jnp.where(lane == q, moved, 0.0)
    scores = logit_ref[0] * scores
    scores_ref[...] = scores
    valid, _, item_pair, row_txt, _ = tile_masks(place_ref)
    masked = jnp.where(valid, scores, LOW)
    item_part = log_total(masked, 0)
    hit = valid & (row_txt == 0) & (row_pos_ref[...] == item_pair)
    matched = jnp.sum(
        jnp.sum(jnp.where(hit, scores, 0.0), axis=1, keepdims=True), axis=0, keepdims=True
    )
    lane = lax.broadcasted_iota(jnp.int32, (1, 512), 1)
    item_part = jnp.where(lane == 3, matched, item_part)
    lines = jnp.concatenate([item_part[:, 128 * k : 128 * k + 128] for k in range(4)] * 2, 0)
    for k in range(32):
        far_ref[8 * k : 8 * k + 8, :] = lines


def in_parts(values, count):
    parts = []
    for _ in range(count):
        part = values.astype(BF).astype(F32)
        parts.append(part)
        values = values - part
    return parts


def coef_kernel(
    place_ref, logit_ref, scores_ref, far_ref, row_pos_ref, item_pos_ref, fa_ref, fb_ref, out_ref
):
    logit = logit_ref[0]
    scores = scores_ref[...]
    seen = far_ref[...].reshape(32, 8, 128)
    largest = jnp.max(seen, axis=0)
    largest = jnp.maximum(largest[:4], largest[4:])
    both = jnp.concatenate([largest, largest], 0)
    total = jnp.sum(jnp.exp(seen - both[None]), axis=0)
    lines = largest + jnp.log(total[:4] + total[4:])
    item_lse = jnp.concatenate([lines[k : k + 1] for k in range(4)], 1)
    summed = jnp.sum(seen, axis=0)
    summed = summed[:1] + summed[4:5]
    valid, row_pair, item_pair, row_txt, item = tile_masks(place_ref)
    from_img = row_txt == 0
    hit = valid & (
        jnp.where(from_img, row_pos_ref[...], row_pair)
        == jnp.where(from_img, item_pair, item_pos_ref[...])
    )
    real = item[:1] % 4 < 3
    lse_total = jnp.sum(jnp.where(real, item_lse, 0.0), axis=1, keepdims=True)
    lane = lax.broadcasted_iota(jnp.int32, (1, 128), 1)
    matched = jnp.sum(jnp.where(lane == 3, summed, 0.0), axis=1, keepdims=True)
    value = lse_total - 2.0 * matched
    masked = jnp.where(valid, scores, LOW)
    row_part = log_total(masked, 1)
    by_row = (0.5 * logit) * jnp.exp(masked - row_part)
    by_item = (0.5 * logit) * (jnp.exp(masked - item_lse) - jnp.where(hit, 2.0, 0.0))
    coefs = [jnp.where(valid, part, 0.0).astype(BF) for part in (by_row, by_item)]
    along = [
        jnp.sum(part.astype(F32) * scores, axis=1, keepdims=True) / logit for part in coefs
    ]
    coef = jnp.concatenate(coefs, 0)

    def times_items(left, columns):
        return jnp.dot(left[:, :256], fa_ref[:, columns], preferred_element_type=F32) + jnp.dot(
            left[:, 256:], fb_ref[:, columns], preferred_element_type=F32
        )

    cot = times_items(coef, slice(0, 1024))
    last = lax.broadcasted_iota(jnp.int32, (96, 512), 1) % 4 == 3
    wide = coef.astype(F32)
    ends = jnp.zeros((96, 256), F32)
    for q in range(3):
        moved = jnp.where(last, pltpu.roll(wide, 3 - q, 1), 0.0).astype(BF)
        ends += times_items(moved, slice(256 * q, 256 * q + 256))
    cot = jnp.concatenate([cot, ends], 1)

    riders = (
        in_parts(row_part, 3)
        + in_parts(along[0], 2)
        + in_parts(along[1], 2)
        + in_parts(jnp.broadcast_to(value, (48, 1)), 2)
    )
    column = lax.broadcasted_iota(jnp.int32, (48, 64), 1)
    extra = jnp.zeros((48, 64), F32)
    for k, rider in enumerate(riders):
        extra = jnp.where(column == k, rider, extra)
    blank = jnp.zeros((48, 64), F32)
    width = cot.shape[1] // 4
    for k in range(4):
        part = cot[:, width * k : width * k + width]
        way = jnp.concatenate([part[:48], extra, part[48:], blank], 1).astype(BF)
        out_ref[48 * k : 48 * k + 48, :] = way
        out_ref[192 + 48 * k : 240 + 48 * k, :] = way


def back_kernel(got_ref, unit_ref, wa_ref, wb_ref, out_ref, loss_ref):
    width = unit_ref.shape[1]
    got = [got_ref[48 * k : 48 * k + 48, :].astype(F32) for k in range(8)]
    riders = [[part[:, width + k : width + k + 1] for k in range(9)] for part in got]
    parts = [r[0] + r[1] + r[2] for r in riders]
    largest = functools.reduce(jnp.maximum, parts)
    total = sum(jnp.exp(part - largest) for part in parts)
    lse = largest + jnp.log(total)
    along = jnp.zeros((48, 1), F32)
    value = jnp.zeros((48, 1), F32)
    summed = jnp.zeros((48, width), F32)
    for part, r, own in zip(got, riders, parts):
        weight = jnp.exp(own - lse)
        along += weight * (r[3] + r[4]) + (r[5] + r[6])
        value += r[7] + r[8]
        summed += weight * part[:, :width] + part[:, width + 64 : 2 * width + 64]
    loss_ref[...] = jnp.broadcast_to(value[:8] / (2.0 * 1536), (8, 128))
    proj_cot = (summed - unit_ref[...].astype(F32) * along).astype(BF)
    mixed = []
    for ref in (wa_ref, wb_ref):
        pool = lax.dot_general(proj_cot, ref[...], ROWS_DOT, preferred_element_type=F32)
        is_img = lax.broadcasted_iota(jnp.int32, pool.shape, 1) % 24 < 13
        mixed.append(jnp.where(is_img, pool, pltpu.roll(pool, 45, 0)))
    blank = jnp.zeros((1, pool.shape[1]), F32)
    pieces = []
    for k in range(8):
        for pool in mixed:
            pieces += [pool[6 * k : 6 * k + 3], blank]
    out_ref[...] = jnp.concatenate(pieces, 0).astype(BF)


def token_kernel(pool_ref, inv_ref, img_ref, txt_ref, ig_ref, tg_ref, img_out, txt_out):
    pool = pool_ref[...]
    inv = inv_ref[...][:, :1]
    for x_ref, gain_ref, out_ref, wide, skip, at in (
        (img_ref, ig_ref, img_out, 13, 0, 0),
        (txt_ref, tg_ref, txt_out, 10, 13, 4),
    ):
        dense = lax.broadcasted_iota(jnp.int32, (1, 32 * wide), 1)
        lane = lax.broadcasted_iota(jnp.int32, (768, 32 * wide), 0)
        pick = jnp.where(lane == slab_place(dense, wide, skip), 1.0, 0.0).astype(BF)
        found = jnp.dot(pool, pick, preferred_element_type=F32)
        halves = [
            found[32 * k : 32 * k + 8]
            + found[32 * k + 8 : 32 * k + 16]
            + found[32 * k + 16 : 32 * k + 24]
            + found[32 * k + 24 : 32 * k + 32]
            for k in range(2)
        ]
        cot = jnp.concatenate([halves[0][:4], halves[0][4:], halves[1][:4], halves[1][4:]], 1)
        cot = cot * inv[at : at + 4] * gain_ref[...][None]
        mean_cot = jnp.mean(cot, axis=1, keepdims=True)
        count = x_ref.shape[0] // 3
        for q in range(3):
            span = slice(count * q, count * q + count)
            values = x_ref[span, :].astype(F32)
            center = values - jnp.mean(values, axis=1, keepdims=True)
            inner = lax.rsqrt(jnp.mean(center * center, axis=1, keepdims=True) + 1e-05)
            mine = cot[q : q + 1]
            along = jnp.mean(center * mine, axis=1, keepdims=True)
            out = inner * (mine - mean_cot[q : q + 1]) - center * (inner * inner * inner * along)
            out_ref[span, :] = out.astype(BF)


def per_device(image_in, text_in, proj_img, proj_txt, img_gain, txt_gain, logit_scale, positive):
    t_index = lax.axis_index("t")
    h_index = lax.axis_index("h")
    g_index = (lax.axis_index("z") * 4 + lax.axis_index("x")) * 2 + lax.axis_index("c")
    y_index = h_index * 4 + t_index
    place = jnp.stack([y_index, h_index, t_index, g_index]).astype(jnp.int32)
    emb = proj_img.shape[1]

    width = emb // 4
    (w,) = kernel_call(weight_kernel, [((768, width), BF)], [place, proj_img, proj_txt], smem=(0,))
    wa, wb = both_cores(exchange(w.reshape(32, 24, width), ZX))

    spot = lax.iota(jnp.int32, 128)[None, :]
    digits = jnp.where(spot == 23, positive[:, None] // 32, 0)
    digits = jnp.where(spot == 47, positive[:, None] % 32, digits).astype(F32)
    digits = jnp.pad(digits, ((0, 4), (0, 0)))
    pooled = pool_call(image_in, text_in, img_gain, txt_gain, digits)
    pooled = lax.all_gather(pooled, "h", axis=0)
    row_pos = pooled[:, :12, 23].astype(F32) * 32.0 + pooled[:, :12, 47].astype(F32)
    row_pos = jnp.pad(row_pos.reshape(8, 3), ((0, 0), (0, 3)), constant_values=-1.0)
    row_pos = row_pos.reshape(48, 1).astype(jnp.int32)

    (part,) = kernel_call(
        project_kernel,
        [((192, 2 * width), BF)],
        [place, pooled.reshape(128, 768), wa, wb],
        smem=(0,),
    )
    parts = exchange(part.reshape(8, 24, 2 * width), Y).reshape(192, 2 * width)

    own_digits = lax.dynamic_slice(positive, (3 * t_index,), (3,))
    own_digits = jnp.concatenate([own_digits // 32, own_digits % 32]).astype(F32)
    own_digits = jnp.pad(own_digits, (0, 122))[None]
    rows, far, inv = kernel_call(
        unit_kernel,
        [((48, emb), BF), ((256, 1024), BF), ((8, 128), F32)],
        [place, parts, own_digits],
        scratch=[pltpu.VMEM((64, emb), F32), pltpu.VMEM((64, 128), F32)],
        smem=(0,),
    )
    fa, fb = both_cores(exchange(far.reshape(32, 8, 1024), ZX))

    scores, far = kernel_call(
        score_kernel,
        [((48, 512), F32), ((256, 128), F32)],
        [place, logit_scale, rows, fa, fb, row_pos],
        smem=(0, 1),
    )
    far = exchange(far.reshape(64, 4, 128), ZXC).reshape(256, 128)

    item_pos = jnp.concatenate([fa.reshape(32, 8, 1024)[:, 3, 768:774], fb.reshape(32, 8, 1024)[:, 3, 768:774]])
    item_pos = item_pos.astype(F32)
    item_pos = item_pos[:, :3] * 32.0 + item_pos[:, 3:]
    item_pos = jnp.pad(item_pos, ((0, 0), (0, 5)), constant_values=-1.0).reshape(1, 512)
    item_pos = item_pos.astype(jnp.int32)
    (ways,) = kernel_call(
        coef_kernel,
        [((384, 768), BF)],
        [place, logit_scale, scores, far, row_pos, item_pos, fa, fb],
        smem=(0, 1),
    )
    got = exchange(ways.reshape(8, 48, 768), Y).reshape(384, 768)
    unit_part = lax.dynamic_slice(rows, (0, width * t_index), (48, width))
    pool, loss = kernel_call(
        back_kernel, [((64, 768), BF), ((8, 128), F32)], [got, unit_part, wa, wb]
    )
    mean_loss = loss[0, :1]
    pool = exchange(pool.reshape(8, 8, 768), Y).reshape(64, 768)
    count_i, width_i = image_in.shape[1:]
    count_t, width_t = text_in.shape[1:]
    img_own = lax.dynamic_slice_in_dim(image_in, 3 * t_index, 3, 0).reshape(-1, width_i)
    txt_own = lax.dynamic_slice_in_dim(text_in, 3 * t_index, 3, 0).reshape(-1, width_t)
    img_grads, txt_grads = kernel_call(
        token_kernel,
        [(img_own.shape, BF), (txt_own.shape, BF)],
        [pool, inv, img_own, txt_own, img_gain, txt_gain],
    )
    img_grads = img_grads.reshape(3, count_i, width_i)
    txt_grads = txt_grads.reshape(3, count_t, width_t)
    return (mean_loss, img_grads[None], txt_grads[None])


def solution(mesh):
    fine = Mesh(mesh.devices.reshape(4, 2, 8, 4, 2), ("t", "h", "z", "x", "c"))
    in_specs = (
        P(DP, None, None),
        P(DP, None, None),
        P(DP, None),
        P(DP, None),
        P(),
        P(),
        P(),
        P(DP),
    )
    out_specs = (P(), P("t", DP, None, None), P("t", DP, None, None))
    return jax.shard_map(
        per_device, mesh=fine, in_specs=in_specs, out_specs=out_specs, check_vma=False
    )
```

```python
import functools

import jax
import jax.numpy as jnp
from jax import lax
from jax.experimental import pallas as pl
from jax.experimental.pallas import tpu as pltpu
from jax.sharding import Mesh, PartitionSpec as P

BF = jnp.bfloat16
F32 = jnp.float32
Y = ("h", "t")
ZX = ("z", "x")
ZXC = ("z", "x", "c")
DP = ("h", "z", "x", "c")
LOW = -1e30
ROWS_DOT = (((1,), (1,)), ((), ()))


def exchange(blocks, axes):
    return lax.all_to_all(blocks, axes, 0, 0, tiled=True)


def both_cores(blocks):
    half = blocks.shape[0] // 2
    parts = [lax.all_gather(part, "c", axis=0) for part in (blocks[:half], blocks[half:])]
    return [part.reshape(-1, blocks.shape[2]) for part in parts]


def kernel_call(body, outs, args, scratch=(), smem=()):
    vmem = pl.BlockSpec(memory_space=pltpu.VMEM)
    return pl.pallas_call(
        body,
        out_shape=[jax.ShapeDtypeStruct(shape, kind) for shape, kind in outs],
        in_specs=[
            pl.BlockSpec(memory_space=pltpu.SMEM) if k in smem else vmem for k in range(len(args))
        ],
        out_specs=[vmem] * len(outs),
        scratch_shapes=list(scratch),
        compiler_params=pltpu.CompilerParams(vmem_limit_bytes=40 * 1024 * 1024),
    )(*args)


def slab_place(dense, wide, skip):
    return ((dense // wide) % 2) * 384 + (dense // (2 * wide)) * 24 + skip + dense % wide


def pool_kernel(
    pos_ref, img_ref, txt_ref, ig_ref, tg_ref, out_ref, img_held, txt_held, img_rows, txt_rows, digits, sems
):
    pairs = img_ref.shape[0]

    def copies(k):
        return (
            pltpu.make_async_copy(img_ref.at[k], img_held.at[k], sems.at[0, k]),
            pltpu.make_async_copy(txt_ref.at[k], txt_held.at[k], sems.at[1, k]),
        )

    for k in range(pairs):
        for copy in copies(k):
            copy.start()
    for rows in (img_rows, txt_rows, digits):
        rows[...] = jnp.zeros_like(rows)
    spot = lax.broadcasted_iota(jnp.int32, (1, 128), 1)

    def one_pair(k, carry):
        for copy in copies(k):
            copy.wait()
        for held, gain_ref, rows in ((img_held, ig_ref, img_rows), (txt_held, tg_ref, txt_rows)):
            values = held[k].astype(F32)
            center = values - jnp.mean(values, axis=1, keepdims=True)
            spread = jnp.mean(center * center, axis=1, keepdims=True)
            mean = jnp.mean(center * lax.rsqrt(spread + 1e-05), axis=0, keepdims=True)
            rows[pl.ds(k, 1), :] = mean * gain_ref[...][None]
        place = pos_ref[k]
        line = jnp.where(spot == 23, place // 32, jnp.where(spot == 47, place % 32, 0))
        digits[pl.ds(k, 1), :] = line.astype(F32)
        return carry

    lax.fori_loop(0, pairs, one_pair, 0)
    found = jnp.zeros((64, 768), F32)
    for rows, wide, skip in ((img_rows, 13, 0), (txt_rows, 10, 13)):
        width = 32 * wide
        dense = lax.broadcasted_iota(jnp.int32, (width, 768), 0)
        lane = lax.broadcasted_iota(jnp.int32, (width, 768), 1)
        pick = jnp.where(lane == slab_place(dense, wide, skip), 1.0, 0.0).astype(BF)
        held = rows[...]
        quarters = [held[:, width * k : width * k + width] for k in range(4)]
        quarters = jnp.concatenate(quarters, 0).astype(BF)
        found += jnp.dot(quarters, pick, preferred_element_type=F32)
    line = digits[...]
    blank = jnp.zeros_like(line)
    line = jnp.concatenate([line, blank, line, blank], 0)
    found = jnp.concatenate([found[:, :128] + line, found[:, 128:]], 1)
    out_ref[...] = found.astype(BF)


def pool_call(image_in, text_in, img_gain, txt_gain, positive):
    pairs, count_i, width_i = image_in.shape
    _, count_t, width_t = text_in.shape
    vmem = pl.BlockSpec(memory_space=pltpu.VMEM)
    return pl.pallas_call(
        pool_kernel,
        out_shape=jax.ShapeDtypeStruct((64, 768), BF),
        in_specs=[
            pl.BlockSpec(memory_space=pltpu.SMEM),
            pl.BlockSpec(memory_space=pl.ANY),
            pl.BlockSpec(memory_space=pl.ANY),
            vmem,
            vmem,
        ],
        out_specs=vmem,
        scratch_shapes=[
            pltpu.VMEM(image_in.shape, BF),
            pltpu.VMEM(text_in.shape, BF),
            pltpu.VMEM((16, width_i), F32),
            pltpu.VMEM((16, width_t), F32),
            pltpu.VMEM((16, 128), F32),
            pltpu.SemaphoreType.DMA((2, pairs)),
        ],
        cost_estimate=pl.CostEstimate(
            flops=10 * (image_in.size + text_in.size),
            bytes_accessed=2 * (image_in.size + text_in.size),
            transcendentals=0,
        ),
        compiler_params=pltpu.CompilerParams(vmem_limit_bytes=60 * 1024 * 1024),
    )(positive, image_in, text_in, img_gain, txt_gain)


def project_kernel(place_ref, pooled_ref, wa_ref, wb_ref, out_ref):
    part = jnp.zeros((48, wa_ref.shape[1]), F32)
    inside = lax.broadcasted_iota(jnp.int32, (12, 768), 1) % 24
    for a, w_ref in enumerate((wa_ref, wb_ref)):
        pieces = []
        for h in range(2):
            start = pl.multiple_of(64 * h + 32 * place_ref[1] + 16 * a, 16)
            rows = pooled_ref[pl.ds(start, 16), :].astype(F32)[:12]
            img_rows = jnp.where(inside < 13, rows, 0.0)
            txt_rows = jnp.where((inside >= 13) & (inside < 23), rows, 0.0)
            for t in range(4):
                pieces += [img_rows[3 * t : 3 * t + 3], txt_rows[3 * t : 3 * t + 3]]
        left = jnp.concatenate(pieces, 0).astype(BF)
        part += jnp.dot(left, w_ref[...], preferred_element_type=F32)
    packed = jnp.concatenate([part[:24], part[24:]], 1)
    out_ref[...] = jnp.concatenate([packed] * 8, 0).astype(BF)


def in_blocks(values):
    blank = jnp.zeros((1, values.shape[1]), F32)
    pieces = []
    for k in range(8):
        pieces += [values[6 * k : 6 * k + 3], blank, values[6 * k + 3 : 6 * k + 6], blank]
    return jnp.concatenate(pieces, 0)


def unit_kernel(place_ref, parts_ref, digits_ref, rows_ref, far_ref, inv_ref, held, held_inv):
    spread = parts_ref[...].astype(F32)
    width = spread.shape[1] // 2
    blocks = [spread[24 * k : 24 * k + 24] + spread[96 + 24 * k : 120 + 24 * k] for k in range(4)]
    blocks = [jnp.concatenate([part[:, :width], part[:, width:]], 0) for part in blocks]
    projected = jnp.concatenate(blocks, 1)
    inv = lax.rsqrt(jnp.sum(projected * projected, axis=1, keepdims=True) + 1e-06)
    unit = projected * inv
    rows_ref[...] = unit.astype(BF)
    held[...] = in_blocks(unit)
    held_inv[...] = in_blocks(jnp.broadcast_to(inv, (48, 128)))
    own = pl.ds(pl.multiple_of(8 * place_ref[0], 8), 8)
    inv_ref[...] = held_inv[own, :]
    block = held[own, :]
    free = jnp.concatenate([digits_ref[...], jnp.zeros((1, 128), F32)], 1)
    pieces = []
    for k in (0, 4):
        ends = [block[k + q : k + q + 1, 1024:] for q in range(3)]
        pieces += [block[k : k + 3, :1024], jnp.concatenate(ends + [free], 1)]
    block = jnp.concatenate(pieces, 0)
    block = jnp.concatenate([block, block], 0).astype(BF)
    for k in range(16):
        far_ref[16 * k : 16 * k + 16, :] = block


def tile_masks(place_ref):
    h, t, g = place_ref[1], place_ref[2], place_ref[3]
    row = lax.broadcasted_iota(jnp.int32, (48, 512), 0)
    item = lax.broadcasted_iota(jnp.int32, (48, 512), 1)
    item_g = ((item // 256) * 16 + (item % 128) // 8) * 2 + (item // 128) % 2
    item_pair = (h * 64 + item_g) * 12 + 3 * t + item % 4
    row_pair = ((row // 24) * 64 + g) * 12 + ((row // 6) % 4) * 3 + row % 3
    row_txt, item_txt = (row % 6) // 3, (item % 8) // 4
    valid = (row_txt != item_txt) & (item % 4 < 3)
    return valid, row_pair, item_pair, row_txt, item


def log_total(values, axis):
    largest = jnp.max(values, axis=axis, keepdims=True)
    return largest + jnp.log(jnp.sum(jnp.exp(values - largest), axis=axis, keepdims=True))


def score_kernel(place_ref, logit_ref, rows_ref, fa_ref, fb_ref, row_pos_ref, scores_ref, far_ref):
    rows = rows_ref[...]
    ends = rows[:, 1024:]
    blank = jnp.zeros_like(ends)
    ends = [[ends if k == q else blank for k in range(3)] for q in range(3)]
    ends = jnp.concatenate([jnp.concatenate(line, 1) for line in ends], 0)

    def dots(left, width):
        return jnp.concatenate(
            [
                lax.dot_general(left, ref[:, :width], ROWS_DOT, preferred_element_type=F32)
                for ref in (fa_ref, fb_ref)
            ],
            1,
        )

    scores = dots(rows[:, :1024], 1024)
    ends = dots(ends, 768)
    lane = lax.broadcasted_iota(jnp.int32, (48, 512), 1) % 4
    for q in range(3):
        moved = pltpu.roll(ends[48 * q : 48 * q + 48], 512 - (3 - q), 1)
        scores += jnp.where(lane == q, moved, 0.0)
    scores = logit_ref[0] * scores
    scores_ref[...] = scores
    valid, _, item_pair, row_txt, _ = tile_masks(place_ref)
    masked = jnp.where(valid, scores, LOW)
    item_part = log_total(masked, 0)
    hit = valid & (row_txt == 0) & (row_pos_ref[...] == item_pair)
    matched = jnp.sum(
        jnp.sum(jnp.where(hit, scores, 0.0), axis=1, keepdims=True), axis=0, keepdims=True
    )
    lane = lax.broadcasted_iota(jnp.int32, (1, 512), 1)
    item_part = jnp.where(lane == 3, matched, item_part)
    lines = jnp.concatenate([item_part[:, 128 * k : 128 * k + 128] for k in range(4)] * 2, 0)
    for k in range(32):
        far_ref[8 * k : 8 * k + 8, :] = lines


def in_parts(values, count):
    parts = []
    for _ in range(count):
        part = values.astype(BF).astype(F32)
        parts.append(part)
        values = values - part
    return parts


def coef_kernel(
    place_ref, logit_ref, scores_ref, far_ref, row_pos_ref, item_pos_ref, fa_ref, fb_ref, out_ref
):
    logit = logit_ref[0]
    scores = scores_ref[...]
    seen = far_ref[...].reshape(32, 8, 128)
    largest = jnp.max(seen, axis=0)
    largest = jnp.maximum(largest[:4], largest[4:])
    both = jnp.concatenate([largest, largest], 0)
    total = jnp.sum(jnp.exp(seen - both[None]), axis=0)
    lines = largest + jnp.log(total[:4] + total[4:])
    item_lse = jnp.concatenate([lines[k : k + 1] for k in range(4)], 1)
    summed = jnp.sum(seen, axis=0)
    summed = summed[:1] + summed[4:5]
    valid, row_pair, item_pair, row_txt, item = tile_masks(place_ref)
    from_img = row_txt == 0
    hit = valid & (
        jnp.where(from_img, row_pos_ref[...], row_pair)
        == jnp.where(from_img, item_pair, item_pos_ref[...])
    )
    real = item[:1] % 4 < 3
    lse_total = jnp.sum(jnp.where(real, item_lse, 0.0), axis=1, keepdims=True)
    lane = lax.broadcasted_iota(jnp.int32, (1, 128), 1)
    matched = jnp.sum(jnp.where(lane == 3, summed, 0.0), axis=1, keepdims=True)
    value = lse_total - 2.0 * matched
    masked = jnp.where(valid, scores, LOW)
    row_part = log_total(masked, 1)
    by_row = (0.5 * logit) * jnp.exp(masked - row_part)
    by_item = (0.5 * logit) * (jnp.exp(masked - item_lse) - jnp.where(hit, 2.0, 0.0))
    coefs = [jnp.where(valid, part, 0.0).astype(BF) for part in (by_row, by_item)]
    along = [
        jnp.sum(part.astype(F32) * scores, axis=1, keepdims=True) / logit for part in coefs
    ]
    coef = jnp.concatenate(coefs, 0)

    def times_items(left, columns):
        return jnp.dot(left[:, :256], fa_ref[:, columns], preferred_element_type=F32) + jnp.dot(
            left[:, 256:], fb_ref[:, columns], preferred_element_type=F32
        )

    cot = times_items(coef, slice(0, 1024))
    last = lax.broadcasted_iota(jnp.int32, (96, 512), 1) % 4 == 3
    wide = coef.astype(F32)
    ends = jnp.zeros((96, 256), F32)
    for q in range(3):
        moved = jnp.where(last, pltpu.roll(wide, 3 - q, 1), 0.0).astype(BF)
        ends += times_items(moved, slice(256 * q, 256 * q + 256))
    cot = jnp.concatenate([cot, ends], 1)

    riders = (
        in_parts(row_part, 3)
        + in_parts(along[0], 2)
        + in_parts(along[1], 2)
        + in_parts(jnp.broadcast_to(value, (48, 1)), 2)
    )
    column = lax.broadcasted_iota(jnp.int32, (48, 64), 1)
    extra = jnp.zeros((48, 64), F32)
    for k, rider in enumerate(riders):
        extra = jnp.where(column == k, rider, extra)
    blank = jnp.zeros((48, 64), F32)
    width = cot.shape[1] // 4
    for k in range(4):
        part = cot[:, width * k : width * k + width]
        way = jnp.concatenate([part[:48], extra, part[48:], blank], 1).astype(BF)
        out_ref[48 * k : 48 * k + 48, :] = way
        out_ref[192 + 48 * k : 240 + 48 * k, :] = way


def back_kernel(got_ref, unit_ref, wa_ref, wb_ref, out_ref, loss_ref):
    width = unit_ref.shape[1]
    got = [got_ref[48 * k : 48 * k + 48, :].astype(F32) for k in range(8)]
    riders = [[part[:, width + k : width + k + 1] for k in range(9)] for part in got]
    parts = [r[0] + r[1] + r[2] for r in riders]
    largest = functools.reduce(jnp.maximum, parts)
    total = sum(jnp.exp(part - largest) for part in parts)
    lse = largest + jnp.log(total)
    along = jnp.zeros((48, 1), F32)
    value = jnp.zeros((48, 1), F32)
    summed = jnp.zeros((48, width), F32)
    for part, r, own in zip(got, riders, parts):
        weight = jnp.exp(own - lse)
        along += weight * (r[3] + r[4]) + (r[5] + r[6])
        value += r[7] + r[8]
        summed += weight * part[:, :width] + part[:, width + 64 : 2 * width + 64]
    loss_ref[...] = jnp.broadcast_to(value[:8] / (2.0 * 1536), (8, 128))
    proj_cot = (summed - unit_ref[...].astype(F32) * along).astype(BF)
    mixed = []
    for ref in (wa_ref, wb_ref):
        pool = lax.dot_general(proj_cot, ref[...], ROWS_DOT, preferred_element_type=F32)
        is_img = lax.broadcasted_iota(jnp.int32, pool.shape, 1) % 24 < 13
        mixed.append(jnp.where(is_img, pool, pltpu.roll(pool, 45, 0)))
    blank = jnp.zeros((1, pool.shape[1]), F32)
    pieces = []
    for k in range(8):
        for pool in mixed:
            pieces += [pool[6 * k : 6 * k + 3], blank]
    out_ref[...] = jnp.concatenate(pieces, 0).astype(BF)


def token_kernel(pool_ref, inv_ref, img_ref, txt_ref, ig_ref, tg_ref, img_out, txt_out):
    pool = pool_ref[...]
    inv = inv_ref[...][:, :1]
    for x_ref, gain_ref, out_ref, wide, skip, at in (
        (img_ref, ig_ref, img_out, 13, 0, 0),
        (txt_ref, tg_ref, txt_out, 10, 13, 4),
    ):
        dense = lax.broadcasted_iota(jnp.int32, (1, 32 * wide), 1)
        lane = lax.broadcasted_iota(jnp.int32, (768, 32 * wide), 0)
        pick = jnp.where(lane == slab_place(dense, wide, skip), 1.0, 0.0).astype(BF)
        found = jnp.dot(pool, pick, preferred_element_type=F32)
        halves = [
            found[32 * k : 32 * k + 8]
            + found[32 * k + 8 : 32 * k + 16]
            + found[32 * k + 16 : 32 * k + 24]
            + found[32 * k + 24 : 32 * k + 32]
            for k in range(2)
        ]
        cot = jnp.concatenate([halves[0][:4], halves[0][4:], halves[1][:4], halves[1][4:]], 1)
        cot = cot * inv[at : at + 4] * gain_ref[...][None]
        mean_cot = jnp.mean(cot, axis=1, keepdims=True)
        count = x_ref.shape[0] // 3
        for q in range(3):
            span = slice(count * q, count * q + count)
            values = x_ref[span, :].astype(F32)
            center = values - jnp.mean(values, axis=1, keepdims=True)
            inner = lax.rsqrt(jnp.mean(center * center, axis=1, keepdims=True) + 1e-05)
            mine = cot[q : q + 1]
            along = jnp.mean(center * mine, axis=1, keepdims=True)
            out = inner * (mine - mean_cot[q : q + 1]) - center * (inner * inner * inner * along)
            out_ref[span, :] = out.astype(BF)


def per_device(image_in, text_in, proj_img, proj_txt, img_gain, txt_gain, logit_scale, positive):
    t_index = lax.axis_index("t")
    h_index = lax.axis_index("h")
    g_index = (lax.axis_index("z") * 4 + lax.axis_index("x")) * 2 + lax.axis_index("c")
    y_index = h_index * 4 + t_index
    place = jnp.stack([y_index, h_index, t_index, g_index]).astype(jnp.int32)
    emb = proj_img.shape[1]

    width = emb // 4
    w = jnp.concatenate([proj_img, proj_txt, jnp.zeros((1, emb), BF)], 0)
    w = lax.dynamic_slice(w, (0, width * t_index), (24, width))
    w = jnp.broadcast_to(w[None], (32, 24, width))
    wa, wb = both_cores(exchange(w, ZX))

    pooled = pool_call(image_in, text_in, img_gain, txt_gain, positive)
    pooled = lax.all_gather(pooled, Y, axis=0, axis_index_groups=[[0, 6], [1, 7], [2, 4], [3, 5]])
    row_pos = pooled[:, :12, 23].astype(F32) * 32.0 + pooled[:, :12, 47].astype(F32)
    row_pos = jnp.pad(row_pos.reshape(8, 3), ((0, 0), (0, 3)), constant_values=-1.0)
    row_pos = row_pos.reshape(48, 1).astype(jnp.int32)

    (part,) = kernel_call(
        project_kernel,
        [((192, 2 * width), BF)],
        [place, pooled.reshape(128, 768), wa, wb],
        smem=(0,),
    )
    parts = exchange(part.reshape(8, 24, 2 * width), Y).reshape(192, 2 * width)

    own_digits = lax.dynamic_slice(positive, (3 * t_index,), (3,))
    own_digits = jnp.concatenate([own_digits // 32, own_digits % 32]).astype(F32)
    own_digits = jnp.pad(own_digits, (0, 122))[None]
    rows, far, inv = kernel_call(
        unit_kernel,
        [((48, emb), BF), ((256, 1024), BF), ((8, 128), F32)],
        [place, parts, own_digits],
        scratch=[pltpu.VMEM((64, emb), F32), pltpu.VMEM((64, 128), F32)],
        smem=(0,),
    )
    fa, fb = both_cores(exchange(far.reshape(32, 8, 1024), ZX))

    scores, far = kernel_call(
        score_kernel,
        [((48, 512), F32), ((256, 128), F32)],
        [place, logit_scale, rows, fa, fb, row_pos],
        smem=(0, 1),
    )
    far = exchange(far.reshape(64, 4, 128), ZXC).reshape(256, 128)

    item_pos = jnp.concatenate([fa.reshape(32, 8, 1024)[:, 3, 768:774], fb.reshape(32, 8, 1024)[:, 3, 768:774]])
    item_pos = item_pos.astype(F32)
    item_pos = item_pos[:, :3] * 32.0 + item_pos[:, 3:]
    item_pos = jnp.pad(item_pos, ((0, 0), (0, 5)), constant_values=-1.0).reshape(1, 512)
    item_pos = item_pos.astype(jnp.int32)
    (ways,) = kernel_call(
        coef_kernel,
        [((384, 768), BF)],
        [place, logit_scale, scores, far, row_pos, item_pos, fa, fb],
        smem=(0, 1),
    )
    got = exchange(ways.reshape(8, 48, 768), Y).reshape(384, 768)
    unit_part = lax.dynamic_slice(rows, (0, width * t_index), (48, width))
    pool, loss = kernel_call(
        back_kernel, [((64, 768), BF), ((8, 128), F32)], [got, unit_part, wa, wb]
    )
    mean_loss = loss[0, :1]
    pool = exchange(pool.reshape(8, 8, 768), Y).reshape(64, 768)
    count_i, width_i = image_in.shape[1:]
    count_t, width_t = text_in.shape[1:]
    img_own = lax.dynamic_slice_in_dim(image_in, 3 * t_index, 3, 0).reshape(-1, width_i)
    txt_own = lax.dynamic_slice_in_dim(text_in, 3 * t_index, 3, 0).reshape(-1, width_t)
    img_grads, txt_grads = kernel_call(
        token_kernel,
        [(img_own.shape, BF), (txt_own.shape, BF)],
        [pool, inv, img_own, txt_own, img_gain, txt_gain],
    )
    img_grads = img_grads.reshape(3, count_i, width_i)
    txt_grads = txt_grads.reshape(3, count_t, width_t)
    return (mean_loss, img_grads[None], txt_grads[None])


def solution(mesh):
    fine = Mesh(mesh.devices.reshape(4, 2, 8, 4, 2), ("t", "h", "z", "x", "c"))
    in_specs = (
        P(DP, None, None),
        P(DP, None, None),
        P(DP, None),
        P(DP, None),
        P(),
        P(),
        P(),
        P(DP),
    )
    out_specs = (P(), P("t", DP, None, None), P("t", DP, None, None))
    return jax.shard_map(
        per_device, mesh=fine, in_specs=in_specs, out_specs=out_specs, check_vma=False
    )
```

```python
import functools

import jax
import jax.numpy as jnp
from jax import lax
from jax.experimental import pallas as pl
from jax.experimental.pallas import tpu as pltpu
from jax.sharding import Mesh, PartitionSpec as P

BF = jnp.bfloat16
F32 = jnp.float32
Y = ("h", "t")
ZX = ("z", "x")
ZXC = ("z", "x", "c")
DP = ("h", "z", "x", "c")
LOW = -1e30
ROWS_DOT = (((1,), (1,)), ((), ()))


def exchange(blocks, axes):
    return lax.all_to_all(blocks, axes, 0, 0, tiled=True)


def both_cores(blocks):
    half = blocks.shape[0] // 2
    parts = [lax.all_gather(part, "c", axis=0) for part in (blocks[:half], blocks[half:])]
    return [part.reshape(-1, blocks.shape[2]) for part in parts]


def kernel_call(body, outs, args, scratch=(), smem=()):
    vmem = pl.BlockSpec(memory_space=pltpu.VMEM)
    return pl.pallas_call(
        body,
        out_shape=[jax.ShapeDtypeStruct(shape, kind) for shape, kind in outs],
        in_specs=[
            pl.BlockSpec(memory_space=pltpu.SMEM) if k in smem else vmem for k in range(len(args))
        ],
        out_specs=[vmem] * len(outs),
        scratch_shapes=list(scratch),
        compiler_params=pltpu.CompilerParams(vmem_limit_bytes=40 * 1024 * 1024),
    )(*args)


def slab_place(dense, wide, skip):
    row = skip + dense % wide
    return (row // 8) * 256 + ((dense // wide) % 2) * 128 + (dense // (2 * wide)) * 8 + row % 8


def slab_row(shape):
    lane = lax.broadcasted_iota(jnp.int32, shape, 1)
    return (lane // 256) * 8 + lane % 8


def pool_kernel(
    pos_ref, img_ref, txt_ref, ig_ref, tg_ref, out_ref, img_held, txt_held, img_rows, txt_rows, digits, sems
):
    pairs = img_ref.shape[0]

    def copies(k):
        return (
            pltpu.make_async_copy(img_ref.at[k], img_held.at[k], sems.at[0, k]),
            pltpu.make_async_copy(txt_ref.at[k], txt_held.at[k], sems.at[1, k]),
        )

    for k in range(pairs):
        for copy in copies(k):
            copy.start()
    for rows in (img_rows, txt_rows, digits):
        rows[...] = jnp.zeros_like(rows)
    spot = lax.broadcasted_iota(jnp.int32, (1, 128), 1)

    def one_pair(k, carry):
        for copy in copies(k):
            copy.wait()
        for held, gain_ref, rows in ((img_held, ig_ref, img_rows), (txt_held, tg_ref, txt_rows)):
            values = held[k].astype(F32)
            center = values - jnp.mean(values, axis=1, keepdims=True)
            spread = jnp.mean(center * center, axis=1, keepdims=True)
            mean = jnp.mean(center * lax.rsqrt(spread + 1e-05), axis=0, keepdims=True)
            rows[pl.ds(k, 1), :] = mean * gain_ref[...][None]
        place = pos_ref[k]
        line = jnp.where(spot == 7, place // 32, jnp.where(spot == 15, place % 32, 0))
        digits[pl.ds(k, 1), :] = line.astype(F32)
        return carry

    lax.fori_loop(0, pairs, one_pair, 0)
    found = jnp.zeros((64, 768), F32)
    for rows, wide, skip in ((img_rows, 13, 0), (txt_rows, 10, 13)):
        width = 32 * wide
        dense = lax.broadcasted_iota(jnp.int32, (width, 768), 0)
        lane = lax.broadcasted_iota(jnp.int32, (width, 768), 1)
        pick = jnp.where(lane == slab_place(dense, wide, skip), 1.0, 0.0).astype(BF)
        held = rows[...]
        quarters = [held[:, width * k : width * k + width] for k in range(4)]
        quarters = jnp.concatenate(quarters, 0).astype(BF)
        found += jnp.dot(quarters, pick, preferred_element_type=F32)
    line = digits[...]
    blank = jnp.zeros_like(line)
    line = jnp.concatenate([line, blank, line, blank], 0)
    found = jnp.concatenate([found[:, :512], found[:, 512:640] + line, found[:, 640:]], 1)
    out_ref[...] = found.astype(BF)


def pool_call(image_in, text_in, img_gain, txt_gain, positive):
    pairs, count_i, width_i = image_in.shape
    _, count_t, width_t = text_in.shape
    vmem = pl.BlockSpec(memory_space=pltpu.VMEM)
    return pl.pallas_call(
        pool_kernel,
        out_shape=jax.ShapeDtypeStruct((64, 768), BF),
        in_specs=[
            pl.BlockSpec(memory_space=pltpu.SMEM),
            pl.BlockSpec(memory_space=pl.ANY),
            pl.BlockSpec(memory_space=pl.ANY),
            vmem,
            vmem,
        ],
        out_specs=vmem,
        scratch_shapes=[
            pltpu.VMEM(image_in.shape, BF),
            pltpu.VMEM(text_in.shape, BF),
            pltpu.VMEM((16, width_i), F32),
            pltpu.VMEM((16, width_t), F32),
            pltpu.VMEM((16, 128), F32),
            pltpu.SemaphoreType.DMA((2, pairs)),
        ],
        cost_estimate=pl.CostEstimate(
            flops=10 * (image_in.size + text_in.size),
            bytes_accessed=2 * (image_in.size + text_in.size),
            transcendentals=0,
        ),
        compiler_params=pltpu.CompilerParams(vmem_limit_bytes=60 * 1024 * 1024),
    )(positive, image_in, text_in, img_gain, txt_gain)


def project_kernel(place_ref, pooled_ref, wa_ref, wb_ref, out_ref):
    width = wa_ref.shape[1] // 3
    part = jnp.zeros((48, width), F32)
    inside = slab_row((12, 768))
    for a, w_ref in enumerate((wa_ref, wb_ref)):
        pieces = []
        for h in range(2):
            start = pl.multiple_of(64 * h + 32 * place_ref[1] + 16 * a, 16)
            rows = pooled_ref[pl.ds(start, 16), :].astype(F32)[:12]
            img_rows = jnp.where(inside < 13, rows, 0.0)
            txt_rows = jnp.where((inside >= 13) & (inside < 23), rows, 0.0)
            for t in range(4):
                pieces += [img_rows[3 * t : 3 * t + 3], txt_rows[3 * t : 3 * t + 3]]
        left = jnp.concatenate(pieces, 0).astype(BF)
        for j in range(3):
            part += jnp.dot(
                left[:, 256 * j : 256 * j + 256],
                w_ref[:, width * j : width * j + width],
                preferred_element_type=F32,
            )
    packed = jnp.concatenate([part[:24], part[24:]], 1)
    out_ref[...] = jnp.concatenate([packed] * 8, 0).astype(BF)


def in_blocks(values):
    blank = jnp.zeros((1, values.shape[1]), F32)
    pieces = []
    for k in range(8):
        pieces += [values[6 * k : 6 * k + 3], blank, values[6 * k + 3 : 6 * k + 6], blank]
    return jnp.concatenate(pieces, 0)


def unit_kernel(place_ref, parts_ref, digits_ref, rows_ref, far_ref, inv_ref, held, held_inv):
    spread = parts_ref[...].astype(F32)
    width = spread.shape[1] // 2
    blocks = [spread[24 * k : 24 * k + 24] + spread[96 + 24 * k : 120 + 24 * k] for k in range(4)]
    blocks = [jnp.concatenate([part[:, :width], part[:, width:]], 0) for part in blocks]
    projected = jnp.concatenate(blocks, 1)
    inv = lax.rsqrt(jnp.sum(projected * projected, axis=1, keepdims=True) + 1e-06)
    unit = projected * inv
    rows_ref[...] = unit.astype(BF)
    held[...] = in_blocks(unit)
    held_inv[...] = in_blocks(jnp.broadcast_to(inv, (48, 128)))
    own = pl.ds(pl.multiple_of(8 * place_ref[0], 8), 8)
    inv_ref[...] = held_inv[own, :]
    block = held[own, :]
    free = jnp.concatenate([digits_ref[...], jnp.zeros((1, 128), F32)], 1)
    pieces = []
    for k in (0, 4):
        ends = [block[k + q : k + q + 1, 1024:] for q in range(3)]
        pieces += [block[k : k + 3, :1024], jnp.concatenate(ends + [free], 1)]
    block = jnp.concatenate(pieces, 0)
    block = jnp.concatenate([block, block], 0).astype(BF)
    for k in range(16):
        far_ref[16 * k : 16 * k + 16, :] = block


def tile_masks(place_ref):
    h, t, g = place_ref[1], place_ref[2], place_ref[3]
    row = lax.broadcasted_iota(jnp.int32, (48, 512), 0)
    item = lax.broadcasted_iota(jnp.int32, (48, 512), 1)
    item_g = ((item // 256) * 16 + (item % 128) // 8) * 2 + (item // 128) % 2
    item_pair = (h * 64 + item_g) * 12 + 3 * t + item % 4
    row_pair = ((row // 24) * 64 + g) * 12 + ((row // 6) % 4) * 3 + row % 3
    row_txt, item_txt = (row % 6) // 3, (item % 8) // 4
    valid = (row_txt != item_txt) & (item % 4 < 3)
    return valid, row_pair, item_pair, row_txt, item


def log_total(values, axis):
    largest = jnp.max(values, axis=axis, keepdims=True)
    return largest + jnp.log(jnp.sum(jnp.exp(values - largest), axis=axis, keepdims=True))


def score_kernel(place_ref, logit_ref, rows_ref, fa_ref, fb_ref, row_pos_ref, scores_ref, far_ref):
    rows = rows_ref[...]
    ends = rows[:, 1024:]
    blank = jnp.zeros_like(ends)
    ends = [[ends if k == q else blank for k in range(3)] for q in range(3)]
    ends = jnp.concatenate([jnp.concatenate(line, 1) for line in ends], 0)

    def dots(left, width):
        return jnp.concatenate(
            [
                lax.dot_general(left, ref[:, :width], ROWS_DOT, preferred_element_type=F32)
                for ref in (fa_ref, fb_ref)
            ],
            1,
        )

    scores = dots(rows[:, :1024], 1024)
    ends = dots(ends, 768)
    lane = lax.broadcasted_iota(jnp.int32, (48, 512), 1) % 4
    for q in range(3):
        moved = pltpu.roll(ends[48 * q : 48 * q + 48], 512 - (3 - q), 1)
        scores += jnp.where(lane == q, moved, 0.0)
    scores = logit_ref[0] * scores
    scores_ref[...] = scores
    valid, _, item_pair, row_txt, _ = tile_masks(place_ref)
    masked = jnp.where(valid, scores, LOW)
    item_part = log_total(masked, 0)
    hit = valid & (row_txt == 0) & (row_pos_ref[...] == item_pair)
    matched = jnp.sum(
        jnp.sum(jnp.where(hit, scores, 0.0), axis=1, keepdims=True), axis=0, keepdims=True
    )
    lane = lax.broadcasted_iota(jnp.int32, (1, 512), 1)
    item_part = jnp.where(lane == 3, matched, item_part)
    lines = jnp.concatenate([item_part[:, 128 * k : 128 * k + 128] for k in range(4)] * 2, 0)
    for k in range(32):
        far_ref[8 * k : 8 * k + 8, :] = lines


def in_parts(values, count):
    parts = []
    for _ in range(count):
        part = values.astype(BF).astype(F32)
        parts.append(part)
        values = values - part
    return parts


def times_items(left, fa_ref, fb_ref):
    def times(part, columns):
        return jnp.dot(part[:, :256], fa_ref[:, columns], preferred_element_type=F32) + jnp.dot(
            part[:, 256:], fb_ref[:, columns], preferred_element_type=F32
        )

    start = times(left, slice(0, 1024))
    last = lax.broadcasted_iota(jnp.int32, left.shape, 1) % 4 == 3
    wide = left.astype(F32)
    ends = jnp.zeros((left.shape[0], 256), F32)
    for q in range(3):
        moved = jnp.where(last, pltpu.roll(wide, 3 - q, 1), 0.0).astype(BF)
        ends += times(moved, slice(256 * q, 256 * q + 256))
    return jnp.concatenate([start, ends], 1)


def in_columns(parts, first):
    column = lax.broadcasted_iota(jnp.int32, (48, 128), 1)
    out = jnp.zeros((48, 128), F32)
    for k, part in enumerate(parts):
        out = jnp.where(column == first + k, part, out)
    return out


def row_kernel(place_ref, logit_ref, scores_ref, fa_ref, fb_ref, cot_ref, riders_ref):
    logit = logit_ref[0]
    scores = scores_ref[...]
    valid = tile_masks(place_ref)[0]
    masked = jnp.where(valid, scores, LOW)
    row_part = log_total(masked, 1)
    coef = jnp.where(valid, (0.5 * logit) * jnp.exp(masked - row_part), 0.0).astype(BF)
    along = jnp.sum(coef.astype(F32) * scores, axis=1, keepdims=True) / logit
    cot_ref[...] = times_items(coef, fa_ref, fb_ref)
    riders_ref[...] = in_columns(in_parts(row_part, 3) + in_parts(along, 2), 0)


def coef_kernel(
    place_ref,
    logit_ref,
    scores_ref,
    far_ref,
    row_pos_ref,
    item_pos_ref,
    fa_ref,
    fb_ref,
    by_row_ref,
    riders_ref,
    out_ref,
):
    logit = logit_ref[0]
    scores = scores_ref[...]
    seen = far_ref[...].reshape(32, 8, 128)
    largest = jnp.max(seen, axis=0)
    largest = jnp.maximum(largest[:4], largest[4:])
    both = jnp.concatenate([largest, largest], 0)
    total = jnp.sum(jnp.exp(seen - both[None]), axis=0)
    lines = largest + jnp.log(total[:4] + total[4:])
    item_lse = jnp.concatenate([lines[k : k + 1] for k in range(4)], 1)
    summed = jnp.sum(seen, axis=0)
    summed = summed[:1] + summed[4:5]
    valid, row_pair, item_pair, row_txt, item = tile_masks(place_ref)
    from_img = row_txt == 0
    hit = valid & (
        jnp.where(from_img, row_pos_ref[...], row_pair)
        == jnp.where(from_img, item_pair, item_pos_ref[...])
    )
    real = item[:1] % 4 < 3
    lse_total = jnp.sum(jnp.where(real, item_lse, 0.0), axis=1, keepdims=True)
    lane = lax.broadcasted_iota(jnp.int32, (1, 128), 1)
    matched = jnp.sum(jnp.where(lane == 3, summed, 0.0), axis=1, keepdims=True)
    value = lse_total - 2.0 * matched
    masked = jnp.where(valid, scores, LOW)
    coef = (0.5 * logit) * (jnp.exp(masked - item_lse) - jnp.where(hit, 2.0, 0.0))
    coef = jnp.where(valid, coef, 0.0).astype(BF)
    along = jnp.sum(coef.astype(F32) * scores, axis=1, keepdims=True) / logit
    by_item = times_items(coef, fa_ref, fb_ref)
    by_row = by_row_ref[...]
    value = jnp.broadcast_to(value, (48, 1))
    extra = riders_ref[...] + in_columns(in_parts(along, 2) + in_parts(value, 2), 5)
    extra = extra[:, :64]
    blank = jnp.zeros((48, 64), F32)
    width = by_row.shape[1] // 4
    ways = []
    for k in range(4):
        span = slice(width * k, width * k + width)
        ways.append(jnp.concatenate([by_row[:, span], extra, by_item[:, span], blank], 1))
    ways = [way[:24] for way in ways] + [way[24:] for way in ways]
    out_ref[...] = jnp.concatenate(ways, 0).astype(BF)


def back_kernel(got_ref, unit_ref, w_ref, out_ref, loss_ref):
    width = unit_ref.shape[1]
    every = got_ref[...].astype(F32)
    got = [every[24 * k : 24 * k + 24] for k in range(8)]
    riders = [[part[:, width + k : width + k + 1] for k in range(9)] for part in got]
    parts = [r[0] + r[1] + r[2] for r in riders]
    largest = functools.reduce(jnp.maximum, parts)
    total = sum(jnp.exp(part - largest) for part in parts)
    lse = largest + jnp.log(total)
    along = jnp.zeros((24, 1), F32)
    value = jnp.zeros((24, 1), F32)
    summed = jnp.zeros((24, width), F32)
    for part, r, own in zip(got, riders, parts):
        weight = jnp.exp(own - lse)
        along += weight * (r[3] + r[4]) + (r[5] + r[6])
        value += r[7] + r[8]
        summed += weight * part[:, :width] + part[:, width + 64 : 2 * width + 64]
    loss_ref[...] = jnp.broadcast_to(value[:8] / (2.0 * 1536), (8, 128))
    proj_cot = (summed - unit_ref[...].astype(F32) * along).astype(BF)
    is_img = slab_row((24, 768)) < 13
    mixed = []
    for k in range(4):
        pool = [
            lax.dot_general(
                proj_cot,
                w_ref[256 * k : 256 * k + 256, width * j : width * j + width],
                ROWS_DOT,
                preferred_element_type=F32,
            )
            for j in range(3)
        ]
        pool = jnp.concatenate(pool, 1)
        mixed.append(jnp.where(is_img, pool, pltpu.roll(pool, 21, 0)))
    blank = jnp.zeros((1, 768), F32)
    pieces = []
    for t in range(4):
        for pool in mixed:
            pieces += [pool[6 * t : 6 * t + 3], blank]
    out_ref[...] = jnp.concatenate(pieces, 0).astype(BF)


def token_kernel(pool_ref, inv_ref, img_ref, txt_ref, ig_ref, tg_ref, img_out, txt_out):
    pool = pool_ref[...]
    inv = inv_ref[...][:, :1]
    for x_ref, gain_ref, out_ref, wide, skip, at in (
        (img_ref, ig_ref, img_out, 13, 0, 0),
        (txt_ref, tg_ref, txt_out, 10, 13, 4),
    ):
        dense = lax.broadcasted_iota(jnp.int32, (1, 32 * wide), 1)
        lane = lax.broadcasted_iota(jnp.int32, (768, 32 * wide), 0)
        pick = jnp.where(lane == slab_place(dense, wide, skip), 1.0, 0.0).astype(BF)
        found = jnp.dot(pool, pick, preferred_element_type=F32)
        found = found[:16] + found[16:32] + found[32:48] + found[48:]
        cot = jnp.concatenate([found[4 * k : 4 * k + 4] for k in range(4)], 1)
        cot = cot * inv[at : at + 4] * gain_ref[...][None]
        mean_cot = jnp.mean(cot, axis=1, keepdims=True)
        count = x_ref.shape[0] // 3
        for q in range(3):
            span = slice(count * q, count * q + count)
            values = x_ref[span, :].astype(F32)
            center = values - jnp.mean(values, axis=1, keepdims=True)
            inner = lax.rsqrt(jnp.mean(center * center, axis=1, keepdims=True) + 1e-05)
            mine = cot[q : q + 1]
            along = jnp.mean(center * mine, axis=1, keepdims=True)
            out = inner * (mine - mean_cot[q : q + 1]) - center * (inner * inner * inner * along)
            out_ref[span, :] = out.astype(BF)


def per_device(image_in, text_in, proj_img, proj_txt, img_gain, txt_gain, logit_scale, positive):
    t_index = lax.axis_index("t")
    h_index = lax.axis_index("h")
    g_index = (lax.axis_index("z") * 4 + lax.axis_index("x")) * 2 + lax.axis_index("c")
    y_index = h_index * 4 + t_index
    place = jnp.stack([y_index, h_index, t_index, g_index]).astype(jnp.int32)
    emb = proj_img.shape[1]

    width = emb // 4
    w = jnp.concatenate([proj_img, proj_txt, jnp.zeros((1, emb), BF)], 0)
    w = lax.dynamic_slice(w, (0, width * t_index), (24, width))
    w = jnp.concatenate([w[:8], w[8:16], w[16:]], 1)
    w = jnp.broadcast_to(w[None], (32, 8, 3 * width))
    wa, wb = both_cores(exchange(w, ZX))

    pooled = pool_call(image_in, text_in, img_gain, txt_gain, positive)
    pooled = lax.all_gather(pooled, Y, axis=0, axis_index_groups=[[0, 6], [1, 7], [2, 4], [3, 5]])
    row_pos = pooled[:, :12, 519].astype(F32) * 32.0 + pooled[:, :12, 527].astype(F32)
    row_pos = jnp.pad(row_pos.reshape(8, 3), ((0, 0), (0, 3)), constant_values=-1.0)
    row_pos = row_pos.reshape(48, 1).astype(jnp.int32)

    (part,) = kernel_call(
        project_kernel,
        [((192, 2 * width), BF)],
        [place, pooled.reshape(128, 768), wa, wb],
        smem=(0,),
    )
    parts = exchange(part.reshape(8, 24, 2 * width), Y).reshape(192, 2 * width)

    own_digits = lax.dynamic_slice(positive, (3 * t_index,), (3,))
    own_digits = jnp.concatenate([own_digits // 32, own_digits % 32]).astype(F32)
    own_digits = jnp.pad(own_digits, (0, 122))[None]
    rows, far, inv = kernel_call(
        unit_kernel,
        [((48, emb), BF), ((256, 1024), BF), ((8, 128), F32)],
        [place, parts, own_digits],
        scratch=[pltpu.VMEM((64, emb), F32), pltpu.VMEM((64, 128), F32)],
        smem=(0,),
    )
    w_mine, far = lax.optimization_barrier((jnp.concatenate([wa, wb], 0), far))
    w_all = lax.all_gather(w_mine, "h", axis=0, tiled=True)
    fa, fb = both_cores(exchange(far.reshape(32, 8, 1024), ZX))

    scores, far = kernel_call(
        score_kernel,
        [((48, 512), F32), ((256, 128), F32)],
        [place, logit_scale, rows, fa, fb, row_pos],
        smem=(0, 1),
    )
    far = exchange(far.reshape(64, 4, 128), ZXC).reshape(256, 128)

    item_pos = jnp.concatenate([fa.reshape(32, 8, 1024)[:, 3, 768:774], fb.reshape(32, 8, 1024)[:, 3, 768:774]])
    item_pos = item_pos.astype(F32)
    item_pos = item_pos[:, :3] * 32.0 + item_pos[:, 3:]
    item_pos = jnp.pad(item_pos, ((0, 0), (0, 5)), constant_values=-1.0).reshape(1, 512)
    item_pos = item_pos.astype(jnp.int32)
    by_row, riders = kernel_call(
        row_kernel,
        [((48, emb), F32), ((48, 128), F32)],
        [place, logit_scale, scores, fa, fb],
        smem=(0, 1),
    )
    (ways,) = kernel_call(
        coef_kernel,
        [((192, 768), BF)],
        [place, logit_scale, scores, far, row_pos, item_pos, fa, fb, by_row, riders],
        smem=(0, 1),
    )
    got = exchange(ways.reshape(8, 24, 768), Y).reshape(192, 768)
    unit_part = lax.dynamic_slice(rows, (24 * h_index, width * t_index), (24, width))
    pool, loss = kernel_call(
        back_kernel, [((64, 768), BF), ((8, 128), F32)], [got, unit_part, w_all]
    )
    mean_loss = loss[0, :1]
    pool = exchange(pool.reshape(4, 16, 768), "t").reshape(64, 768)
    count_i, width_i = image_in.shape[1:]
    count_t, width_t = text_in.shape[1:]
    img_own = lax.dynamic_slice_in_dim(image_in, 3 * t_index, 3, 0).reshape(-1, width_i)
    txt_own = lax.dynamic_slice_in_dim(text_in, 3 * t_index, 3, 0).reshape(-1, width_t)
    img_grads, txt_grads = kernel_call(
        token_kernel,
        [(img_own.shape, BF), (txt_own.shape, BF)],
        [pool, inv, img_own, txt_own, img_gain, txt_gain],
    )
    img_grads = img_grads.reshape(3, count_i, width_i)
    txt_grads = txt_grads.reshape(3, count_t, width_t)
    return (mean_loss, img_grads[None], txt_grads[None])


def solution(mesh):
    fine = Mesh(mesh.devices.reshape(4, 2, 8, 4, 2), ("t", "h", "z", "x", "c"))
    in_specs = (
        P(DP, None, None),
        P(DP, None, None),
        P(DP, None),
        P(DP, None),
        P(),
        P(),
        P(),
        P(DP),
    )
    out_specs = (P(), P("t", DP, None, None), P("t", DP, None, None))
    return jax.shard_map(
        per_device, mesh=fine, in_specs=in_specs, out_specs=out_specs, check_vma=False
    )
```

```python
import functools

import jax
import jax.numpy as jnp
from jax import lax
from jax.experimental import pallas as pl
from jax.experimental.pallas import tpu as pltpu
from jax.sharding import Mesh, PartitionSpec as P

BF = jnp.bfloat16
F32 = jnp.float32
Y = ("h", "t")
ZX = ("z", "x")
ZXC = ("z", "x", "c")
DP = ("h", "z", "x", "c")
LOW = -1e30
ROWS_DOT = (((1,), (1,)), ((), ()))


def exchange(blocks, axes):
    return lax.all_to_all(blocks, axes, 0, 0, tiled=True)


def both_cores(blocks):
    half = blocks.shape[0] // 2
    parts = [lax.all_gather(part, "c", axis=0) for part in (blocks[:half], blocks[half:])]
    return [part.reshape(-1, blocks.shape[2]) for part in parts]


def kernel_call(body, outs, args, scratch=(), smem=()):
    vmem = pl.BlockSpec(memory_space=pltpu.VMEM)
    return pl.pallas_call(
        body,
        out_shape=[jax.ShapeDtypeStruct(shape, kind) for shape, kind in outs],
        in_specs=[
            pl.BlockSpec(memory_space=pltpu.SMEM) if k in smem else vmem for k in range(len(args))
        ],
        out_specs=[vmem] * len(outs),
        scratch_shapes=list(scratch),
        compiler_params=pltpu.CompilerParams(vmem_limit_bytes=40 * 1024 * 1024),
    )(*args)


def slab_place(dense, wide, skip):
    row = skip + dense % wide
    return (row // 8) * 256 + ((dense // wide) % 2) * 128 + (dense // (2 * wide)) * 8 + row % 8


def slab_row(shape):
    lane = lax.broadcasted_iota(jnp.int32, shape, 1)
    return (lane // 256) * 8 + lane % 8


def pool_kernel(
    pos_ref,
    img_ref,
    txt_ref,
    ig_ref,
    tg_ref,
    w_ref,
    out_ref,
    img_held,
    txt_held,
    img_rows,
    txt_rows,
    digits,
    sems,
):
    pairs = img_ref.shape[0]

    def copies(k):
        return (
            pltpu.make_async_copy(img_ref.at[k], img_held.at[k], sems.at[0, k]),
            pltpu.make_async_copy(txt_ref.at[k], txt_held.at[k], sems.at[1, k]),
        )

    for k in range(pairs):
        for copy in copies(k):
            copy.start()
    for rows in (img_rows, txt_rows, digits):
        rows[...] = jnp.zeros_like(rows)
    spot = lax.broadcasted_iota(jnp.int32, (1, 128), 1)

    def one_pair(k, carry):
        for copy in copies(k):
            copy.wait()
        for held, gain_ref, rows in ((img_held, ig_ref, img_rows), (txt_held, tg_ref, txt_rows)):
            values = held[k].astype(F32)
            center = values - jnp.mean(values, axis=1, keepdims=True)
            spread = jnp.mean(center * center, axis=1, keepdims=True)
            mean = jnp.mean(center * lax.rsqrt(spread + 1e-05), axis=0, keepdims=True)
            rows[pl.ds(k, 1), :] = mean * gain_ref[...][None]
        place = pos_ref[k]
        line = jnp.where(spot == 7, place // 32, jnp.where(spot == 15, place % 32, 0))
        digits[pl.ds(k, 1), :] = line.astype(F32)
        return carry

    lax.fori_loop(0, pairs, one_pair, 0)
    found = jnp.zeros((64, 768), F32)
    for rows, wide, skip in ((img_rows, 13, 0), (txt_rows, 10, 13)):
        width = 32 * wide
        dense = lax.broadcasted_iota(jnp.int32, (width, 768), 0)
        lane = lax.broadcasted_iota(jnp.int32, (width, 768), 1)
        pick = jnp.where(lane == slab_place(dense, wide, skip), 1.0, 0.0).astype(BF)
        held = rows[...]
        quarters = [held[:, width * k : width * k + width] for k in range(4)]
        quarters = jnp.concatenate(quarters, 0).astype(BF)
        found += jnp.dot(quarters, pick, preferred_element_type=F32)
    line = digits[...]
    blank = jnp.zeros_like(line)
    line = jnp.concatenate([line, blank, line, blank], 0)
    found = jnp.concatenate([found[:, :512], found[:, 512:640] + line, found[:, 640:]], 1)
    out_ref[:64, :] = found.astype(BF)
    out_ref[64:, :] = w_ref[...]


def pool_call(image_in, text_in, img_gain, txt_gain, positive, w_theirs):
    pairs, count_i, width_i = image_in.shape
    _, count_t, width_t = text_in.shape
    vmem = pl.BlockSpec(memory_space=pltpu.VMEM)
    return pl.pallas_call(
        pool_kernel,
        out_shape=jax.ShapeDtypeStruct((80, 768), BF),
        in_specs=[
            pl.BlockSpec(memory_space=pltpu.SMEM),
            pl.BlockSpec(memory_space=pl.ANY),
            pl.BlockSpec(memory_space=pl.ANY),
            vmem,
            vmem,
            vmem,
        ],
        out_specs=vmem,
        scratch_shapes=[
            pltpu.VMEM(image_in.shape, BF),
            pltpu.VMEM(text_in.shape, BF),
            pltpu.VMEM((16, width_i), F32),
            pltpu.VMEM((16, width_t), F32),
            pltpu.VMEM((16, 128), F32),
            pltpu.SemaphoreType.DMA((2, pairs)),
        ],
        cost_estimate=pl.CostEstimate(
            flops=10 * (image_in.size + text_in.size),
            bytes_accessed=2 * (image_in.size + text_in.size),
            transcendentals=0,
        ),
        compiler_params=pltpu.CompilerParams(vmem_limit_bytes=60 * 1024 * 1024),
    )(positive, image_in, text_in, img_gain, txt_gain, w_theirs)


def project_kernel(place_ref, pooled_ref, wa_ref, wb_ref, out_ref):
    width = wa_ref.shape[1] // 3
    part = jnp.zeros((48, width), F32)
    inside = slab_row((12, 768))
    for a, w_ref in enumerate((wa_ref, wb_ref)):
        pieces = []
        for h in range(2):
            start = pl.multiple_of(80 * h + 32 * place_ref[1] + 16 * a, 16)
            rows = pooled_ref[pl.ds(start, 16), :].astype(F32)[:12]
            img_rows = jnp.where(inside < 13, rows, 0.0)
            txt_rows = jnp.where((inside >= 13) & (inside < 23), rows, 0.0)
            for t in range(4):
                pieces += [img_rows[3 * t : 3 * t + 3], txt_rows[3 * t : 3 * t + 3]]
        left = jnp.concatenate(pieces, 0).astype(BF)
        for j in range(3):
            part += jnp.dot(
                left[:, 256 * j : 256 * j + 256],
                w_ref[:, width * j : width * j + width],
                preferred_element_type=F32,
            )
    packed = jnp.concatenate([part[:24], part[24:]], 1)
    out_ref[...] = jnp.concatenate([packed] * 8, 0).astype(BF)


def in_blocks(values):
    blank = jnp.zeros((1, values.shape[1]), F32)
    pieces = []
    for k in range(8):
        pieces += [values[6 * k : 6 * k + 3], blank, values[6 * k + 3 : 6 * k + 6], blank]
    return jnp.concatenate(pieces, 0)


def unit_kernel(place_ref, parts_ref, digits_ref, rows_ref, far_ref, inv_ref, held, held_inv):
    spread = parts_ref[...].astype(F32)
    width = spread.shape[1] // 2
    blocks = [spread[24 * k : 24 * k + 24] + spread[96 + 24 * k : 120 + 24 * k] for k in range(4)]
    blocks = [jnp.concatenate([part[:, :width], part[:, width:]], 0) for part in blocks]
    projected = jnp.concatenate(blocks, 1)
    inv = lax.rsqrt(jnp.sum(projected * projected, axis=1, keepdims=True) + 1e-06)
    unit = projected * inv
    rows_ref[...] = unit.astype(BF)
    held[...] = in_blocks(unit)
    held_inv[...] = in_blocks(jnp.broadcast_to(inv, (48, 128)))
    own = pl.ds(pl.multiple_of(8 * place_ref[0], 8), 8)
    inv_ref[...] = held_inv[own, :]
    block = held[own, :]
    free = jnp.concatenate([digits_ref[...], jnp.zeros((1, 128), F32)], 1)
    pieces = []
    for k in (0, 4):
        ends = [block[k + q : k + q + 1, 1024:] for q in range(3)]
        pieces += [block[k : k + 3, :1024], jnp.concatenate(ends + [free], 1)]
    block = jnp.concatenate(pieces, 0)
    block = jnp.concatenate([block, block], 0).astype(BF)
    for k in range(16):
        far_ref[16 * k : 16 * k + 16, :] = block


def tile_masks(place_ref):
    h, t, g = place_ref[1], place_ref[2], place_ref[3]
    row = lax.broadcasted_iota(jnp.int32, (48, 512), 0)
    item = lax.broadcasted_iota(jnp.int32, (48, 512), 1)
    item_g = ((item // 256) * 16 + (item % 128) // 8) * 2 + (item // 128) % 2
    item_pair = (h * 64 + item_g) * 12 + 3 * t + item % 4
    row_pair = ((row // 24) * 64 + g) * 12 + ((row // 6) % 4) * 3 + row % 3
    row_txt, item_txt = (row % 6) // 3, (item % 8) // 4
    valid = (row_txt != item_txt) & (item % 4 < 3)
    return valid, row_pair, item_pair, row_txt, item


def log_total(values, axis):
    largest = jnp.max(values, axis=axis, keepdims=True)
    return largest + jnp.log(jnp.sum(jnp.exp(values - largest), axis=axis, keepdims=True))


def score_kernel(place_ref, logit_ref, rows_ref, fa_ref, fb_ref, row_pos_ref, scores_ref, far_ref):
    rows = rows_ref[...]
    ends = rows[:, 1024:]
    blank = jnp.zeros_like(ends)
    ends = [[ends if k == q else blank for k in range(3)] for q in range(3)]
    ends = jnp.concatenate([jnp.concatenate(line, 1) for line in ends], 0)

    def dots(left, width):
        return jnp.concatenate(
            [
                lax.dot_general(left, ref[:, :width], ROWS_DOT, preferred_element_type=F32)
                for ref in (fa_ref, fb_ref)
            ],
            1,
        )

    scores = dots(rows[:, :1024], 1024)
    ends = dots(ends, 768)
    lane = lax.broadcasted_iota(jnp.int32, (48, 512), 1) % 4
    for q in range(3):
        moved = pltpu.roll(ends[48 * q : 48 * q + 48], 512 - (3 - q), 1)
        scores += jnp.where(lane == q, moved, 0.0)
    scores = logit_ref[0] * scores
    scores_ref[...] = scores
    valid, _, item_pair, row_txt, _ = tile_masks(place_ref)
    masked = jnp.where(valid, scores, LOW)
    item_part = log_total(masked, 0)
    hit = valid & (row_txt == 0) & (row_pos_ref[...] == item_pair)
    matched = jnp.sum(
        jnp.sum(jnp.where(hit, scores, 0.0), axis=1, keepdims=True), axis=0, keepdims=True
    )
    lane = lax.broadcasted_iota(jnp.int32, (1, 512), 1)
    item_part = jnp.where(lane == 3, matched, item_part)
    lines = jnp.concatenate([item_part[:, 128 * k : 128 * k + 128] for k in range(4)] * 2, 0)
    for k in range(32):
        far_ref[8 * k : 8 * k + 8, :] = lines


def in_parts(values, count):
    parts = []
    for _ in range(count):
        part = values.astype(BF).astype(F32)
        parts.append(part)
        values = values - part
    return parts


def times_items(left, fa_ref, fb_ref):
    def times(part, columns):
        return jnp.dot(part[:, :256], fa_ref[:, columns], preferred_element_type=F32) + jnp.dot(
            part[:, 256:], fb_ref[:, columns], preferred_element_type=F32
        )

    start = times(left, slice(0, 1024))
    last = lax.broadcasted_iota(jnp.int32, left.shape, 1) % 4 == 3
    wide = left.astype(F32)
    ends = jnp.zeros((left.shape[0], 256), F32)
    for q in range(3):
        moved = jnp.where(last, pltpu.roll(wide, 3 - q, 1), 0.0).astype(BF)
        ends += times(moved, slice(256 * q, 256 * q + 256))
    return jnp.concatenate([start, ends], 1)


def in_columns(parts, first):
    column = lax.broadcasted_iota(jnp.int32, (48, 128), 1)
    out = jnp.zeros((48, 128), F32)
    for k, part in enumerate(parts):
        out = jnp.where(column == first + k, part, out)
    return out


def row_kernel(place_ref, logit_ref, scores_ref, fa_ref, fb_ref, cot_ref, riders_ref):
    logit = logit_ref[0]
    scores = scores_ref[...]
    valid = tile_masks(place_ref)[0]
    masked = jnp.where(valid, scores, LOW)
    row_part = log_total(masked, 1)
    coef = jnp.where(valid, (0.5 * logit) * jnp.exp(masked - row_part), 0.0).astype(BF)
    along = jnp.sum(coef.astype(F32) * scores, axis=1, keepdims=True) / logit
    cot_ref[...] = times_items(coef, fa_ref, fb_ref)
    riders_ref[...] = in_columns(in_parts(row_part, 3) + in_parts(along, 2), 0)


def coef_kernel(
    place_ref,
    logit_ref,
    scores_ref,
    far_ref,
    row_pos_ref,
    item_pos_ref,
    fa_ref,
    fb_ref,
    by_row_ref,
    riders_ref,
    out_ref,
):
    logit = logit_ref[0]
    scores = scores_ref[...]
    seen = far_ref[...].reshape(32, 8, 128)
    largest = jnp.max(seen, axis=0)
    largest = jnp.maximum(largest[:4], largest[4:])
    both = jnp.concatenate([largest, largest], 0)
    total = jnp.sum(jnp.exp(seen - both[None]), axis=0)
    lines = largest + jnp.log(total[:4] + total[4:])
    item_lse = jnp.concatenate([lines[k : k + 1] for k in range(4)], 1)
    summed = jnp.sum(seen, axis=0)
    summed = summed[:1] + summed[4:5]
    valid, row_pair, item_pair, row_txt, item = tile_masks(place_ref)
    from_img = row_txt == 0
    hit = valid & (
        jnp.where(from_img, row_pos_ref[...], row_pair)
        == jnp.where(from_img, item_pair, item_pos_ref[...])
    )
    real = item[:1] % 4 < 3
    lse_total = jnp.sum(jnp.where(real, item_lse, 0.0), axis=1, keepdims=True)
    lane = lax.broadcasted_iota(jnp.int32, (1, 128), 1)
    matched = jnp.sum(jnp.where(lane == 3, summed, 0.0), axis=1, keepdims=True)
    value = lse_total - 2.0 * matched
    masked = jnp.where(valid, scores, LOW)
    coef = (0.5 * logit) * (jnp.exp(masked - item_lse) - jnp.where(hit, 2.0, 0.0))
    coef = jnp.where(valid, coef, 0.0).astype(BF)
    along = jnp.sum(coef.astype(F32) * scores, axis=1, keepdims=True) / logit
    by_item = times_items(coef, fa_ref, fb_ref)
    by_row = by_row_ref[...]
    value = jnp.broadcast_to(value, (48, 1))
    extra = riders_ref[...] + in_columns(in_parts(along, 2) + in_parts(value, 2), 5)
    extra = extra[:, :64]
    blank = jnp.zeros((48, 64), F32)
    width = by_row.shape[1] // 4
    ways = []
    for k in range(4):
        span = slice(width * k, width * k + width)
        ways.append(jnp.concatenate([by_row[:, span], extra, by_item[:, span], blank], 1))
    ways = [way[:24] for way in ways] + [way[24:] for way in ways]
    out_ref[...] = jnp.concatenate(ways, 0).astype(BF)


def back_kernel(place_ref, got_ref, unit_ref, wa_ref, wb_ref, wo_ref, out_ref, loss_ref):
    width = unit_ref.shape[1]
    every = got_ref[...].astype(F32)
    got = [every[24 * k : 24 * k + 24] for k in range(8)]
    riders = [[part[:, width + k : width + k + 1] for k in range(9)] for part in got]
    parts = [r[0] + r[1] + r[2] for r in riders]
    largest = functools.reduce(jnp.maximum, parts)
    total = sum(jnp.exp(part - largest) for part in parts)
    lse = largest + jnp.log(total)
    along = jnp.zeros((24, 1), F32)
    value = jnp.zeros((24, 1), F32)
    summed = jnp.zeros((24, width), F32)
    for part, r, own in zip(got, riders, parts):
        weight = jnp.exp(own - lse)
        along += weight * (r[3] + r[4]) + (r[5] + r[6])
        value += r[7] + r[8]
        summed += weight * part[:, :width] + part[:, width + 64 : 2 * width + 64]
    loss_ref[...] = jnp.broadcast_to(value[:8] / (2.0 * 1536), (8, 128))
    proj_cot = (summed - unit_ref[...].astype(F32) * along).astype(BF)
    is_img = slab_row((24, 768)) < 13

    def features(w):
        pool = [
            lax.dot_general(
                proj_cot,
                w[:, width * j : width * j + width],
                ROWS_DOT,
                preferred_element_type=F32,
            )
            for j in range(3)
        ]
        pool = jnp.concatenate(pool, 1)
        return jnp.where(is_img, pool, pltpu.roll(pool, 21, 0))

    own = [features(wa_ref[...]), features(wb_ref[...])]
    other = []
    for a in range(2):
        parts = [wo_ref[k + 128 * a : k + 128 * a + 128, :] for k in (0, 256)]
        other.append(features(jnp.concatenate(parts, 0)))
    first = place_ref[1] == 0
    mixed = [jnp.where(first, x, y) for x, y in zip(own + other, other + own)]
    blank = jnp.zeros((1, 768), F32)
    pieces = []
    for t in range(4):
        for pool in mixed:
            pieces += [pool[6 * t : 6 * t + 3], blank]
    out_ref[...] = jnp.concatenate(pieces, 0).astype(BF)


def token_kernel(pool_ref, inv_ref, img_ref, txt_ref, ig_ref, tg_ref, img_out, txt_out):
    pool = pool_ref[...]
    inv = inv_ref[...][:, :1]
    for x_ref, gain_ref, out_ref, wide, skip, at in (
        (img_ref, ig_ref, img_out, 13, 0, 0),
        (txt_ref, tg_ref, txt_out, 10, 13, 4),
    ):
        dense = lax.broadcasted_iota(jnp.int32, (1, 32 * wide), 1)
        lane = lax.broadcasted_iota(jnp.int32, (768, 32 * wide), 0)
        pick = jnp.where(lane == slab_place(dense, wide, skip), 1.0, 0.0).astype(BF)
        found = jnp.dot(pool, pick, preferred_element_type=F32)
        found = found[:16] + found[16:32] + found[32:48] + found[48:]
        cot = jnp.concatenate([found[4 * k : 4 * k + 4] for k in range(4)], 1)
        cot = cot * inv[at : at + 4] * gain_ref[...][None]
        mean_cot = jnp.mean(cot, axis=1, keepdims=True)
        count = x_ref.shape[0] // 3
        for q in range(3):
            span = slice(count * q, count * q + count)
            values = x_ref[span, :].astype(F32)
            center = values - jnp.mean(values, axis=1, keepdims=True)
            inner = lax.rsqrt(jnp.mean(center * center, axis=1, keepdims=True) + 1e-05)
            mine = cot[q : q + 1]
            along = jnp.mean(center * mine, axis=1, keepdims=True)
            out = inner * (mine - mean_cot[q : q + 1]) - center * (inner * inner * inner * along)
            out_ref[span, :] = out.astype(BF)


def per_device(image_in, text_in, proj_img, proj_txt, img_gain, txt_gain, logit_scale, positive):
    t_index = lax.axis_index("t")
    h_index = lax.axis_index("h")
    g_index = (lax.axis_index("z") * 4 + lax.axis_index("x")) * 2 + lax.axis_index("c")
    y_index = h_index * 4 + t_index
    place = jnp.stack([y_index, h_index, t_index, g_index]).astype(jnp.int32)
    emb = proj_img.shape[1]

    width = emb // 4
    w = jnp.concatenate([proj_img, proj_txt, jnp.zeros((1, emb), BF)], 0)

    def columns_of(tower):
        part = lax.dynamic_slice(w, (0, width * tower), (24, width))
        return jnp.concatenate([part[:8], part[8:16], part[16:]], 1)

    w_sent = jnp.broadcast_to(columns_of(t_index)[None], (32, 8, 3 * width))
    wa, wb = both_cores(exchange(w_sent, ZX))

    w_theirs = columns_of((t_index + 2) % 4)
    w_theirs = jnp.concatenate(
        [w_theirs[:, :768], jnp.pad(w_theirs[:, 768:], ((0, 0), (0, 1536 - 3 * width)))], 0
    )
    pooled = pool_call(image_in, text_in, img_gain, txt_gain, positive, w_theirs)
    pooled = lax.all_gather(pooled, Y, axis=0, axis_index_groups=[[0, 6], [1, 7], [2, 4], [3, 5]])
    row_pos = pooled[:, :12, 519].astype(F32) * 32.0 + pooled[:, :12, 527].astype(F32)
    row_pos = jnp.pad(row_pos.reshape(8, 3), ((0, 0), (0, 3)), constant_values=-1.0)
    row_pos = row_pos.reshape(48, 1).astype(jnp.int32)

    (part,) = kernel_call(
        project_kernel,
        [((192, 2 * width), BF)],
        [place, pooled.reshape(160, 768), wa, wb],
        smem=(0,),
    )
    parts = exchange(part.reshape(8, 24, 2 * width), Y).reshape(192, 2 * width)

    own_digits = lax.dynamic_slice(positive, (3 * t_index,), (3,))
    own_digits = jnp.concatenate([own_digits // 32, own_digits % 32]).astype(F32)
    own_digits = jnp.pad(own_digits, (0, 122))[None]
    rows, far, inv = kernel_call(
        unit_kernel,
        [((48, emb), BF), ((256, 1024), BF), ((8, 128), F32)],
        [place, parts, own_digits],
        scratch=[pltpu.VMEM((64, emb), F32), pltpu.VMEM((64, 128), F32)],
        smem=(0,),
    )
    w_other = lax.dynamic_slice(pooled, (1 - h_index, 64, 0), (1, 16, 768))[0]
    w_other = jnp.concatenate([w_other[:8], w_other[8:, : 3 * width - 768]], 1)
    w_other = lax.all_gather(w_other, ("c", "z", "x"), axis=0, tiled=True)
    fa, fb = both_cores(exchange(far.reshape(32, 8, 1024), ZX))

    scores, far = kernel_call(
        score_kernel,
        [((48, 512), F32), ((256, 128), F32)],
        [place, logit_scale, rows, fa, fb, row_pos],
        smem=(0, 1),
    )
    far = exchange(far.reshape(64, 4, 128), ZXC).reshape(256, 128)

    item_pos = jnp.concatenate([fa.reshape(32, 8, 1024)[:, 3, 768:774], fb.reshape(32, 8, 1024)[:, 3, 768:774]])
    item_pos = item_pos.astype(F32)
    item_pos = item_pos[:, :3] * 32.0 + item_pos[:, 3:]
    item_pos = jnp.pad(item_pos, ((0, 0), (0, 5)), constant_values=-1.0).reshape(1, 512)
    item_pos = item_pos.astype(jnp.int32)
    by_row, riders = kernel_call(
        row_kernel,
        [((48, emb), F32), ((48, 128), F32)],
        [place, logit_scale, scores, fa, fb],
        smem=(0, 1),
    )
    (ways,) = kernel_call(
        coef_kernel,
        [((192, 768), BF)],
        [place, logit_scale, scores, far, row_pos, item_pos, fa, fb, by_row, riders],
        smem=(0, 1),
    )
    got = exchange(ways.reshape(8, 24, 768), Y).reshape(192, 768)
    unit_part = lax.dynamic_slice(rows, (24 * h_index, width * t_index), (24, width))
    pool, loss = kernel_call(
        back_kernel, [((64, 768), BF), ((8, 128), F32)], [place, got, unit_part, wa, wb, w_other], smem=(0,)
    )
    mean_loss = loss[0, :1]
    pool = exchange(pool.reshape(4, 16, 768), "t").reshape(64, 768)
    count_i, width_i = image_in.shape[1:]
    count_t, width_t = text_in.shape[1:]
    img_own = lax.dynamic_slice_in_dim(image_in, 3 * t_index, 3, 0).reshape(-1, width_i)
    txt_own = lax.dynamic_slice_in_dim(text_in, 3 * t_index, 3, 0).reshape(-1, width_t)
    img_grads, txt_grads = kernel_call(
        token_kernel,
        [(img_own.shape, BF), (txt_own.shape, BF)],
        [pool, inv, img_own, txt_own, img_gain, txt_gain],
    )
    img_grads = img_grads.reshape(3, count_i, width_i)
    txt_grads = txt_grads.reshape(3, count_t, width_t)
    return (mean_loss, img_grads[None], txt_grads[None])


def solution(mesh):
    fine = Mesh(mesh.devices.reshape(4, 2, 8, 4, 2), ("t", "h", "z", "x", "c"))
    in_specs = (
        P(DP, None, None),
        P(DP, None, None),
        P(DP, None),
        P(DP, None),
        P(),
        P(),
        P(),
        P(DP),
    )
    out_specs = (P(), P("t", DP, None, None), P("t", DP, None, None))
    return jax.shard_map(
        per_device, mesh=fine, in_specs=in_specs, out_specs=out_specs, check_vma=False
    )
```

```python
import functools

import jax
import jax.numpy as jnp
from jax import lax
from jax.experimental import pallas as pl
from jax.experimental.pallas import tpu as pltpu
from jax.sharding import Mesh, PartitionSpec as P

BF = jnp.bfloat16
F32 = jnp.float32
Y = ("h", "t")
ZX = ("z", "x")
ZXC = ("z", "x", "c")
DP = ("h", "z", "x", "c")
LOW = -1e30
ROWS_DOT = (((1,), (1,)), ((), ()))


def exchange(blocks, axes):
    return lax.all_to_all(blocks, axes, 0, 0, tiled=True)


def both_cores(blocks):
    half = blocks.shape[0] // 2
    parts = [lax.all_gather(part, "c", axis=0) for part in (blocks[:half], blocks[half:])]
    return [part.reshape(-1, blocks.shape[2]) for part in parts]


def kernel_call(body, outs, args, scratch=(), smem=()):
    vmem = pl.BlockSpec(memory_space=pltpu.VMEM)
    return pl.pallas_call(
        body,
        out_shape=[jax.ShapeDtypeStruct(shape, kind) for shape, kind in outs],
        in_specs=[
            pl.BlockSpec(memory_space=pltpu.SMEM) if k in smem else vmem for k in range(len(args))
        ],
        out_specs=[vmem] * len(outs),
        scratch_shapes=list(scratch),
        compiler_params=pltpu.CompilerParams(vmem_limit_bytes=40 * 1024 * 1024),
    )(*args)


def slab_place(dense, wide, skip):
    row = skip + dense % wide
    return (row // 8) * 256 + ((dense // wide) % 2) * 128 + (dense // (2 * wide)) * 8 + row % 8


def slab_row(shape):
    lane = lax.broadcasted_iota(jnp.int32, shape, 1)
    return (lane // 256) * 8 + lane % 8


def pool_kernel(
    pos_ref,
    img_ref,
    txt_ref,
    ig_ref,
    tg_ref,
    w_ref,
    out_ref,
    img_held,
    txt_held,
    img_rows,
    txt_rows,
    digits,
    sems,
):
    pairs = img_ref.shape[0]

    def copies(k):
        return (
            pltpu.make_async_copy(img_ref.at[k], img_held.at[k], sems.at[0, k]),
            pltpu.make_async_copy(txt_ref.at[k], txt_held.at[k], sems.at[1, k]),
        )

    for k in range(pairs):
        for copy in copies(k):
            copy.start()
    for rows in (img_rows, txt_rows, digits):
        rows[...] = jnp.zeros_like(rows)
    spot = lax.broadcasted_iota(jnp.int32, (1, 128), 1)

    def one_pair(k, carry):
        for copy in copies(k):
            copy.wait()
        for held, gain_ref, rows in ((img_held, ig_ref, img_rows), (txt_held, tg_ref, txt_rows)):
            values = held[k].astype(F32)
            center = values - jnp.mean(values, axis=1, keepdims=True)
            spread = jnp.mean(center * center, axis=1, keepdims=True)
            mean = jnp.mean(center * lax.rsqrt(spread + 1e-05), axis=0, keepdims=True)
            rows[pl.ds(k, 1), :] = mean * gain_ref[...][None]
        place = pos_ref[k]
        line = jnp.where(spot == 7, place // 32, jnp.where(spot == 15, place % 32, 0))
        digits[pl.ds(k, 1), :] = line.astype(F32)
        return carry

    lax.fori_loop(0, pairs, one_pair, 0)
    found = jnp.zeros((64, 768), F32)
    for rows, wide, skip in ((img_rows, 13, 0), (txt_rows, 10, 13)):
        width = 32 * wide
        dense = lax.broadcasted_iota(jnp.int32, (width, 768), 0)
        lane = lax.broadcasted_iota(jnp.int32, (width, 768), 1)
        pick = jnp.where(lane == slab_place(dense, wide, skip), 1.0, 0.0).astype(BF)
        held = rows[...]
        quarters = [held[:, width * k : width * k + width] for k in range(4)]
        quarters = jnp.concatenate(quarters, 0).astype(BF)
        found += jnp.dot(quarters, pick, preferred_element_type=F32)
    line = digits[...]
    blank = jnp.zeros_like(line)
    line = jnp.concatenate([line, blank, line, blank], 0)
    found = jnp.concatenate([found[:, :512], found[:, 512:640] + line, found[:, 640:]], 1)
    out_ref[:64, :] = found.astype(BF)
    out_ref[64:, :] = w_ref[...]


def pool_call(image_in, text_in, img_gain, txt_gain, positive, w_theirs):
    pairs, count_i, width_i = image_in.shape
    _, count_t, width_t = text_in.shape
    vmem = pl.BlockSpec(memory_space=pltpu.VMEM)
    return pl.pallas_call(
        pool_kernel,
        out_shape=jax.ShapeDtypeStruct((80, 768), BF),
        in_specs=[
            pl.BlockSpec(memory_space=pltpu.SMEM),
            pl.BlockSpec(memory_space=pl.ANY),
            pl.BlockSpec(memory_space=pl.ANY),
            vmem,
            vmem,
            vmem,
        ],
        out_specs=vmem,
        scratch_shapes=[
            pltpu.VMEM(image_in.shape, BF),
            pltpu.VMEM(text_in.shape, BF),
            pltpu.VMEM((16, width_i), F32),
            pltpu.VMEM((16, width_t), F32),
            pltpu.VMEM((16, 128), F32),
            pltpu.SemaphoreType.DMA((2, pairs)),
        ],
        cost_estimate=pl.CostEstimate(
            flops=10 * (image_in.size + text_in.size),
            bytes_accessed=2 * (image_in.size + text_in.size),
            transcendentals=0,
        ),
        compiler_params=pltpu.CompilerParams(vmem_limit_bytes=60 * 1024 * 1024),
    )(positive, image_in, text_in, img_gain, txt_gain, w_theirs)


def project_kernel(place_ref, pooled_ref, wa_ref, wb_ref, out_ref):
    width = wa_ref.shape[1] // 3
    part = jnp.zeros((48, width), F32)
    inside = slab_row((12, 768))
    for a, w_ref in enumerate((wa_ref, wb_ref)):
        pieces = []
        for h in range(2):
            start = pl.multiple_of(80 * h + 32 * place_ref[1] + 16 * a, 16)
            rows = pooled_ref[pl.ds(start, 16), :].astype(F32)[:12]
            img_rows = jnp.where(inside < 13, rows, 0.0)
            txt_rows = jnp.where((inside >= 13) & (inside < 23), rows, 0.0)
            for t in range(4):
                pieces += [img_rows[3 * t : 3 * t + 3], txt_rows[3 * t : 3 * t + 3]]
        left = jnp.concatenate(pieces, 0).astype(BF)
        for j in range(3):
            part += jnp.dot(
                left[:, 256 * j : 256 * j + 256],
                w_ref[:, width * j : width * j + width],
                preferred_element_type=F32,
            )
    packed = jnp.concatenate([part[:24], part[24:]], 1)
    out_ref[...] = jnp.concatenate([packed] * 8, 0).astype(BF)


def in_blocks(values):
    blank = jnp.zeros((1, values.shape[1]), F32)
    pieces = []
    for k in range(8):
        pieces += [values[6 * k : 6 * k + 3], blank, values[6 * k + 3 : 6 * k + 6], blank]
    return jnp.concatenate(pieces, 0)


def unit_kernel(place_ref, parts_ref, digits_ref, rows_ref, far_ref, inv_ref, held, held_inv):
    spread = parts_ref[...].astype(F32)
    width = spread.shape[1] // 2
    blocks = [spread[24 * k : 24 * k + 24] + spread[96 + 24 * k : 120 + 24 * k] for k in range(4)]
    blocks = [jnp.concatenate([part[:, :width], part[:, width:]], 0) for part in blocks]
    projected = jnp.concatenate(blocks, 1)
    inv = lax.rsqrt(jnp.sum(projected * projected, axis=1, keepdims=True) + 1e-06)
    unit = projected * inv
    rows_ref[...] = unit.astype(BF)
    held[...] = in_blocks(unit)
    held_inv[...] = in_blocks(jnp.broadcast_to(inv, (48, 128)))
    own = pl.ds(pl.multiple_of(8 * place_ref[0], 8), 8)
    inv_ref[...] = held_inv[own, :]
    block = held[own, :]
    free = jnp.concatenate([digits_ref[...], jnp.zeros((1, 128), F32)], 1)
    pieces = []
    for k in (0, 4):
        ends = [block[k + q : k + q + 1, 1024:] for q in range(3)]
        pieces += [block[k : k + 3, :1024], jnp.concatenate(ends + [free], 1)]
    block = jnp.concatenate(pieces, 0)
    block = jnp.concatenate([block, block], 0).astype(BF)
    for k in range(16):
        far_ref[16 * k : 16 * k + 16, :] = block


def tile_masks(place_ref):
    h, t, g = place_ref[1], place_ref[2], place_ref[3]
    row = lax.broadcasted_iota(jnp.int32, (48, 512), 0)
    item = lax.broadcasted_iota(jnp.int32, (48, 512), 1)
    item_g = ((item // 256) * 16 + (item % 128) // 8) * 2 + (item // 128) % 2
    item_pair = (h * 64 + item_g) * 12 + 3 * t + item % 4
    row_pair = ((row // 24) * 64 + g) * 12 + ((row // 6) % 4) * 3 + row % 3
    row_txt, item_txt = (row % 6) // 3, (item % 8) // 4
    valid = (row_txt != item_txt) & (item % 4 < 3)
    return valid, row_pair, item_pair, row_txt, item


def log_total(values, axis):
    largest = jnp.max(values, axis=axis, keepdims=True)
    return largest + jnp.log(jnp.sum(jnp.exp(values - largest), axis=axis, keepdims=True))


def score_kernel(place_ref, logit_ref, rows_ref, fa_ref, fb_ref, row_pos_ref, scores_ref, far_ref):
    rows = rows_ref[...]
    ends = rows[:, 1024:]
    blank = jnp.zeros_like(ends)
    ends = [[ends if k == q else blank for k in range(3)] for q in range(3)]
    ends = jnp.concatenate([jnp.concatenate(line, 1) for line in ends], 0)

    def dots(left, width):
        return jnp.concatenate(
            [
                lax.dot_general(left, ref[:, :width], ROWS_DOT, preferred_element_type=F32)
                for ref in (fa_ref, fb_ref)
            ],
            1,
        )

    scores = dots(rows[:, :1024], 1024)
    ends = dots(ends, 768)
    lane = lax.broadcasted_iota(jnp.int32, (48, 512), 1) % 4
    for q in range(3):
        moved = pltpu.roll(ends[48 * q : 48 * q + 48], 512 - (3 - q), 1)
        scores += jnp.where(lane == q, moved, 0.0)
    scores = logit_ref[0] * scores
    scores_ref[...] = scores
    valid, _, item_pair, row_txt, _ = tile_masks(place_ref)
    masked = jnp.where(valid, scores, LOW)
    item_part = log_total(masked, 0)
    hit = valid & (row_txt == 0) & (row_pos_ref[...] == item_pair)
    matched = jnp.sum(
        jnp.sum(jnp.where(hit, scores, 0.0), axis=1, keepdims=True), axis=0, keepdims=True
    )
    lane = lax.broadcasted_iota(jnp.int32, (1, 512), 1)
    item_part = jnp.where(lane == 3, matched, item_part)
    lines = jnp.concatenate([item_part[:, 128 * k : 128 * k + 128] for k in range(4)] * 2, 0)
    for k in range(32):
        far_ref[8 * k : 8 * k + 8, :] = lines


def in_parts(values, count):
    parts = []
    for _ in range(count):
        part = values.astype(BF).astype(F32)
        parts.append(part)
        values = values - part
    return parts


def times_items(left, fa_ref, fb_ref):
    def times(part, columns):
        return jnp.dot(part[:, :256], fa_ref[:, columns], preferred_element_type=F32) + jnp.dot(
            part[:, 256:], fb_ref[:, columns], preferred_element_type=F32
        )

    start = times(left, slice(0, 1024))
    last = lax.broadcasted_iota(jnp.int32, left.shape, 1) % 4 == 3
    wide = left.astype(F32)
    ends = jnp.zeros((left.shape[0], 256), F32)
    for q in range(3):
        moved = jnp.where(last, pltpu.roll(wide, 3 - q, 1), 0.0).astype(BF)
        ends += times(moved, slice(256 * q, 256 * q + 256))
    return jnp.concatenate([start, ends], 1)


def in_columns(parts, first):
    column = lax.broadcasted_iota(jnp.int32, (48, 128), 1)
    out = jnp.zeros((48, 128), F32)
    for k, part in enumerate(parts):
        out = jnp.where(column == first + k, part, out)
    return out


def row_kernel(place_ref, logit_ref, scores_ref, fa_ref, fb_ref, cot_ref, riders_ref):
    logit = logit_ref[0]
    scores = scores_ref[...]
    valid = tile_masks(place_ref)[0]
    masked = jnp.where(valid, scores, LOW)
    row_part = log_total(masked, 1)
    coef = jnp.where(valid, (0.5 * logit) * jnp.exp(masked - row_part), 0.0).astype(BF)
    along = jnp.sum(coef.astype(F32) * scores, axis=1, keepdims=True) / logit
    cot_ref[...] = times_items(coef, fa_ref, fb_ref)
    riders_ref[...] = in_columns(in_parts(row_part, 3) + in_parts(along, 2), 0)


def coef_kernel(
    place_ref,
    logit_ref,
    scores_ref,
    far_ref,
    row_pos_ref,
    item_pos_ref,
    fa_ref,
    fb_ref,
    by_row_ref,
    riders_ref,
    out_ref,
):
    logit = logit_ref[0]
    scores = scores_ref[...]
    seen = far_ref[...].reshape(32, 8, 128)
    largest = jnp.max(seen, axis=0)
    largest = jnp.maximum(largest[:4], largest[4:])
    both = jnp.concatenate([largest, largest], 0)
    total = jnp.sum(jnp.exp(seen - both[None]), axis=0)
    lines = largest + jnp.log(total[:4] + total[4:])
    item_lse = jnp.concatenate([lines[k : k + 1] for k in range(4)], 1)
    summed = jnp.sum(seen, axis=0)
    summed = summed[:1] + summed[4:5]
    valid, row_pair, item_pair, row_txt, item = tile_masks(place_ref)
    from_img = row_txt == 0
    hit = valid & (
        jnp.where(from_img, row_pos_ref[...], row_pair)
        == jnp.where(from_img, item_pair, item_pos_ref[...])
    )
    real = item[:1] % 4 < 3
    lse_total = jnp.sum(jnp.where(real, item_lse, 0.0), axis=1, keepdims=True)
    lane = lax.broadcasted_iota(jnp.int32, (1, 128), 1)
    matched = jnp.sum(jnp.where(lane == 3, summed, 0.0), axis=1, keepdims=True)
    value = lse_total - 2.0 * matched
    masked = jnp.where(valid, scores, LOW)
    coef = (0.5 * logit) * (jnp.exp(masked - item_lse) - jnp.where(hit, 2.0, 0.0))
    coef = jnp.where(valid, coef, 0.0).astype(BF)
    along = jnp.sum(coef.astype(F32) * scores, axis=1, keepdims=True) / logit
    by_item = times_items(coef, fa_ref, fb_ref)
    by_row = by_row_ref[...]
    value = jnp.broadcast_to(value, (48, 1))
    extra = riders_ref[...] + in_columns(in_parts(along, 2) + in_parts(value, 2), 5)
    extra = extra[:, :64]
    blank = jnp.zeros((48, 64), F32)
    width = by_row.shape[1] // 4
    ways = []
    for k in range(4):
        span = slice(width * k, width * k + width)
        ways.append(jnp.concatenate([by_row[:, span], extra, by_item[:, span], blank], 1))
    ways = [way[:24] for way in ways] + [way[24:] for way in ways]
    out_ref[...] = jnp.concatenate(ways, 0).astype(BF)


def back_kernel(place_ref, got_ref, unit_ref, wa_ref, wb_ref, wo_ref, out_ref, loss_ref):
    width = unit_ref.shape[1]
    every = got_ref[...].astype(F32)
    got = [every[24 * k : 24 * k + 24] for k in range(8)]
    riders = [[part[:, width + k : width + k + 1] for k in range(9)] for part in got]
    parts = [r[0] + r[1] + r[2] for r in riders]
    largest = functools.reduce(jnp.maximum, parts)
    total = sum(jnp.exp(part - largest) for part in parts)
    lse = largest + jnp.log(total)
    along = jnp.zeros((24, 1), F32)
    value = jnp.zeros((24, 1), F32)
    summed = jnp.zeros((24, width), F32)
    for part, r, own in zip(got, riders, parts):
        weight = jnp.exp(own - lse)
        along += weight * (r[3] + r[4]) + (r[5] + r[6])
        value += r[7] + r[8]
        summed += weight * part[:, :width] + part[:, width + 64 : 2 * width + 64]
    loss_ref[...] = jnp.broadcast_to(value[:8] / (2.0 * 1536), (8, 128))
    proj_cot = (summed - unit_ref[...].astype(F32) * along).astype(BF)
    is_img = slab_row((24, 768)) < 13

    def features(w):
        pool = [
            lax.dot_general(
                proj_cot,
                w[:, width * j : width * j + width],
                ROWS_DOT,
                preferred_element_type=F32,
            )
            for j in range(3)
        ]
        pool = jnp.concatenate(pool, 1)
        return jnp.where(is_img, pool, pltpu.roll(pool, 21, 0))

    own = [features(wa_ref[...]), features(wb_ref[...])]
    other = []
    for a in range(2):
        other.append(features(wo_ref[256 * a : 256 * a + 256, :]))
    first = place_ref[1] == 0
    mixed = [jnp.where(first, x, y) for x, y in zip(own + other, other + own)]
    blank = jnp.zeros((1, 768), F32)
    pieces = []
    for t in range(4):
        for pool in mixed:
            pieces += [pool[6 * t : 6 * t + 3], blank]
    out_ref[...] = jnp.concatenate(pieces, 0).astype(BF)


def token_kernel(pool_ref, inv_ref, img_ref, txt_ref, ig_ref, tg_ref, img_out, txt_out):
    pool = pool_ref[...]
    inv = inv_ref[...][:, :1]
    for x_ref, gain_ref, out_ref, wide, skip, at in (
        (img_ref, ig_ref, img_out, 13, 0, 0),
        (txt_ref, tg_ref, txt_out, 10, 13, 4),
    ):
        dense = lax.broadcasted_iota(jnp.int32, (1, 32 * wide), 1)
        lane = lax.broadcasted_iota(jnp.int32, (768, 32 * wide), 0)
        pick = jnp.where(lane == slab_place(dense, wide, skip), 1.0, 0.0).astype(BF)
        found = jnp.dot(pool, pick, preferred_element_type=F32)
        found = found[:16] + found[16:32] + found[32:48] + found[48:]
        cot = jnp.concatenate([found[4 * k : 4 * k + 4] for k in range(4)], 1)
        cot = cot * inv[at : at + 4] * gain_ref[...][None]
        mean_cot = jnp.mean(cot, axis=1, keepdims=True)
        count = x_ref.shape[0] // 3
        for q in range(3):
            span = slice(count * q, count * q + count)
            values = x_ref[span, :].astype(F32)
            center = values - jnp.mean(values, axis=1, keepdims=True)
            inner = lax.rsqrt(jnp.mean(center * center, axis=1, keepdims=True) + 1e-05)
            mine = cot[q : q + 1]
            along = jnp.mean(center * mine, axis=1, keepdims=True)
            out = inner * (mine - mean_cot[q : q + 1]) - center * (inner * inner * inner * along)
            out_ref[span, :] = out.astype(BF)


def per_device(image_in, text_in, proj_img, proj_txt, img_gain, txt_gain, logit_scale, positive):
    t_index = lax.axis_index("t")
    h_index = lax.axis_index("h")
    g_index = (lax.axis_index("z") * 4 + lax.axis_index("x")) * 2 + lax.axis_index("c")
    y_index = h_index * 4 + t_index
    place = jnp.stack([y_index, h_index, t_index, g_index]).astype(jnp.int32)
    emb = proj_img.shape[1]

    width = emb // 4
    w = jnp.concatenate([proj_img, proj_txt, jnp.zeros((1, emb), BF)], 0)

    def columns_of(tower):
        part = lax.dynamic_slice(w, (0, width * tower), (24, width))
        return jnp.concatenate([part[:8], part[8:16], part[16:]], 1)

    w_sent = jnp.broadcast_to(columns_of(t_index)[None], (32, 8, 3 * width))
    wa, wb = both_cores(exchange(w_sent, ZX))

    w_theirs = columns_of((t_index + 2) % 4)
    w_theirs = jnp.concatenate(
        [w_theirs[:, :768], jnp.pad(w_theirs[:, 768:], ((0, 0), (0, 1536 - 3 * width)))], 0
    )
    pooled = pool_call(image_in, text_in, img_gain, txt_gain, positive, w_theirs)
    pooled = lax.all_gather(pooled, Y, axis=0, axis_index_groups=[[0, 6], [1, 7], [2, 4], [3, 5]])
    row_pos = pooled[:, :12, 519].astype(F32) * 32.0 + pooled[:, :12, 527].astype(F32)
    row_pos = jnp.pad(row_pos.reshape(8, 3), ((0, 0), (0, 3)), constant_values=-1.0)
    row_pos = row_pos.reshape(48, 1).astype(jnp.int32)

    (part,) = kernel_call(
        project_kernel,
        [((192, 2 * width), BF)],
        [place, pooled.reshape(160, 768), wa, wb],
        smem=(0,),
    )
    parts = exchange(part.reshape(8, 24, 2 * width), Y).reshape(192, 2 * width)

    own_digits = lax.dynamic_slice(positive, (3 * t_index,), (3,))
    own_digits = jnp.concatenate([own_digits // 32, own_digits % 32]).astype(F32)
    own_digits = jnp.pad(own_digits, (0, 122))[None]
    rows, far, inv = kernel_call(
        unit_kernel,
        [((48, emb), BF), ((256, 1024), BF), ((8, 128), F32)],
        [place, parts, own_digits],
        scratch=[pltpu.VMEM((64, emb), F32), pltpu.VMEM((64, 128), F32)],
        smem=(0,),
    )
    w_other = lax.dynamic_slice(pooled, (1 - h_index, 64, 0), (1, 16, 768))[0]
    w_other = jnp.concatenate([w_other[:8], w_other[8:, :384]], 1)
    w_other = lax.all_gather(w_other, ZXC, axis=0, tiled=True)
    w_other = w_other.reshape(2, 16, 2, 8, 1152).transpose(0, 2, 1, 3, 4).reshape(512, 1152)
    fa, fb = both_cores(exchange(far.reshape(32, 8, 1024), ZX))

    scores, far = kernel_call(
        score_kernel,
        [((48, 512), F32), ((256, 128), F32)],
        [place, logit_scale, rows, fa, fb, row_pos],
        smem=(0, 1),
    )
    far = exchange(far.reshape(64, 4, 128), ZXC).reshape(256, 128)

    item_pos = jnp.concatenate([fa.reshape(32, 8, 1024)[:, 3, 768:774], fb.reshape(32, 8, 1024)[:, 3, 768:774]])
    item_pos = item_pos.astype(F32)
    item_pos = item_pos[:, :3] * 32.0 + item_pos[:, 3:]
    item_pos = jnp.pad(item_pos, ((0, 0), (0, 5)), constant_values=-1.0).reshape(1, 512)
    item_pos = item_pos.astype(jnp.int32)
    by_row, riders = kernel_call(
        row_kernel,
        [((48, emb), F32), ((48, 128), F32)],
        [place, logit_scale, scores, fa, fb],
        smem=(0, 1),
    )
    (ways,) = kernel_call(
        coef_kernel,
        [((192, 768), BF)],
        [place, logit_scale, scores, far, row_pos, item_pos, fa, fb, by_row, riders],
        smem=(0, 1),
    )
    got = exchange(ways.reshape(8, 24, 768), Y).reshape(192, 768)
    unit_part = lax.dynamic_slice(rows, (24 * h_index, width * t_index), (24, width))
    pool, loss = kernel_call(
        back_kernel, [((64, 768), BF), ((8, 128), F32)], [place, got, unit_part, wa, wb, w_other], smem=(0,)
    )
    mean_loss = loss[0, :1]
    pool = exchange(pool.reshape(4, 16, 768), "t").reshape(64, 768)
    count_i, width_i = image_in.shape[1:]
    count_t, width_t = text_in.shape[1:]
    img_own = lax.dynamic_slice_in_dim(image_in, 3 * t_index, 3, 0).reshape(-1, width_i)
    txt_own = lax.dynamic_slice_in_dim(text_in, 3 * t_index, 3, 0).reshape(-1, width_t)
    img_grads, txt_grads = kernel_call(
        token_kernel,
        [(img_own.shape, BF), (txt_own.shape, BF)],
        [pool, inv, img_own, txt_own, img_gain, txt_gain],
    )
    img_grads = img_grads.reshape(3, count_i, width_i)
    txt_grads = txt_grads.reshape(3, count_t, width_t)
    return (mean_loss, img_grads[None], txt_grads[None])


def solution(mesh):
    fine = Mesh(mesh.devices.reshape(4, 2, 8, 4, 2), ("t", "h", "z", "x", "c"))
    in_specs = (
        P(DP, None, None),
        P(DP, None, None),
        P(DP, None),
        P(DP, None),
        P(),
        P(),
        P(),
        P(DP),
    )
    out_specs = (P(), P("t", DP, None, None), P("t", DP, None, None))
    return jax.shard_map(
        per_device, mesh=fine, in_specs=in_specs, out_specs=out_specs, check_vma=False
    )
```

```python
import functools

import jax
import jax.numpy as jnp
from jax import lax
from jax.experimental import pallas as pl
from jax.experimental.pallas import tpu as pltpu
from jax.sharding import Mesh, PartitionSpec as P

BF = jnp.bfloat16
F32 = jnp.float32
Y = ("h", "t")
ZX = ("z", "x")
ZXC = ("z", "x", "c")
DP = ("h", "z", "x", "c")
LOW = -1e30
ROWS_DOT = (((1,), (1,)), ((), ()))


def exchange(blocks, axes):
    return lax.all_to_all(blocks, axes, 0, 0, tiled=True)


def both_cores(blocks):
    half = blocks.shape[0] // 2
    parts = [lax.all_gather(part, "c", axis=0) for part in (blocks[:half], blocks[half:])]
    return [part.reshape(-1, blocks.shape[2]) for part in parts]


def kernel_call(body, outs, args, scratch=(), smem=()):
    vmem = pl.BlockSpec(memory_space=pltpu.VMEM)
    return pl.pallas_call(
        body,
        out_shape=[jax.ShapeDtypeStruct(shape, kind) for shape, kind in outs],
        in_specs=[
            pl.BlockSpec(memory_space=pltpu.SMEM) if k in smem else vmem for k in range(len(args))
        ],
        out_specs=[vmem] * len(outs),
        scratch_shapes=list(scratch),
        compiler_params=pltpu.CompilerParams(vmem_limit_bytes=40 * 1024 * 1024),
    )(*args)


def slab_place(dense, wide, skip):
    row = skip + dense % wide
    return (row // 8) * 256 + ((dense // wide) % 2) * 128 + (dense // (2 * wide)) * 8 + row % 8


def slab_row(shape):
    lane = lax.broadcasted_iota(jnp.int32, shape, 1)
    return (lane // 256) * 8 + lane % 8


def pool_kernel(
    place_ref,
    pos_ref,
    img_ref,
    txt_ref,
    ig_ref,
    tg_ref,
    mine_ref,
    theirs_ref,
    img_held,
    txt_held,
    img_rows,
    txt_rows,
    digits,
    sems,
):
    steps = img_ref.shape[0] // 2

    def copies(k):
        span = pl.ds(2 * k, 2)
        return (
            pltpu.make_async_copy(img_ref.at[span], img_held.at[span], sems.at[0, k]),
            pltpu.make_async_copy(txt_ref.at[span], txt_held.at[span], sems.at[1, k]),
        )

    for k in range(steps):
        for copy in copies(k):
            copy.start()
    for rows in (img_rows, txt_rows, digits):
        rows[...] = jnp.zeros_like(rows)
    spot = lax.broadcasted_iota(jnp.int32, (1, 128), 1)

    def two_pairs(k, carry):
        for copy in copies(k):
            copy.wait()
        for held, gain_ref, rows in ((img_held, ig_ref, img_rows), (txt_held, tg_ref, txt_rows)):
            values = held[pl.ds(2 * k, 2)].astype(F32)
            center = values - jnp.mean(values, axis=2, keepdims=True)
            spread = jnp.mean(center * center, axis=2, keepdims=True)
            mean = jnp.mean(center * lax.rsqrt(spread + 1e-05), axis=1)
            for b in range(2):
                rows[pl.ds(2 * k + b, 1), :] = mean[b : b + 1] * gain_ref[...][None]
        for b in range(2):
            place = pos_ref[2 * k + b]
            line = jnp.where(spot == 7, place // 32, jnp.where(spot == 15, place % 32, 0))
            digits[pl.ds(2 * k + b, 1), :] = line.astype(F32)
        return carry

    lax.fori_loop(0, steps, two_pairs, 0)
    found = jnp.zeros((64, 768), F32)
    lane = lax.broadcasted_iota(jnp.int32, (1, 768), 1)
    slab = (lane % 128) // 8 * 2 + (lane // 128) % 2
    for rows, wide, skip in ((img_rows, 13, 0), (txt_rows, 10, 13)):
        width = 32 * wide
        row = slab_row((1, 768)) - skip
        wanted = jnp.where((row >= 0) & (row < wide), slab * wide + row, -1)
        dense = lax.broadcasted_iota(jnp.int32, (width, 768), 0)
        pick = jnp.where(dense == wanted, 1.0, 0.0).astype(BF)
        held = rows[...]
        quarters = [held[:, width * k : width * k + width] for k in range(4)]
        quarters = jnp.concatenate(quarters, 0).astype(BF)
        found += jnp.dot(quarters, pick, preferred_element_type=F32)
    line = digits[...]
    blank = jnp.zeros_like(line)
    line = jnp.concatenate([line, blank, line, blank], 0)
    found = jnp.concatenate([found[:, :512], found[:, 512:640] + line, found[:, 640:]], 1)
    first = place_ref[1] == 0
    mine_ref[...] = jnp.where(first, found[:32], found[32:]).astype(BF)
    theirs_ref[...] = jnp.where(first, found[32:], found[:32]).astype(BF)


def pool_call(place, image_in, text_in, img_gain, txt_gain, positive):
    pairs, _, width_i = image_in.shape
    width_t = text_in.shape[2]
    vmem = pl.BlockSpec(memory_space=pltpu.VMEM)
    smem = pl.BlockSpec(memory_space=pltpu.SMEM)
    whole = pl.BlockSpec(memory_space=pl.ANY)
    return pl.pallas_call(
        pool_kernel,
        out_shape=[jax.ShapeDtypeStruct((32, 768), BF)] * 2,
        in_specs=[smem, smem, whole, whole, vmem, vmem],
        out_specs=[vmem, vmem],
        scratch_shapes=[
            pltpu.VMEM(image_in.shape, BF),
            pltpu.VMEM(text_in.shape, BF),
            pltpu.VMEM((16, width_i), F32),
            pltpu.VMEM((16, width_t), F32),
            pltpu.VMEM((16, 128), F32),
            pltpu.SemaphoreType.DMA((2, pairs // 2)),
        ],
        cost_estimate=pl.CostEstimate(
            flops=10 * (image_in.size + text_in.size),
            bytes_accessed=2 * (image_in.size + text_in.size),
            transcendentals=0,
        ),
        compiler_params=pltpu.CompilerParams(vmem_limit_bytes=60 * 1024 * 1024),
    )(place, positive, image_in, text_in, img_gain, txt_gain)


def weight_quarter(w_ref, a):
    return jnp.concatenate([w_ref[k + 128 * a : k + 128 * a + 128, :] for k in (0, 256)], 0)


def project_kernel(place_ref, mine_ref, theirs_ref, w_ref, out_ref):
    width = w_ref.shape[1] // 3
    part = jnp.zeros((48, width), F32)
    inside = slab_row((12, 768))
    for a in range(2):
        pieces = []
        for h in range(2):
            rows = jnp.where(
                place_ref[1] == h,
                mine_ref[16 * a : 16 * a + 16, :].astype(F32),
                theirs_ref[32 * h + 16 * a : 32 * h + 16 * a + 16, :].astype(F32),
            )[:12]
            img_rows = jnp.where(inside < 13, rows, 0.0)
            txt_rows = jnp.where((inside >= 13) & (inside < 23), rows, 0.0)
            for t in range(4):
                pieces += [img_rows[3 * t : 3 * t + 3], txt_rows[3 * t : 3 * t + 3]]
        left = jnp.concatenate(pieces, 0).astype(BF)
        quarter = weight_quarter(w_ref, a)
        for j in range(3):
            part += jnp.dot(
                left[:, 256 * j : 256 * j + 256],
                quarter[:, width * j : width * j + width],
                preferred_element_type=F32,
            )
    packed = jnp.concatenate([part[:24], part[24:]], 1)
    out_ref[...] = jnp.concatenate([packed] * 8, 0).astype(BF)


def in_blocks(values):
    blank = jnp.zeros((1, values.shape[1]), F32)
    pieces = []
    for k in range(8):
        pieces += [values[6 * k : 6 * k + 3], blank, values[6 * k + 3 : 6 * k + 6], blank]
    return jnp.concatenate(pieces, 0)


def unit_kernel(place_ref, parts_ref, digits_ref, rows_ref, far_ref, inv_ref, held, held_inv):
    spread = parts_ref[...].astype(F32)
    width = spread.shape[1] // 2
    blocks = [spread[24 * k : 24 * k + 24] + spread[96 + 24 * k : 120 + 24 * k] for k in range(4)]
    blocks = [jnp.concatenate([part[:, :width], part[:, width:]], 0) for part in blocks]
    projected = jnp.concatenate(blocks, 1)
    inv = lax.rsqrt(jnp.sum(projected * projected, axis=1, keepdims=True) + 1e-06)
    unit = projected * inv
    rows_ref[...] = unit.astype(BF)
    held[...] = in_blocks(unit)
    held_inv[...] = in_blocks(jnp.broadcast_to(inv, (48, 128)))
    own = pl.ds(pl.multiple_of(8 * place_ref[0], 8), 8)
    inv_ref[...] = held_inv[own, :]
    block = held[own, :]
    free = jnp.concatenate([digits_ref[...], jnp.zeros((1, 128), F32)], 1)
    pieces = []
    for k in (0, 4):
        ends = [block[k + q : k + q + 1, 1024:] for q in range(3)]
        pieces += [block[k : k + 3, :1024], jnp.concatenate(ends + [free], 1)]
    block = jnp.concatenate(pieces, 0)
    block = jnp.concatenate([block, block], 0).astype(BF)
    for k in range(16):
        far_ref[16 * k : 16 * k + 16, :] = block


def tile_masks(place_ref):
    h, t, g = place_ref[1], place_ref[2], place_ref[3]
    row = lax.broadcasted_iota(jnp.int32, (48, 512), 0)
    item = lax.broadcasted_iota(jnp.int32, (48, 512), 1)
    item_g = ((item // 256) * 16 + (item % 128) // 8) * 2 + (item // 128) % 2
    item_pair = (h * 64 + item_g) * 12 + 3 * t + item % 4
    row_pair = ((row // 24) * 64 + g) * 12 + ((row // 6) % 4) * 3 + row % 3
    row_txt, item_txt = (row % 6) // 3, (item % 8) // 4
    valid = (row_txt != item_txt) & (item % 4 < 3)
    return valid, row_pair, item_pair, row_txt, item


def log_total(values, axis):
    largest = jnp.max(values, axis=axis, keepdims=True)
    return largest + jnp.log(jnp.sum(jnp.exp(values - largest), axis=axis, keepdims=True))


def score_kernel(place_ref, logit_ref, rows_ref, fa_ref, fb_ref, row_pos_ref, scores_ref, far_ref):
    rows = rows_ref[...]
    ends = rows[:, 1024:]
    blank = jnp.zeros_like(ends)
    ends = [[ends if k == q else blank for k in range(3)] for q in range(3)]
    ends = jnp.concatenate([jnp.concatenate(line, 1) for line in ends], 0)

    def dots(left, width):
        return jnp.concatenate(
            [
                lax.dot_general(left, ref[:, :width], ROWS_DOT, preferred_element_type=F32)
                for ref in (fa_ref, fb_ref)
            ],
            1,
        )

    scores = dots(rows[:, :1024], 1024)
    ends = dots(ends, 768)
    lane = lax.broadcasted_iota(jnp.int32, (48, 512), 1) % 4
    for q in range(3):
        moved = pltpu.roll(ends[48 * q : 48 * q + 48], 512 - (3 - q), 1)
        scores += jnp.where(lane == q, moved, 0.0)
    scores = logit_ref[0] * scores
    scores_ref[...] = scores
    valid, _, item_pair, row_txt, _ = tile_masks(place_ref)
    masked = jnp.where(valid, scores, LOW)
    item_part = log_total(masked, 0)
    hit = valid & (row_txt == 0) & (row_pos_ref[...] == item_pair)
    matched = jnp.sum(
        jnp.sum(jnp.where(hit, scores, 0.0), axis=1, keepdims=True), axis=0, keepdims=True
    )
    lane = lax.broadcasted_iota(jnp.int32, (1, 512), 1)
    item_part = jnp.where(lane == 3, matched, item_part)
    lines = jnp.concatenate([item_part[:, 128 * k : 128 * k + 128] for k in range(4)] * 2, 0)
    for k in range(32):
        far_ref[8 * k : 8 * k + 8, :] = lines


def in_parts(values, count):
    parts = []
    for _ in range(count):
        part = values.astype(BF).astype(F32)
        parts.append(part)
        values = values - part
    return parts


def times_items(left, fa_ref, fb_ref):
    def times(part, columns):
        return jnp.dot(part[:, :256], fa_ref[:, columns], preferred_element_type=F32) + jnp.dot(
            part[:, 256:], fb_ref[:, columns], preferred_element_type=F32
        )

    start = times(left, slice(0, 1024))
    last = lax.broadcasted_iota(jnp.int32, left.shape, 1) % 4 == 3
    wide = left.astype(F32)
    ends = jnp.zeros((left.shape[0], 256), F32)
    for q in range(3):
        moved = jnp.where(last, pltpu.roll(wide, 3 - q, 1), 0.0).astype(BF)
        ends += times(moved, slice(256 * q, 256 * q + 256))
    return jnp.concatenate([start, ends], 1)


def coef_kernel(
    place_ref, logit_ref, scores_ref, far_ref, row_pos_ref, item_pos_ref, fa_ref, fb_ref, out_ref
):
    logit = logit_ref[0]
    scores = scores_ref[...]
    seen = far_ref[...].reshape(32, 8, 128)
    largest = jnp.max(seen, axis=0)
    largest = jnp.maximum(largest[:4], largest[4:])
    both = jnp.concatenate([largest, largest], 0)
    total = jnp.sum(jnp.exp(seen - both[None]), axis=0)
    lines = largest + jnp.log(total[:4] + total[4:])
    item_lse = jnp.concatenate([lines[k : k + 1] for k in range(4)], 1)
    summed = jnp.sum(seen, axis=0)
    summed = summed[:1] + summed[4:5]
    valid, row_pair, item_pair, row_txt, item = tile_masks(place_ref)
    from_img = row_txt == 0
    hit = valid & (
        jnp.where(from_img, row_pos_ref[...], row_pair)
        == jnp.where(from_img, item_pair, item_pos_ref[...])
    )
    real = item[:1] % 4 < 3
    lse_total = jnp.sum(jnp.where(real, item_lse, 0.0), axis=1, keepdims=True)
    lane = lax.broadcasted_iota(jnp.int32, (1, 128), 1)
    matched = jnp.sum(jnp.where(lane == 3, summed, 0.0), axis=1, keepdims=True)
    value = lse_total - 2.0 * matched
    masked = jnp.where(valid, scores, LOW)
    row_part = log_total(masked, 1)
    by_row = (0.5 * logit) * jnp.exp(masked - row_part)
    by_item = (0.5 * logit) * (jnp.exp(masked - item_lse) - jnp.where(hit, 2.0, 0.0))
    coefs = [jnp.where(valid, part, 0.0).astype(BF) for part in (by_row, by_item)]
    along = [
        jnp.sum(part.astype(F32) * scores, axis=1, keepdims=True) / logit for part in coefs
    ]
    cot = times_items(jnp.concatenate(coefs, 0), fa_ref, fb_ref)
    riders = (
        in_parts(row_part, 3)
        + in_parts(along[0], 2)
        + in_parts(along[1], 2)
        + in_parts(jnp.broadcast_to(value, (48, 1)), 2)
    )
    column = lax.broadcasted_iota(jnp.int32, (48, 64), 1)
    extra = jnp.zeros((48, 64), F32)
    for k, rider in enumerate(riders):
        extra = jnp.where(column == k, rider, extra)
    blank = jnp.zeros((48, 64), F32)
    width = cot.shape[1] // 4
    for k in range(4):
        part = cot[:, width * k : width * k + width]
        way = jnp.concatenate([part[:48], extra, part[48:], blank], 1).astype(BF)
        out_ref[48 * k : 48 * k + 48, :] = way
        out_ref[192 + 48 * k : 240 + 48 * k, :] = way


def back_kernel(got_ref, unit_ref, w_ref, out_ref, loss_ref):
    width = unit_ref.shape[1]
    got = [got_ref[48 * k : 48 * k + 48, :].astype(F32) for k in range(8)]
    riders = [[part[:, width + k : width + k + 1] for k in range(9)] for part in got]
    parts = [r[0] + r[1] + r[2] for r in riders]
    largest = functools.reduce(jnp.maximum, parts)
    total = sum(jnp.exp(part - largest) for part in parts)
    lse = largest + jnp.log(total)
    along = jnp.zeros((48, 1), F32)
    value = jnp.zeros((48, 1), F32)
    summed = jnp.zeros((48, width), F32)
    for part, r, own in zip(got, riders, parts):
        weight = jnp.exp(own - lse)
        along += weight * (r[3] + r[4]) + (r[5] + r[6])
        value += r[7] + r[8]
        summed += weight * part[:, :width] + part[:, width + 64 : 2 * width + 64]
    loss_ref[...] = jnp.broadcast_to(value[:8] / (2.0 * 1536), (8, 128))
    proj_cot = (summed - unit_ref[...].astype(F32) * along).astype(BF)
    is_img = slab_row((48, 768)) < 13
    mixed = []
    for a in range(2):
        quarter = weight_quarter(w_ref, a)
        pool = [
            lax.dot_general(
                proj_cot,
                quarter[:, width * j : width * j + width],
                ROWS_DOT,
                preferred_element_type=F32,
            )
            for j in range(3)
        ]
        pool = jnp.concatenate(pool, 1)
        mixed.append(jnp.where(is_img, pool, pltpu.roll(pool, 45, 0)))
    blank = jnp.zeros((1, pool.shape[1]), F32)
    pieces = []
    for k in range(8):
        for pool in mixed:
            pieces += [pool[6 * k : 6 * k + 3], blank]
    out_ref[...] = jnp.concatenate(pieces, 0).astype(BF)


def token_kernel(pool_ref, inv_ref, img_ref, txt_ref, ig_ref, tg_ref, img_out, txt_out):
    pool = pool_ref[...]
    inv = inv_ref[...][:, :1]
    for x_ref, gain_ref, out_ref, wide, skip, at in (
        (img_ref, ig_ref, img_out, 13, 0, 0),
        (txt_ref, tg_ref, txt_out, 10, 13, 4),
    ):
        dense = lax.broadcasted_iota(jnp.int32, (1, 32 * wide), 1)
        lane = lax.broadcasted_iota(jnp.int32, (768, 32 * wide), 0)
        pick = jnp.where(lane == slab_place(dense, wide, skip), 1.0, 0.0).astype(BF)
        found = jnp.dot(pool, pick, preferred_element_type=F32)
        halves = [
            found[32 * k : 32 * k + 8]
            + found[32 * k + 8 : 32 * k + 16]
            + found[32 * k + 16 : 32 * k + 24]
            + found[32 * k + 24 : 32 * k + 32]
            for k in range(2)
        ]
        cot = jnp.concatenate([halves[0][:4], halves[0][4:], halves[1][:4], halves[1][4:]], 1)
        cot = cot * inv[at : at + 4] * gain_ref[...][None]
        mean_cot = jnp.mean(cot, axis=1, keepdims=True)
        count = x_ref.shape[0] // 3
        for q in range(3):
            span = slice(count * q, count * q + count)
            values = x_ref[span, :].astype(F32)
            center = values - jnp.mean(values, axis=1, keepdims=True)
            inner = lax.rsqrt(jnp.mean(center * center, axis=1, keepdims=True) + 1e-05)
            mine = cot[q : q + 1]
            along = jnp.mean(center * mine, axis=1, keepdims=True)
            out = inner * (mine - mean_cot[q : q + 1]) - center * (inner * inner * inner * along)
            out_ref[span, :] = out.astype(BF)


def per_device(image_in, text_in, proj_img, proj_txt, img_gain, txt_gain, logit_scale, positive):
    t_index = lax.axis_index("t")
    h_index = lax.axis_index("h")
    g_index = (lax.axis_index("z") * 4 + lax.axis_index("x")) * 2 + lax.axis_index("c")
    y_index = h_index * 4 + t_index
    place = jnp.stack([y_index, h_index, t_index, g_index]).astype(jnp.int32)
    emb = proj_img.shape[1]

    width = emb // 4
    w = jnp.concatenate([proj_img, proj_txt, jnp.zeros((1, emb), BF)], 0)
    w = lax.dynamic_slice(w, (0, width * t_index), (24, width))
    w = jnp.concatenate([w[:8], w[8:16], w[16:]], 1)
    w = jnp.broadcast_to(w[None], (32, 8, 3 * width))
    w = lax.all_gather(exchange(w, ZX), "c", axis=0).reshape(512, 3 * width)

    mine, theirs = pool_call(place, image_in, text_in, img_gain, txt_gain, positive)
    theirs = lax.all_gather(theirs, Y, axis=0, axis_index_groups=[[0, 6], [1, 7], [2, 4], [3, 5]])
    row_pos = theirs[:, :12, 519].astype(F32) * 32.0 + theirs[:, :12, 527].astype(F32)
    is_mine = lax.iota(jnp.int32, 2)[:, None] == h_index
    row_pos = jnp.where(is_mine, positive.astype(F32)[None], row_pos)
    row_pos = jnp.pad(row_pos.reshape(8, 3), ((0, 0), (0, 3)), constant_values=-1.0)
    row_pos = row_pos.reshape(48, 1).astype(jnp.int32)

    (part,) = kernel_call(
        project_kernel,
        [((192, 2 * width), BF)],
        [place, mine, theirs.reshape(64, 768), w],
        smem=(0,),
    )
    parts = exchange(part.reshape(8, 24, 2 * width), Y).reshape(192, 2 * width)

    own_digits = lax.dynamic_slice(positive, (3 * t_index,), (3,))
    own_digits = jnp.concatenate([own_digits // 32, own_digits % 32]).astype(F32)
    own_digits = jnp.pad(own_digits, (0, 122))[None]
    rows, far, inv = kernel_call(
        unit_kernel,
        [((48, emb), BF), ((256, 1024), BF), ((8, 128), F32)],
        [place, parts, own_digits],
        scratch=[pltpu.VMEM((64, emb), F32), pltpu.VMEM((64, 128), F32)],
        smem=(0,),
    )
    fa, fb = both_cores(exchange(far.reshape(32, 8, 1024), ZX))

    scores, far = kernel_call(
        score_kernel,
        [((48, 512), F32), ((256, 128), F32)],
        [place, logit_scale, rows, fa, fb, row_pos],
        smem=(0, 1),
    )
    far = exchange(far.reshape(64, 4, 128), ZXC).reshape(256, 128)

    item_pos = jnp.concatenate([fa.reshape(32, 8, 1024)[:, 3, 768:774], fb.reshape(32, 8, 1024)[:, 3, 768:774]])
    item_pos = item_pos.astype(F32)
    item_pos = item_pos[:, :3] * 32.0 + item_pos[:, 3:]
    item_pos = jnp.pad(item_pos, ((0, 0), (0, 5)), constant_values=-1.0).reshape(1, 512)
    item_pos = item_pos.astype(jnp.int32)
    (ways,) = kernel_call(
        coef_kernel,
        [((384, 768), BF)],
        [place, logit_scale, scores, far, row_pos, item_pos, fa, fb],
        smem=(0, 1),
    )
    got = exchange(ways.reshape(8, 48, 768), Y).reshape(384, 768)
    unit_part = lax.dynamic_slice(rows, (0, width * t_index), (48, width))
    pool, loss = kernel_call(
        back_kernel, [((64, 768), BF), ((8, 128), F32)], [got, unit_part, w]
    )
    mean_loss = loss[0, :1]
    pool = exchange(pool.reshape(8, 8, 768), Y).reshape(64, 768)
    count_i, width_i = image_in.shape[1:]
    count_t, width_t = text_in.shape[1:]
    img_own = lax.dynamic_slice_in_dim(image_in, 3 * t_index, 3, 0).reshape(-1, width_i)
    txt_own = lax.dynamic_slice_in_dim(text_in, 3 * t_index, 3, 0).reshape(-1, width_t)
    img_grads, txt_grads = kernel_call(
        token_kernel,
        [(img_own.shape, BF), (txt_own.shape, BF)],
        [pool, inv, img_own, txt_own, img_gain, txt_gain],
    )
    img_grads = img_grads.reshape(3, count_i, width_i)
    txt_grads = txt_grads.reshape(3, count_t, width_t)
    return (mean_loss, img_grads[None], txt_grads[None])


def solution(mesh):
    fine = Mesh(mesh.devices.reshape(4, 2, 8, 4, 2), ("t", "h", "z", "x", "c"))
    in_specs = (
        P(DP, None, None),
        P(DP, None, None),
        P(DP, None),
        P(DP, None),
        P(),
        P(),
        P(),
        P(DP),
    )
    out_specs = (P(), P("t", DP, None, None), P("t", DP, None, None))
    return jax.shard_map(
        per_device, mesh=fine, in_specs=in_specs, out_specs=out_specs, check_vma=False
    )
```

```python
import functools

import jax
import jax.numpy as jnp
from jax import lax
from jax.experimental import pallas as pl
from jax.experimental.pallas import tpu as pltpu
from jax.sharding import Mesh, PartitionSpec as P

BF = jnp.bfloat16
F32 = jnp.float32
Y = ("h", "t")
ZX = ("z", "x")
ZXC = ("z", "x", "c")
DP = ("h", "z", "x", "c")
LOW = -1e30
ROWS_DOT = (((1,), (1,)), ((), ()))


def exchange(blocks, axes):
    return lax.all_to_all(blocks, axes, 0, 0, tiled=True)


def both_cores(blocks):
    half = blocks.shape[0] // 2
    parts = [lax.all_gather(part, "c", axis=0) for part in (blocks[:half], blocks[half:])]
    return [part.reshape(-1, blocks.shape[2]) for part in parts]


def kernel_call(body, outs, args, scratch=(), smem=()):
    vmem = pl.BlockSpec(memory_space=pltpu.VMEM)
    return pl.pallas_call(
        body,
        out_shape=[jax.ShapeDtypeStruct(shape, kind) for shape, kind in outs],
        in_specs=[
            pl.BlockSpec(memory_space=pltpu.SMEM) if k in smem else vmem for k in range(len(args))
        ],
        out_specs=[vmem] * len(outs),
        scratch_shapes=list(scratch),
        compiler_params=pltpu.CompilerParams(vmem_limit_bytes=40 * 1024 * 1024),
    )(*args)


def slab_place(dense, wide, skip):
    row = skip + dense % wide
    return (row // 8) * 256 + ((dense // wide) % 2) * 128 + (dense // (2 * wide)) * 8 + row % 8


def slab_row(shape):
    lane = lax.broadcasted_iota(jnp.int32, shape, 1)
    return (lane // 256) * 8 + lane % 8


def pool_kernel(
    place_ref,
    pos_ref,
    img_ref,
    txt_ref,
    ig_ref,
    tg_ref,
    mine_ref,
    theirs_ref,
    img_held,
    txt_held,
    img_rows,
    txt_rows,
    digits,
    sems,
):
    steps = img_ref.shape[0] // 2

    def copies(k):
        span = pl.ds(2 * k, 2)
        return (
            pltpu.make_async_copy(img_ref.at[span], img_held.at[span], sems.at[0, k]),
            pltpu.make_async_copy(txt_ref.at[span], txt_held.at[span], sems.at[1, k]),
        )

    for k in range(steps):
        for copy in copies(k):
            copy.start()
    for rows in (img_rows, txt_rows, digits):
        rows[...] = jnp.zeros_like(rows)
    spot = lax.broadcasted_iota(jnp.int32, (1, 128), 1)

    def two_pairs(k, carry):
        for copy in copies(k):
            copy.wait()
        for held, gain_ref, rows in ((img_held, ig_ref, img_rows), (txt_held, tg_ref, txt_rows)):
            values = held[pl.ds(2 * k, 2)].astype(F32)
            center = values - jnp.mean(values, axis=2, keepdims=True)
            spread = jnp.mean(center * center, axis=2, keepdims=True)
            mean = jnp.mean(center * lax.rsqrt(spread + 1e-05), axis=1)
            for b in range(2):
                rows[pl.ds(2 * k + b, 1), :] = mean[b : b + 1] * gain_ref[...][None]
        for b in range(2):
            place = pos_ref[2 * k + b]
            line = jnp.where(spot == 7, place // 32, jnp.where(spot == 15, place % 32, 0))
            digits[pl.ds(2 * k + b, 1), :] = line.astype(F32)
        return carry

    lax.fori_loop(0, steps, two_pairs, 0)
    found = jnp.zeros((64, 768), F32)
    lane = lax.broadcasted_iota(jnp.int32, (1, 768), 1)
    slab = (lane % 128) // 8 * 2 + (lane // 128) % 2
    for rows, wide, skip in ((img_rows, 13, 0), (txt_rows, 10, 13)):
        width = 32 * wide
        row = slab_row((1, 768)) - skip
        wanted = jnp.where((row >= 0) & (row < wide), slab * wide + row, -1)
        dense = lax.broadcasted_iota(jnp.int32, (width, 768), 0)
        pick = jnp.where(dense == wanted, 1.0, 0.0).astype(BF)
        held = rows[...]
        quarters = [held[:, width * k : width * k + width] for k in range(4)]
        quarters = jnp.concatenate(quarters, 0).astype(BF)
        found += jnp.dot(quarters, pick, preferred_element_type=F32)
    line = digits[...]
    blank = jnp.zeros_like(line)
    line = jnp.concatenate([line, blank, line, blank], 0)
    found = jnp.concatenate([found[:, :512], found[:, 512:640] + line, found[:, 640:]], 1)
    first = place_ref[1] == 0
    mine_ref[...] = jnp.where(first, found[:32], found[32:]).astype(BF)
    theirs_ref[...] = jnp.where(first, found[32:], found[:32]).astype(BF)


def pool_call(place, image_in, text_in, img_gain, txt_gain, positive):
    pairs, _, width_i = image_in.shape
    width_t = text_in.shape[2]
    vmem = pl.BlockSpec(memory_space=pltpu.VMEM)
    smem = pl.BlockSpec(memory_space=pltpu.SMEM)
    whole = pl.BlockSpec(memory_space=pl.ANY)
    return pl.pallas_call(
        pool_kernel,
        out_shape=[jax.ShapeDtypeStruct((32, 768), BF)] * 2,
        in_specs=[smem, smem, whole, whole, vmem, vmem],
        out_specs=[vmem, vmem],
        scratch_shapes=[
            pltpu.VMEM(image_in.shape, BF),
            pltpu.VMEM(text_in.shape, BF),
            pltpu.VMEM((16, width_i), F32),
            pltpu.VMEM((16, width_t), F32),
            pltpu.VMEM((16, 128), F32),
            pltpu.SemaphoreType.DMA((2, pairs // 2)),
        ],
        cost_estimate=pl.CostEstimate(
            flops=10 * (image_in.size + text_in.size),
            bytes_accessed=2 * (image_in.size + text_in.size),
            transcendentals=0,
        ),
        compiler_params=pltpu.CompilerParams(vmem_limit_bytes=60 * 1024 * 1024),
    )(place, positive, image_in, text_in, img_gain, txt_gain)


def weight_quarter(w_ref, a):
    return jnp.concatenate([w_ref[k + 128 * a : k + 128 * a + 128, :] for k in (0, 256)], 0)


def project_kernel(place_ref, mine_ref, theirs_ref, w_ref, out_ref):
    width = w_ref.shape[1] // 3
    part = jnp.zeros((48, width), F32)
    inside = slab_row((12, 768))
    for a in range(2):
        pieces = []
        for h in range(2):
            rows = jnp.where(
                place_ref[1] == h,
                mine_ref[16 * a : 16 * a + 16, :].astype(F32),
                theirs_ref[32 * h + 16 * a : 32 * h + 16 * a + 16, :].astype(F32),
            )[:12]
            img_rows = jnp.where(inside < 13, rows, 0.0)
            txt_rows = jnp.where((inside >= 13) & (inside < 23), rows, 0.0)
            for t in range(4):
                pieces += [img_rows[3 * t : 3 * t + 3], txt_rows[3 * t : 3 * t + 3]]
        left = jnp.concatenate(pieces, 0).astype(BF)
        quarter = weight_quarter(w_ref, a)
        for j in range(3):
            part += jnp.dot(
                left[:, 256 * j : 256 * j + 256],
                quarter[:, width * j : width * j + width],
                preferred_element_type=F32,
            )
    packed = jnp.concatenate([part[:24], part[24:]], 1)
    out_ref[...] = jnp.concatenate([packed] * 8, 0).astype(BF)


def in_blocks(values):
    blank = jnp.zeros((1, values.shape[1]), F32)
    pieces = []
    for k in range(8):
        pieces += [values[6 * k : 6 * k + 3], blank, values[6 * k + 3 : 6 * k + 6], blank]
    return jnp.concatenate(pieces, 0)


def unit_kernel(place_ref, parts_ref, digits_ref, rows_ref, far_ref, inv_ref, held, held_inv):
    spread = parts_ref[...].astype(F32)
    width = spread.shape[1] // 2
    blocks = [spread[24 * k : 24 * k + 24] + spread[96 + 24 * k : 120 + 24 * k] for k in range(4)]
    blocks = [jnp.concatenate([part[:, :width], part[:, width:]], 0) for part in blocks]
    projected = jnp.concatenate(blocks, 1)
    inv = lax.rsqrt(jnp.sum(projected * projected, axis=1, keepdims=True) + 1e-06)
    unit = projected * inv
    rows_ref[...] = unit.astype(BF)
    held[...] = in_blocks(unit)
    held_inv[...] = in_blocks(jnp.broadcast_to(inv, (48, 128)))
    own = pl.ds(pl.multiple_of(8 * place_ref[0], 8), 8)
    inv_ref[...] = held_inv[own, :]
    block = held[own, :]
    free = jnp.concatenate([digits_ref[...], jnp.zeros((1, 128), F32)], 1)
    pieces = []
    for k in (0, 4):
        ends = [block[k + q : k + q + 1, 1024:] for q in range(3)]
        pieces += [block[k : k + 3, :1024], jnp.concatenate(ends + [free], 1)]
    block = jnp.concatenate(pieces, 0)
    block = jnp.concatenate([block, block], 0).astype(BF)
    for k in range(16):
        far_ref[16 * k : 16 * k + 16, :] = block


def tile_masks(place_ref):
    h, t, g = place_ref[1], place_ref[2], place_ref[3]
    row = lax.broadcasted_iota(jnp.int32, (48, 1), 0)
    item = lax.broadcasted_iota(jnp.int32, (1, 512), 1)
    item_g = ((item // 256) * 16 + (item % 128) // 8) * 2 + (item // 128) % 2
    item_pair = (h * 64 + item_g) * 12 + 3 * t + item % 4
    row_pair = ((row // 24) * 64 + g) * 12 + ((row // 6) % 4) * 3 + row % 3
    row_txt = (row % 6) // 3
    item_txt = jnp.where(item % 4 < 3, (item % 8) // 4, -1)
    valid = item_txt == 1 - row_txt
    return valid, row_pair, item_pair, row_txt, item_txt


def log_total(values, axis):
    largest = jnp.max(values, axis=axis, keepdims=True)
    return largest + jnp.log(jnp.sum(jnp.exp(values - largest), axis=axis, keepdims=True))


def score_kernel(place_ref, logit_ref, rows_ref, fa_ref, fb_ref, row_pos_ref, scores_ref, far_ref):
    rows = rows_ref[...]
    ends = rows[:, 1024:]
    blank = jnp.zeros_like(ends)
    ends = [[ends if k == q else blank for k in range(3)] for q in range(3)]
    ends = jnp.concatenate([jnp.concatenate(line, 1) for line in ends], 0)

    def dots(left, width):
        return jnp.concatenate(
            [
                lax.dot_general(left, ref[:, :width], ROWS_DOT, preferred_element_type=F32)
                for ref in (fa_ref, fb_ref)
            ],
            1,
        )

    scores = dots(rows[:, :1024], 1024)
    ends = dots(ends, 768)
    lane = lax.broadcasted_iota(jnp.int32, (48, 512), 1) % 4
    for q in range(3):
        moved = pltpu.roll(ends[48 * q : 48 * q + 48], 512 - (3 - q), 1)
        scores += jnp.where(lane == q, moved, 0.0)
    scores = logit_ref[0] * scores
    scores_ref[...] = scores
    valid, _, item_pair, row_txt, item_txt = tile_masks(place_ref)
    masked = jnp.where(valid, scores, LOW)
    item_part = log_total(masked, 0)
    hit = jnp.where(item_txt == 1, item_pair, -1) == jnp.where(row_txt == 0, row_pos_ref[...], -2)
    matched = jnp.sum(
        jnp.sum(jnp.where(hit, scores, 0.0), axis=1, keepdims=True), axis=0, keepdims=True
    )
    lane = lax.broadcasted_iota(jnp.int32, (1, 512), 1)
    item_part = jnp.where(lane == 3, matched, item_part)
    lines = jnp.concatenate([item_part[:, 128 * k : 128 * k + 128] for k in range(4)] * 2, 0)
    for k in range(32):
        far_ref[8 * k : 8 * k + 8, :] = lines


def in_parts(values, count):
    parts = []
    for _ in range(count):
        part = values.astype(BF).astype(F32)
        parts.append(part)
        values = values - part
    return parts


def times_items(left, fa_ref, fb_ref):
    def times(part, columns):
        return jnp.dot(part[:, :256], fa_ref[:, columns], preferred_element_type=F32) + jnp.dot(
            part[:, 256:], fb_ref[:, columns], preferred_element_type=F32
        )

    start = times(left, slice(0, 1024))
    last = lax.broadcasted_iota(jnp.int32, left.shape, 1) % 4 == 3
    wide = left.astype(F32)
    ends = jnp.zeros((left.shape[0], 256), F32)
    for q in range(3):
        moved = jnp.where(last, pltpu.roll(wide, 3 - q, 1), 0.0).astype(BF)
        ends += times(moved, slice(256 * q, 256 * q + 256))
    return jnp.concatenate([start, ends], 1)


def coef_kernel(
    place_ref, logit_ref, scores_ref, far_ref, row_pos_ref, item_pos_ref, fa_ref, fb_ref, out_ref
):
    logit = logit_ref[0]
    scores = scores_ref[...]
    seen = far_ref[...].reshape(32, 8, 128)
    largest = jnp.max(seen, axis=0)
    largest = jnp.maximum(largest[:4], largest[4:])
    both = jnp.concatenate([largest, largest], 0)
    total = jnp.sum(jnp.exp(seen - both[None]), axis=0)
    lines = largest + jnp.log(total[:4] + total[4:])
    item_lse = jnp.concatenate([lines[k : k + 1] for k in range(4)], 1)
    summed = jnp.sum(seen, axis=0)
    summed = summed[:1] + summed[4:5]
    valid, row_pair, item_pair, row_txt, item_txt = tile_masks(place_ref)
    img_hit = jnp.where(item_txt == 1, item_pair, -1) == jnp.where(
        row_txt == 0, row_pos_ref[...], -2
    )
    txt_hit = jnp.where(item_txt == 0, item_pos_ref[...], -1) == jnp.where(
        row_txt == 1, row_pair, -2
    )
    twice = jnp.where(img_hit, 2.0, jnp.where(txt_hit, 2.0, 0.0))
    lse_total = jnp.sum(jnp.where(item_txt >= 0, item_lse, 0.0), axis=1, keepdims=True)
    lane = lax.broadcasted_iota(jnp.int32, (1, 128), 1)
    matched = jnp.sum(jnp.where(lane == 3, summed, 0.0), axis=1, keepdims=True)
    value = lse_total - 2.0 * matched
    masked = jnp.where(valid, scores, LOW)
    row_part = log_total(masked, 1)
    by_row = (0.5 * logit) * jnp.exp(masked - row_part)
    by_item = (0.5 * logit) * (jnp.exp(masked - item_lse) - twice)
    coefs = [jnp.where(valid, part, 0.0).astype(BF) for part in (by_row, by_item)]
    along = [
        jnp.sum(part.astype(F32) * scores, axis=1, keepdims=True) / logit for part in coefs
    ]
    cot = times_items(jnp.concatenate(coefs, 0), fa_ref, fb_ref)
    riders = (
        in_parts(row_part, 3)
        + in_parts(along[0], 2)
        + in_parts(along[1], 2)
        + in_parts(jnp.broadcast_to(value, (48, 1)), 2)
    )
    column = lax.broadcasted_iota(jnp.int32, (48, 64), 1)
    extra = jnp.zeros((48, 64), F32)
    for k, rider in enumerate(riders):
        extra = jnp.where(column == k, rider, extra)
    width = cot.shape[1] // 8
    for k in range(8):
        first = width * (2 * (k % 4) + k // 4)
        part = cot[:, first : first + width]
        way = jnp.concatenate([part[:48], part[48:], extra], 1).astype(BF)
        out_ref[48 * k : 48 * k + 48, :] = way


def back_kernel(place_ref, got_ref, unit_ref, w_ref, other_ref, out_ref, loss_ref):
    width = unit_ref.shape[1]
    got = [got_ref[48 * k : 48 * k + 48, :].astype(F32) for k in range(8)]
    riders = [[part[:, 2 * width + k : 2 * width + k + 1] for k in range(9)] for part in got]
    parts = [r[0] + r[1] + r[2] for r in riders]
    largest = functools.reduce(jnp.maximum, parts)
    total = sum(jnp.exp(part - largest) for part in parts)
    lse = largest + jnp.log(total)
    along = jnp.zeros((48, 1), F32)
    value = jnp.zeros((48, 1), F32)
    summed = jnp.zeros((48, width), F32)
    for part, r, own in zip(got, riders, parts):
        weight = jnp.exp(own - lse)
        along += weight * (r[3] + r[4]) + (r[5] + r[6])
        value += r[7] + r[8]
        summed += weight * part[:, :width] + part[:, width : 2 * width]
    loss_ref[...] = jnp.broadcast_to(value[:8] / (2.0 * 1536), (8, 128))
    proj_cot = (summed - unit_ref[...].astype(F32) * along).astype(BF)
    is_img = slab_row((48, 768)) < 13
    first = place_ref[1] == 0

    def features(columns):
        pool = [
            lax.dot_general(proj_cot, part, ROWS_DOT, preferred_element_type=F32)
            for part in columns
        ]
        pool = jnp.concatenate(pool, 1)
        return jnp.where(is_img, pool, pltpu.roll(pool, 45, 0))

    own, other = [], []
    for a in range(2):
        quarter = weight_quarter(w_ref, a)
        columns = []
        for j in range(3):
            pair = quarter[:, 2 * width * j : 2 * width * j + 2 * width]
            columns.append(jnp.where(first, pair[:, :width], pair[:, width:]))
        own.append(features(columns))
        quarter = weight_quarter(other_ref, a)
        other.append(features([quarter[:, width * j : width * j + width] for j in range(3)]))
    mixed = [jnp.where(first, x, y) for x, y in zip(own + other, other + own)]
    blank = jnp.zeros((1, 768), F32)
    pieces = []
    for k in range(8):
        for pool in mixed:
            pieces += [pool[6 * k : 6 * k + 3], blank]
    out_ref[...] = jnp.concatenate(pieces, 0).astype(BF)


def token_kernel(pool_ref, inv_ref, img_ref, txt_ref, ig_ref, tg_ref, img_out, txt_out):
    pool = pool_ref[...]
    inv = inv_ref[...][:, :1]
    for x_ref, gain_ref, out_ref, wide, skip, at in (
        (img_ref, ig_ref, img_out, 13, 0, 0),
        (txt_ref, tg_ref, txt_out, 10, 13, 4),
    ):
        dense = lax.broadcasted_iota(jnp.int32, (1, 32 * wide), 1)
        lane = lax.broadcasted_iota(jnp.int32, (768, 32 * wide), 0)
        pick = jnp.where(lane == slab_place(dense, wide, skip), 1.0, 0.0).astype(BF)
        found = jnp.dot(pool, pick, preferred_element_type=F32)
        found = sum(found[16 * k : 16 * k + 16] for k in range(8))
        cot = jnp.concatenate([found[4 * k : 4 * k + 4] for k in range(4)], 1)
        cot = cot * inv[at : at + 4] * gain_ref[...][None]
        mean_cot = jnp.mean(cot, axis=1, keepdims=True)
        count = x_ref.shape[0] // 3
        for q in range(3):
            span = slice(count * q, count * q + count)
            values = x_ref[span, :].astype(F32)
            center = values - jnp.mean(values, axis=1, keepdims=True)
            inner = lax.rsqrt(jnp.mean(center * center, axis=1, keepdims=True) + 1e-05)
            mine = cot[q : q + 1]
            along = jnp.mean(center * mine, axis=1, keepdims=True)
            out = inner * (mine - mean_cot[q : q + 1]) - center * (inner * inner * inner * along)
            out_ref[span, :] = out.astype(BF)


def per_device(image_in, text_in, proj_img, proj_txt, img_gain, txt_gain, logit_scale, positive):
    t_index = lax.axis_index("t")
    h_index = lax.axis_index("h")
    g_index = (lax.axis_index("z") * 4 + lax.axis_index("x")) * 2 + lax.axis_index("c")
    y_index = h_index * 4 + t_index
    place = jnp.stack([y_index, h_index, t_index, g_index]).astype(jnp.int32)
    emb = proj_img.shape[1]

    width = emb // 4
    w = jnp.concatenate([proj_img, proj_txt, jnp.zeros((1, emb), BF)], 0)
    w = lax.dynamic_slice(w, (0, width * t_index), (24, width))
    w = jnp.concatenate([w[:8], w[8:16], w[16:]], 1)
    w = jnp.broadcast_to(w[None], (32, 8, 3 * width))
    w = lax.all_gather(exchange(w, ZX), "c", axis=0).reshape(512, 3 * width)

    mine, theirs = pool_call(place, image_in, text_in, img_gain, txt_gain, positive)
    theirs = lax.all_gather(theirs, Y, axis=0, axis_index_groups=[[0, 6], [1, 7], [2, 4], [3, 5]])
    row_pos = theirs[:, :12, 519].astype(F32) * 32.0 + theirs[:, :12, 527].astype(F32)
    is_mine = lax.iota(jnp.int32, 2)[:, None] == h_index
    row_pos = jnp.where(is_mine, positive.astype(F32)[None], row_pos)
    row_pos = jnp.pad(row_pos.reshape(8, 3), ((0, 0), (0, 3)), constant_values=-1.0)
    row_pos = row_pos.reshape(48, 1).astype(jnp.int32)

    (part,) = kernel_call(
        project_kernel,
        [((192, 2 * width), BF)],
        [place, mine, theirs.reshape(64, 768), w],
        smem=(0,),
    )
    parts = exchange(part.reshape(8, 24, 2 * width), Y).reshape(192, 2 * width)

    own_digits = lax.dynamic_slice(positive, (3 * t_index,), (3,))
    own_digits = jnp.concatenate([own_digits // 32, own_digits % 32]).astype(F32)
    own_digits = jnp.pad(own_digits, (0, 122))[None]
    rows, far, inv = kernel_call(
        unit_kernel,
        [((48, emb), BF), ((256, 1024), BF), ((8, 128), F32)],
        [place, parts, own_digits],
        scratch=[pltpu.VMEM((64, emb), F32), pltpu.VMEM((64, 128), F32)],
        smem=(0,),
    )
    half = width // 2
    w_held, far = lax.optimization_barrier((w, far))
    parts = w_held.reshape(512, 3, 2, half)
    w_other = jnp.where(h_index == 0, parts[:, :, 1], parts[:, :, 0]).reshape(512, 3 * half)
    w_other = lax.ppermute(w_other, "h", [(0, 1), (1, 0)])
    fa, fb = both_cores(exchange(far.reshape(32, 8, 1024), ZX))
    fa, w_other = lax.optimization_barrier((fa, w_other))

    scores, far = kernel_call(
        score_kernel,
        [((48, 512), F32), ((256, 128), F32)],
        [place, logit_scale, rows, fa, fb, row_pos],
        smem=(0, 1),
    )
    far = exchange(far.reshape(64, 4, 128), ZXC).reshape(256, 128)

    item_pos = jnp.concatenate([fa.reshape(32, 8, 1024)[:, 3, 768:774], fb.reshape(32, 8, 1024)[:, 3, 768:774]])
    item_pos = item_pos.astype(F32)
    item_pos = item_pos[:, :3] * 32.0 + item_pos[:, 3:]
    item_pos = jnp.pad(item_pos, ((0, 0), (0, 5)), constant_values=-1.0).reshape(1, 512)
    item_pos = item_pos.astype(jnp.int32)
    (ways,) = kernel_call(
        coef_kernel,
        [((384, 384), BF)],
        [place, logit_scale, scores, far, row_pos, item_pos, fa, fb],
        smem=(0, 1),
    )
    got = exchange(ways.reshape(8, 48, 384), Y).reshape(384, 384)
    unit_part = lax.dynamic_slice(rows, (0, half * (2 * t_index + h_index)), (48, half))
    pool, loss = kernel_call(
        back_kernel,
        [((128, 768), BF), ((8, 128), F32)],
        [place, got, unit_part, w, w_other],
        smem=(0,),
    )
    mean_loss = loss[0, :1]
    pool = exchange(pool.reshape(8, 16, 768), Y).reshape(128, 768)
    count_i, width_i = image_in.shape[1:]
    count_t, width_t = text_in.shape[1:]
    img_own = lax.dynamic_slice_in_dim(image_in, 3 * t_index, 3, 0).reshape(-1, width_i)
    txt_own = lax.dynamic_slice_in_dim(text_in, 3 * t_index, 3, 0).reshape(-1, width_t)
    img_grads, txt_grads = kernel_call(
        token_kernel,
        [(img_own.shape, BF), (txt_own.shape, BF)],
        [pool, inv, img_own, txt_own, img_gain, txt_gain],
    )
    img_grads = img_grads.reshape(3, count_i, width_i)
    txt_grads = txt_grads.reshape(3, count_t, width_t)
    return (mean_loss, img_grads[None], txt_grads[None])


def solution(mesh):
    fine = Mesh(mesh.devices.reshape(4, 2, 8, 4, 2), ("t", "h", "z", "x", "c"))
    in_specs = (
        P(DP, None, None),
        P(DP, None, None),
        P(DP, None),
        P(DP, None),
        P(),
        P(),
        P(),
        P(DP),
    )
    out_specs = (P(), P("t", DP, None, None), P("t", DP, None, None))
    return jax.shard_map(
        per_device, mesh=fine, in_specs=in_specs, out_specs=out_specs, check_vma=False
    )
```

```python
import functools

import jax
import jax.numpy as jnp
from jax import lax
from jax.experimental import pallas as pl
from jax.experimental.pallas import tpu as pltpu
from jax.sharding import Mesh, PartitionSpec as P

BF = jnp.bfloat16
F32 = jnp.float32
Y = ("h", "t")
ZX = ("z", "x")
ZXC = ("z", "x", "c")
DP = ("h", "z", "x", "c")
LOW = -1e30
ROWS_DOT = (((1,), (1,)), ((), ()))


def exchange(blocks, axes):
    return lax.all_to_all(blocks, axes, 0, 0, tiled=True)


def both_cores(blocks):
    half = blocks.shape[0] // 2
    parts = [lax.all_gather(part, "c", axis=0) for part in (blocks[:half], blocks[half:])]
    return [part.reshape(-1, blocks.shape[2]) for part in parts]


def kernel_call(body, outs, args, scratch=(), smem=()):
    vmem = pl.BlockSpec(memory_space=pltpu.VMEM)
    return pl.pallas_call(
        body,
        out_shape=[jax.ShapeDtypeStruct(shape, kind) for shape, kind in outs],
        in_specs=[
            pl.BlockSpec(memory_space=pltpu.SMEM) if k in smem else vmem for k in range(len(args))
        ],
        out_specs=[vmem] * len(outs),
        scratch_shapes=list(scratch),
        compiler_params=pltpu.CompilerParams(vmem_limit_bytes=40 * 1024 * 1024),
    )(*args)


def slab_place(dense, wide, skip):
    row = skip + dense % wide
    return (row // 8) * 256 + ((dense // wide) % 2) * 128 + (dense // (2 * wide)) * 8 + row % 8


def slab_row(shape):
    lane = lax.broadcasted_iota(jnp.int32, shape, 1)
    return (lane // 256) * 8 + lane % 8


def pool_kernel(
    place_ref,
    pos_ref,
    img_ref,
    txt_ref,
    ig_ref,
    tg_ref,
    mine_ref,
    theirs_ref,
    img_held,
    txt_held,
    img_rows,
    txt_rows,
    digits,
    sems,
):
    steps = img_ref.shape[0] // 2

    def copies(k):
        span = pl.ds(2 * k, 2)
        return (
            pltpu.make_async_copy(img_ref.at[span], img_held.at[span], sems.at[0, k]),
            pltpu.make_async_copy(txt_ref.at[span], txt_held.at[span], sems.at[1, k]),
        )

    for k in range(steps):
        for copy in copies(k):
            copy.start()
    for rows in (img_rows, txt_rows, digits):
        rows[...] = jnp.zeros_like(rows)
    spot = lax.broadcasted_iota(jnp.int32, (1, 128), 1)

    def two_pairs(k, carry):
        for copy in copies(k):
            copy.wait()
        for held, gain_ref, rows in ((img_held, ig_ref, img_rows), (txt_held, tg_ref, txt_rows)):
            values = held[pl.ds(2 * k, 2)].astype(F32)
            center = values - jnp.mean(values, axis=2, keepdims=True)
            spread = jnp.mean(center * center, axis=2, keepdims=True)
            mean = jnp.mean(center * lax.rsqrt(spread + 1e-05), axis=1)
            for b in range(2):
                rows[pl.ds(2 * k + b, 1), :] = mean[b : b + 1] * gain_ref[...][None]
        for b in range(2):
            place = pos_ref[2 * k + b]
            line = jnp.where(spot == 7, place // 32, jnp.where(spot == 15, place % 32, 0))
            digits[pl.ds(2 * k + b, 1), :] = line.astype(F32)
        return carry

    lax.fori_loop(0, steps, two_pairs, 0)
    found = jnp.zeros((64, 768), F32)
    lane = lax.broadcasted_iota(jnp.int32, (1, 768), 1)
    slab = (lane % 128) // 8 * 2 + (lane // 128) % 2
    for rows, wide, skip in ((img_rows, 13, 0), (txt_rows, 10, 13)):
        width = 32 * wide
        row = slab_row((1, 768)) - skip
        wanted = jnp.where((row >= 0) & (row < wide), slab * wide + row, -1)
        dense = lax.broadcasted_iota(jnp.int32, (width, 768), 0)
        pick = jnp.where(dense == wanted, 1.0, 0.0).astype(BF)
        held = rows[...]
        quarters = [held[:, width * k : width * k + width] for k in range(4)]
        quarters = jnp.concatenate(quarters, 0).astype(BF)
        found += jnp.dot(quarters, pick, preferred_element_type=F32)
    line = digits[...]
    blank = jnp.zeros_like(line)
    line = jnp.concatenate([line, blank, line, blank], 0)
    found = jnp.concatenate([found[:, :512], found[:, 512:640] + line, found[:, 640:]], 1)
    first = place_ref[1] == 0
    mine_ref[...] = jnp.where(first, found[:32], found[32:]).astype(BF)
    theirs_ref[...] = jnp.where(first, found[32:], found[:32]).astype(BF)


def pool_call(place, image_in, text_in, img_gain, txt_gain, positive):
    pairs, _, width_i = image_in.shape
    width_t = text_in.shape[2]
    vmem = pl.BlockSpec(memory_space=pltpu.VMEM)
    smem = pl.BlockSpec(memory_space=pltpu.SMEM)
    whole = pl.BlockSpec(memory_space=pl.ANY)
    return pl.pallas_call(
        pool_kernel,
        out_shape=[jax.ShapeDtypeStruct((32, 768), BF)] * 2,
        in_specs=[smem, smem, whole, whole, vmem, vmem],
        out_specs=[vmem, vmem],
        scratch_shapes=[
            pltpu.VMEM(image_in.shape, BF),
            pltpu.VMEM(text_in.shape, BF),
            pltpu.VMEM((16, width_i), F32),
            pltpu.VMEM((16, width_t), F32),
            pltpu.VMEM((16, 128), F32),
            pltpu.SemaphoreType.DMA((2, pairs // 2)),
        ],
        cost_estimate=pl.CostEstimate(
            flops=10 * (image_in.size + text_in.size),
            bytes_accessed=2 * (image_in.size + text_in.size),
            transcendentals=0,
        ),
        compiler_params=pltpu.CompilerParams(vmem_limit_bytes=60 * 1024 * 1024),
    )(place, positive, image_in, text_in, img_gain, txt_gain)


def weight_quarter(core_refs, a):
    return jnp.concatenate([ref[128 * a : 128 * a + 128, :] for ref in core_refs], 0)


def project_kernel(place_ref, mine_ref, theirs_ref, w_ref, out_ref):
    width = w_ref.shape[1] // 3
    part = jnp.zeros((48, width), F32)
    inside = slab_row((12, 768))
    for a in range(2):
        pieces = []
        for h in range(2):
            rows = jnp.where(
                place_ref[1] == h,
                mine_ref[16 * a : 16 * a + 16, :].astype(F32),
                theirs_ref[32 * h + 16 * a : 32 * h + 16 * a + 16, :].astype(F32),
            )[:12]
            img_rows = jnp.where(inside < 13, rows, 0.0)
            txt_rows = jnp.where((inside >= 13) & (inside < 23), rows, 0.0)
            for t in range(4):
                pieces += [img_rows[3 * t : 3 * t + 3], txt_rows[3 * t : 3 * t + 3]]
        left = jnp.concatenate(pieces, 0).astype(BF)
        quarter = weight_quarter((w_ref.at[:256], w_ref.at[256:]), a)
        for j in range(3):
            part += jnp.dot(
                left[:, 256 * j : 256 * j + 256],
                quarter[:, width * j : width * j + width],
                preferred_element_type=F32,
            )
    packed = jnp.concatenate([part[:24], part[24:]], 1)
    out_ref[...] = jnp.concatenate([packed] * 8, 0).astype(BF)


def in_blocks(values):
    blank = jnp.zeros((1, values.shape[1]), F32)
    pieces = []
    for k in range(8):
        pieces += [values[6 * k : 6 * k + 3], blank, values[6 * k + 3 : 6 * k + 6], blank]
    return jnp.concatenate(pieces, 0)


def unit_kernel(place_ref, parts_ref, digits_ref, rows_ref, far_ref, inv_ref, held, held_inv):
    spread = parts_ref[...].astype(F32)
    width = spread.shape[1] // 2
    blocks = [spread[24 * k : 24 * k + 24] + spread[96 + 24 * k : 120 + 24 * k] for k in range(4)]
    blocks = [jnp.concatenate([part[:, :width], part[:, width:]], 0) for part in blocks]
    projected = jnp.concatenate(blocks, 1)
    inv = lax.rsqrt(jnp.sum(projected * projected, axis=1, keepdims=True) + 1e-06)
    unit = projected * inv
    rows_ref[...] = unit.astype(BF)
    held[...] = in_blocks(unit)
    held_inv[...] = in_blocks(jnp.broadcast_to(inv, (48, 128)))
    own = pl.ds(pl.multiple_of(8 * place_ref[0], 8), 8)
    inv_ref[...] = held_inv[own, :]
    block = held[own, :]
    free = jnp.concatenate([digits_ref[...], jnp.zeros((1, 128), F32)], 1)
    pieces = []
    for k in (0, 4):
        ends = [block[k + q : k + q + 1, 1024:] for q in range(3)]
        pieces += [block[k : k + 3, :1024], jnp.concatenate(ends + [free], 1)]
    block = jnp.concatenate(pieces, 0)
    block = jnp.concatenate([block, block], 0).astype(BF)
    for k in range(16):
        far_ref[16 * k : 16 * k + 16, :] = block


def tile_masks(place_ref):
    h, t, g = place_ref[1], place_ref[2], place_ref[3]
    row = lax.broadcasted_iota(jnp.int32, (48, 1), 0)
    item = lax.broadcasted_iota(jnp.int32, (1, 512), 1)
    item_g = ((item // 256) * 16 + (item % 128) // 8) * 2 + (item // 128) % 2
    item_pair = (h * 64 + item_g) * 12 + 3 * t + item % 4
    row_pair = ((row // 24) * 64 + g) * 12 + ((row // 6) % 4) * 3 + row % 3
    row_txt = (row % 6) // 3
    item_txt = jnp.where(item % 4 < 3, (item % 8) // 4, -1)
    valid = item_txt == 1 - row_txt
    return valid, row_pair, item_pair, row_txt, item_txt


def log_total(values, axis):
    largest = jnp.max(values, axis=axis, keepdims=True)
    return largest + jnp.log(jnp.sum(jnp.exp(values - largest), axis=axis, keepdims=True))


def score_kernel(place_ref, logit_ref, rows_ref, fa_ref, fb_ref, row_pos_ref, scores_ref, far_ref):
    rows = rows_ref[...]
    ends = rows[:, 1024:]
    blank = jnp.zeros_like(ends)
    ends = [[ends if k == q else blank for k in range(3)] for q in range(3)]
    ends = jnp.concatenate([jnp.concatenate(line, 1) for line in ends], 0)

    def dots(left, width):
        return jnp.concatenate(
            [
                lax.dot_general(left, ref[:, :width], ROWS_DOT, preferred_element_type=F32)
                for ref in (fa_ref, fb_ref)
            ],
            1,
        )

    scores = dots(rows[:, :1024], 1024)
    ends = dots(ends, 768)
    lane = lax.broadcasted_iota(jnp.int32, (48, 512), 1) % 4
    for q in range(3):
        moved = pltpu.roll(ends[48 * q : 48 * q + 48], 512 - (3 - q), 1)
        scores += jnp.where(lane == q, moved, 0.0)
    scores = logit_ref[0] * scores
    scores_ref[...] = scores
    valid, _, item_pair, row_txt, item_txt = tile_masks(place_ref)
    masked = jnp.where(valid, scores, LOW)
    item_part = log_total(masked, 0)
    hit = jnp.where(item_txt == 1, item_pair, -1) == jnp.where(row_txt == 0, row_pos_ref[...], -2)
    matched = jnp.sum(
        jnp.sum(jnp.where(hit, scores, 0.0), axis=1, keepdims=True), axis=0, keepdims=True
    )
    lane = lax.broadcasted_iota(jnp.int32, (1, 512), 1)
    item_part = jnp.where(lane == 3, matched, item_part)
    lines = jnp.concatenate([item_part[:, 128 * k : 128 * k + 128] for k in range(4)] * 2, 0)
    for k in range(32):
        far_ref[8 * k : 8 * k + 8, :] = lines


def in_parts(values, count):
    parts = []
    for _ in range(count):
        part = values.astype(BF).astype(F32)
        parts.append(part)
        values = values - part
    return parts


def times_items(left, fa_ref, fb_ref):
    def times(part, columns):
        return jnp.dot(part[:, :256], fa_ref[:, columns], preferred_element_type=F32) + jnp.dot(
            part[:, 256:], fb_ref[:, columns], preferred_element_type=F32
        )

    start = times(left, slice(0, 1024))
    last = lax.broadcasted_iota(jnp.int32, left.shape, 1) % 4 == 3
    wide = left.astype(F32)
    ends = jnp.zeros((left.shape[0], 256), F32)
    for q in range(3):
        moved = jnp.where(last, pltpu.roll(wide, 3 - q, 1), 0.0).astype(BF)
        ends += times(moved, slice(256 * q, 256 * q + 256))
    return jnp.concatenate([start, ends], 1)


def coef_kernel(
    place_ref, logit_ref, scores_ref, far_ref, row_pos_ref, item_pos_ref, fa_ref, fb_ref, out_ref
):
    logit = logit_ref[0]
    scores = scores_ref[...]
    seen = far_ref[...].reshape(32, 8, 128)
    largest = jnp.max(seen, axis=0)
    largest = jnp.maximum(largest[:4], largest[4:])
    both = jnp.concatenate([largest, largest], 0)
    total = jnp.sum(jnp.exp(seen - both[None]), axis=0)
    lines = largest + jnp.log(total[:4] + total[4:])
    item_lse = jnp.concatenate([lines[k : k + 1] for k in range(4)], 1)
    summed = jnp.sum(seen, axis=0)
    summed = summed[:1] + summed[4:5]
    valid, row_pair, item_pair, row_txt, item_txt = tile_masks(place_ref)
    img_hit = jnp.where(item_txt == 1, item_pair, -1) == jnp.where(
        row_txt == 0, row_pos_ref[...], -2
    )
    txt_hit = jnp.where(item_txt == 0, item_pos_ref[...], -1) == jnp.where(
        row_txt == 1, row_pair, -2
    )
    twice = jnp.where(img_hit, 2.0, jnp.where(txt_hit, 2.0, 0.0))
    lse_total = jnp.sum(jnp.where(item_txt >= 0, item_lse, 0.0), axis=1, keepdims=True)
    lane = lax.broadcasted_iota(jnp.int32, (1, 128), 1)
    matched = jnp.sum(jnp.where(lane == 3, summed, 0.0), axis=1, keepdims=True)
    value = lse_total - 2.0 * matched
    masked = jnp.where(valid, scores, LOW)
    row_part = log_total(masked, 1)
    by_row = (0.5 * logit) * jnp.exp(masked - row_part)
    by_item = (0.5 * logit) * (jnp.exp(masked - item_lse) - twice)
    coefs = [jnp.where(valid, part, 0.0).astype(BF) for part in (by_row, by_item)]
    along = [
        jnp.sum(part.astype(F32) * scores, axis=1, keepdims=True) / logit for part in coefs
    ]
    cot = times_items(jnp.concatenate(coefs, 0), fa_ref, fb_ref)
    riders = (
        in_parts(row_part, 3)
        + in_parts(along[0], 2)
        + in_parts(along[1], 2)
        + in_parts(jnp.broadcast_to(value, (48, 1)), 2)
    )
    column = lax.broadcasted_iota(jnp.int32, (48, 64), 1)
    extra = jnp.zeros((48, 64), F32)
    for k, rider in enumerate(riders):
        extra = jnp.where(column == k, rider, extra)
    width = cot.shape[1] // 8
    for k in range(8):
        first = width * (2 * (k % 4) + k // 4)
        part = cot[:, first : first + width]
        way = jnp.concatenate([part[:48], part[48:], extra], 1).astype(BF)
        out_ref[48 * k : 48 * k + 48, :] = way


def back_kernel(
    place_ref, got_ref, unit_ref, w_ref, first_ref, second_ref, out_ref, loss_ref
):
    width = unit_ref.shape[1]
    got = [got_ref[48 * k : 48 * k + 48, :].astype(F32) for k in range(8)]
    riders = [[part[:, 2 * width + k : 2 * width + k + 1] for k in range(9)] for part in got]
    parts = [r[0] + r[1] + r[2] for r in riders]
    largest = functools.reduce(jnp.maximum, parts)
    total = sum(jnp.exp(part - largest) for part in parts)
    lse = largest + jnp.log(total)
    along = jnp.zeros((48, 1), F32)
    value = jnp.zeros((48, 1), F32)
    summed = jnp.zeros((48, width), F32)
    for part, r, own in zip(got, riders, parts):
        weight = jnp.exp(own - lse)
        along += weight * (r[3] + r[4]) + (r[5] + r[6])
        value += r[7] + r[8]
        summed += weight * part[:, :width] + part[:, width : 2 * width]
    loss_ref[...] = jnp.broadcast_to(value[:8] / (2.0 * 1536), (8, 128))
    proj_cot = (summed - unit_ref[...].astype(F32) * along).astype(BF)
    is_img = slab_row((48, 768)) < 13
    first = place_ref[1] == 0

    def features(columns):
        pool = [
            lax.dot_general(proj_cot, part, ROWS_DOT, preferred_element_type=F32)
            for part in columns
        ]
        pool = jnp.concatenate(pool, 1)
        return jnp.where(is_img, pool, pltpu.roll(pool, 45, 0))

    own, other = [], []
    for a in range(2):
        quarter = weight_quarter((w_ref.at[:256], w_ref.at[256:]), a)
        columns = []
        for j in range(3):
            pair = quarter[:, 2 * width * j : 2 * width * j + 2 * width]
            columns.append(jnp.where(first, pair[:, :width], pair[:, width:]))
        own.append(features(columns))
        quarter = weight_quarter((first_ref, second_ref), a)
        other.append(features([quarter[:, width * j : width * j + width] for j in range(3)]))
    mixed = [jnp.where(first, x, y) for x, y in zip(own + other, other + own)]
    blank = jnp.zeros((1, 768), F32)
    pieces = []
    for k in range(8):
        for pool in mixed:
            pieces += [pool[6 * k : 6 * k + 3], blank]
    out_ref[...] = jnp.concatenate(pieces, 0).astype(BF)


def token_kernel(pool_ref, inv_ref, img_ref, txt_ref, ig_ref, tg_ref, img_out, txt_out):
    pool = pool_ref[...]
    inv = inv_ref[...][:, :1]
    for x_ref, gain_ref, out_ref, wide, skip, at in (
        (img_ref, ig_ref, img_out, 13, 0, 0),
        (txt_ref, tg_ref, txt_out, 10, 13, 4),
    ):
        dense = lax.broadcasted_iota(jnp.int32, (1, 32 * wide), 1)
        lane = lax.broadcasted_iota(jnp.int32, (768, 32 * wide), 0)
        pick = jnp.where(lane == slab_place(dense, wide, skip), 1.0, 0.0).astype(BF)
        found = jnp.dot(pool, pick, preferred_element_type=F32)
        found = sum(found[16 * k : 16 * k + 16] for k in range(8))
        cot = jnp.concatenate([found[4 * k : 4 * k + 4] for k in range(4)], 1)
        cot = cot * inv[at : at + 4] * gain_ref[...][None]
        mean_cot = jnp.mean(cot, axis=1, keepdims=True)
        count = x_ref.shape[0] // 3
        for q in range(3):
            span = slice(count * q, count * q + count)
            values = x_ref[span, :].astype(F32)
            center = values - jnp.mean(values, axis=1, keepdims=True)
            inner = lax.rsqrt(jnp.mean(center * center, axis=1, keepdims=True) + 1e-05)
            mine = cot[q : q + 1]
            along = jnp.mean(center * mine, axis=1, keepdims=True)
            out = inner * (mine - mean_cot[q : q + 1]) - center * (inner * inner * inner * along)
            out_ref[span, :] = out.astype(BF)


def per_device(image_in, text_in, proj_img, proj_txt, img_gain, txt_gain, logit_scale, positive):
    t_index = lax.axis_index("t")
    h_index = lax.axis_index("h")
    g_index = (lax.axis_index("z") * 4 + lax.axis_index("x")) * 2 + lax.axis_index("c")
    y_index = h_index * 4 + t_index
    place = jnp.stack([y_index, h_index, t_index, g_index]).astype(jnp.int32)
    emb = proj_img.shape[1]

    width = emb // 4
    w = jnp.concatenate([proj_img, proj_txt, jnp.zeros((1, emb), BF)], 0)
    w = lax.dynamic_slice(w, (0, width * t_index), (24, width))
    w = jnp.concatenate([w[:8], w[8:16], w[16:]], 1)
    w = jnp.broadcast_to(w[None], (32, 8, 3 * width))
    w = lax.all_gather(exchange(w, ZX), "c", axis=0).reshape(512, 3 * width)

    mine, theirs = pool_call(place, image_in, text_in, img_gain, txt_gain, positive)
    theirs = lax.all_gather(theirs, Y, axis=0, axis_index_groups=[[0, 6], [1, 7], [2, 4], [3, 5]])
    row_pos = theirs[:, :12, 519].astype(F32) * 32.0 + theirs[:, :12, 527].astype(F32)
    is_mine = lax.iota(jnp.int32, 2)[:, None] == h_index
    row_pos = jnp.where(is_mine, positive.astype(F32)[None], row_pos)
    row_pos = jnp.pad(row_pos.reshape(8, 3), ((0, 0), (0, 3)), constant_values=-1.0)
    row_pos = row_pos.reshape(48, 1).astype(jnp.int32)

    (part,) = kernel_call(
        project_kernel,
        [((192, 2 * width), BF)],
        [place, mine, theirs.reshape(64, 768), w],
        smem=(0,),
    )
    parts = exchange(part.reshape(8, 24, 2 * width), Y).reshape(192, 2 * width)

    own_digits = lax.dynamic_slice(positive, (3 * t_index,), (3,))
    own_digits = jnp.concatenate([own_digits // 32, own_digits % 32]).astype(F32)
    own_digits = jnp.pad(own_digits, (0, 122))[None]
    rows, far, inv = kernel_call(
        unit_kernel,
        [((48, emb), BF), ((256, 1024), BF), ((8, 128), F32)],
        [place, parts, own_digits],
        scratch=[pltpu.VMEM((64, emb), F32), pltpu.VMEM((64, 128), F32)],
        smem=(0,),
    )
    half = width // 2
    swap = [(0, 1), (1, 0)]

    def columns_for_other(rows):
        parts = rows.reshape(256, 3, 2, half)
        return jnp.where(h_index == 0, parts[:, :, 1], parts[:, :, 0]).reshape(256, 3 * half)

    w_held, far = lax.optimization_barrier((w, far))
    w_first = lax.ppermute(columns_for_other(w_held[:256]), "h", swap)
    fa, fb = both_cores(exchange(far.reshape(32, 8, 1024), ZX))
    fa, w_first = lax.optimization_barrier((fa, w_first))

    scores, far = kernel_call(
        score_kernel,
        [((48, 512), F32), ((256, 128), F32)],
        [place, logit_scale, rows, fa, fb, row_pos],
        smem=(0, 1),
    )
    w_held, far = lax.optimization_barrier((w, far))
    w_second = lax.ppermute(columns_for_other(w_held[256:]), "h", swap)
    far = exchange(far.reshape(64, 4, 128), ZXC).reshape(256, 128)
    far, w_second = lax.optimization_barrier((far, w_second))

    item_pos = jnp.concatenate([fa.reshape(32, 8, 1024)[:, 3, 768:774], fb.reshape(32, 8, 1024)[:, 3, 768:774]])
    item_pos = item_pos.astype(F32)
    item_pos = item_pos[:, :3] * 32.0 + item_pos[:, 3:]
    item_pos = jnp.pad(item_pos, ((0, 0), (0, 5)), constant_values=-1.0).reshape(1, 512)
    item_pos = item_pos.astype(jnp.int32)
    (ways,) = kernel_call(
        coef_kernel,
        [((384, 384), BF)],
        [place, logit_scale, scores, far, row_pos, item_pos, fa, fb],
        smem=(0, 1),
    )
    got = exchange(ways.reshape(8, 48, 384), Y).reshape(384, 384)
    unit_part = lax.dynamic_slice(rows, (0, half * (2 * t_index + h_index)), (48, half))
    pool, loss = kernel_call(
        back_kernel,
        [((128, 768), BF), ((8, 128), F32)],
        [place, got, unit_part, w, w_first, w_second],
        smem=(0,),
    )
    mean_loss = loss[0, :1]
    pool = exchange(pool.reshape(8, 16, 768), Y).reshape(128, 768)
    count_i, width_i = image_in.shape[1:]
    count_t, width_t = text_in.shape[1:]
    img_own = lax.dynamic_slice_in_dim(image_in, 3 * t_index, 3, 0).reshape(-1, width_i)
    txt_own = lax.dynamic_slice_in_dim(text_in, 3 * t_index, 3, 0).reshape(-1, width_t)
    img_grads, txt_grads = kernel_call(
        token_kernel,
        [(img_own.shape, BF), (txt_own.shape, BF)],
        [pool, inv, img_own, txt_own, img_gain, txt_gain],
    )
    img_grads = img_grads.reshape(3, count_i, width_i)
    txt_grads = txt_grads.reshape(3, count_t, width_t)
    return (mean_loss, img_grads[None], txt_grads[None])


def solution(mesh):
    fine = Mesh(mesh.devices.reshape(4, 2, 8, 4, 2), ("t", "h", "z", "x", "c"))
    in_specs = (
        P(DP, None, None),
        P(DP, None, None),
        P(DP, None),
        P(DP, None),
        P(),
        P(),
        P(),
        P(DP),
    )
    out_specs = (P(), P("t", DP, None, None), P("t", DP, None, None))
    return jax.shard_map(
        per_device, mesh=fine, in_specs=in_specs, out_specs=out_specs, check_vma=False
    )
```

```python
import functools

import jax
import jax.numpy as jnp
from jax import lax
from jax.experimental import pallas as pl
from jax.experimental.pallas import tpu as pltpu
from jax.sharding import Mesh, PartitionSpec as P

BF = jnp.bfloat16
F32 = jnp.float32
Y = ("h", "t")
ZX = ("z", "x")
ZXC = ("z", "x", "c")
DP = ("h", "z", "x", "c")
LOW = -1e30
ROWS_DOT = (((1,), (1,)), ((), ()))


def exchange(blocks, axes):
    return lax.all_to_all(blocks, axes, 0, 0, tiled=True)


def both_cores(blocks):
    half = blocks.shape[0] // 2
    parts = [lax.all_gather(part, "c", axis=0) for part in (blocks[:half], blocks[half:])]
    return [part.reshape(-1, blocks.shape[2]) for part in parts]


def kernel_call(body, outs, args, scratch=(), smem=()):
    vmem = pl.BlockSpec(memory_space=pltpu.VMEM)
    return pl.pallas_call(
        body,
        out_shape=[jax.ShapeDtypeStruct(shape, kind) for shape, kind in outs],
        in_specs=[
            pl.BlockSpec(memory_space=pltpu.SMEM) if k in smem else vmem for k in range(len(args))
        ],
        out_specs=[vmem] * len(outs),
        scratch_shapes=list(scratch),
        compiler_params=pltpu.CompilerParams(vmem_limit_bytes=40 * 1024 * 1024),
    )(*args)


def slab_place(dense, wide, skip):
    row = skip + dense % wide
    return (row // 8) * 256 + ((dense // wide) % 2) * 128 + (dense // (2 * wide)) * 8 + row % 8


def slab_row(shape):
    lane = lax.broadcasted_iota(jnp.int32, shape, 1)
    return (lane // 256) * 8 + lane % 8


def pool_kernel(
    place_ref,
    pos_ref,
    img_ref,
    txt_ref,
    ig_ref,
    tg_ref,
    mine_ref,
    theirs_ref,
    img_held,
    txt_held,
    img_rows,
    txt_rows,
    digits,
    sems,
):
    steps = img_ref.shape[0] // 2

    def copies(k):
        span = pl.ds(2 * k, 2)
        return (
            pltpu.make_async_copy(img_ref.at[span], img_held.at[span], sems.at[0, k]),
            pltpu.make_async_copy(txt_ref.at[span], txt_held.at[span], sems.at[1, k]),
        )

    for k in range(steps):
        for copy in copies(k):
            copy.start()
    for rows in (img_rows, txt_rows, digits):
        rows[...] = jnp.zeros_like(rows)
    spot = lax.broadcasted_iota(jnp.int32, (1, 128), 1)

    def two_pairs(k, carry):
        for copy in copies(k):
            copy.wait()
        for held, gain_ref, rows in ((img_held, ig_ref, img_rows), (txt_held, tg_ref, txt_rows)):
            values = held[pl.ds(2 * k, 2)].astype(F32)
            center = values - jnp.mean(values, axis=2, keepdims=True)
            spread = jnp.mean(center * center, axis=2, keepdims=True)
            mean = jnp.mean(center * lax.rsqrt(spread + 1e-05), axis=1)
            for b in range(2):
                rows[pl.ds(2 * k + b, 1), :] = mean[b : b + 1] * gain_ref[...][None]
        for b in range(2):
            place = pos_ref[2 * k + b]
            line = jnp.where(spot == 7, place // 32, jnp.where(spot == 15, place % 32, 0))
            digits[pl.ds(2 * k + b, 1), :] = line.astype(F32)
        return carry

    lax.fori_loop(0, steps, two_pairs, 0)
    found = jnp.zeros((64, 768), F32)
    lane = lax.broadcasted_iota(jnp.int32, (1, 768), 1)
    slab = (lane % 128) // 8 * 2 + (lane // 128) % 2
    for rows, wide, skip in ((img_rows, 13, 0), (txt_rows, 10, 13)):
        width = 32 * wide
        row = slab_row((1, 768)) - skip
        wanted = jnp.where((row >= 0) & (row < wide), slab * wide + row, -1)
        dense = lax.broadcasted_iota(jnp.int32, (width, 768), 0)
        pick = jnp.where(dense == wanted, 1.0, 0.0).astype(BF)
        held = rows[...]
        quarters = [held[:, width * k : width * k + width] for k in range(4)]
        quarters = jnp.concatenate(quarters, 0).astype(BF)
        found += jnp.dot(quarters, pick, preferred_element_type=F32)
    line = digits[...]
    blank = jnp.zeros_like(line)
    line = jnp.concatenate([line, blank, line, blank], 0)
    found = jnp.concatenate([found[:, :512], found[:, 512:640] + line, found[:, 640:]], 1)
    first = place_ref[1] == 0
    mine_ref[...] = jnp.where(first, found[:32], found[32:]).astype(BF)
    theirs_ref[...] = jnp.where(first, found[32:], found[:32]).astype(BF)


def pool_call(place, image_in, text_in, img_gain, txt_gain, positive):
    pairs, _, width_i = image_in.shape
    width_t = text_in.shape[2]
    vmem = pl.BlockSpec(memory_space=pltpu.VMEM)
    smem = pl.BlockSpec(memory_space=pltpu.SMEM)
    whole = pl.BlockSpec(memory_space=pl.ANY)
    return pl.pallas_call(
        pool_kernel,
        out_shape=[jax.ShapeDtypeStruct((32, 768), BF)] * 2,
        in_specs=[smem, smem, whole, whole, vmem, vmem],
        out_specs=[vmem, vmem],
        scratch_shapes=[
            pltpu.VMEM(image_in.shape, BF),
            pltpu.VMEM(text_in.shape, BF),
            pltpu.VMEM((16, width_i), F32),
            pltpu.VMEM((16, width_t), F32),
            pltpu.VMEM((16, 128), F32),
            pltpu.SemaphoreType.DMA((2, pairs // 2)),
        ],
        cost_estimate=pl.CostEstimate(
            flops=10 * (image_in.size + text_in.size),
            bytes_accessed=2 * (image_in.size + text_in.size),
            transcendentals=0,
        ),
        compiler_params=pltpu.CompilerParams(vmem_limit_bytes=60 * 1024 * 1024),
    )(place, positive, image_in, text_in, img_gain, txt_gain)


def weight_quarter(w_ref, a):
    return jnp.concatenate([w_ref[k + 128 * a : k + 128 * a + 128, :] for k in (0, 256)], 0)


def project_kernel(place_ref, mine_ref, theirs_ref, w_ref, out_ref):
    width = w_ref.shape[1] // 3
    part = jnp.zeros((48, width), F32)
    inside = slab_row((12, 768))
    for a in range(2):
        pieces = []
        for h in range(2):
            rows = jnp.where(
                place_ref[1] == h,
                mine_ref[16 * a : 16 * a + 16, :].astype(F32),
                theirs_ref[32 * h + 16 * a : 32 * h + 16 * a + 16, :].astype(F32),
            )[:12]
            img_rows = jnp.where(inside < 13, rows, 0.0)
            txt_rows = jnp.where((inside >= 13) & (inside < 23), rows, 0.0)
            for t in range(4):
                pieces += [img_rows[3 * t : 3 * t + 3], txt_rows[3 * t : 3 * t + 3]]
        left = jnp.concatenate(pieces, 0).astype(BF)
        quarter = weight_quarter(w_ref, a)
        for j in range(3):
            part += jnp.dot(
                left[:, 256 * j : 256 * j + 256],
                quarter[:, width * j : width * j + width],
                preferred_element_type=F32,
            )
    packed = jnp.concatenate([part[:24], part[24:]], 1)
    out_ref[...] = jnp.concatenate([packed] * 8, 0).astype(BF)


def in_blocks(values):
    blank = jnp.zeros((1, values.shape[1]), F32)
    pieces = []
    for k in range(8):
        pieces += [values[6 * k : 6 * k + 3], blank, values[6 * k + 3 : 6 * k + 6], blank]
    return jnp.concatenate(pieces, 0)


def unit_kernel(place_ref, parts_ref, digits_ref, rows_ref, far_ref, inv_ref, held, held_inv):
    spread = parts_ref[...].astype(F32)
    width = spread.shape[1] // 2
    blocks = [spread[24 * k : 24 * k + 24] + spread[96 + 24 * k : 120 + 24 * k] for k in range(4)]
    blocks = [jnp.concatenate([part[:, :width], part[:, width:]], 0) for part in blocks]
    projected = jnp.concatenate(blocks, 1)
    inv = lax.rsqrt(jnp.sum(projected * projected, axis=1, keepdims=True) + 1e-06)
    unit = projected * inv
    rows_ref[...] = unit.astype(BF)
    held[...] = in_blocks(unit)
    held_inv[...] = in_blocks(jnp.broadcast_to(inv, (48, 128)))
    own = pl.ds(pl.multiple_of(8 * place_ref[0], 8), 8)
    inv_ref[...] = held_inv[own, :]
    block = held[own, :]
    free = jnp.concatenate([digits_ref[...], jnp.zeros((1, 128), F32)], 1)
    pieces = []
    for k in (0, 4):
        ends = [block[k + q : k + q + 1, 1024:] for q in range(3)]
        pieces += [block[k : k + 3, :1024], jnp.concatenate(ends + [free], 1)]
    block = jnp.concatenate(pieces, 0)
    block = jnp.concatenate([block, block], 0).astype(BF)
    for k in range(16):
        far_ref[16 * k : 16 * k + 16, :] = block


def tile_masks(place_ref):
    h, t, g = place_ref[1], place_ref[2], place_ref[3]
    row = lax.broadcasted_iota(jnp.int32, (48, 1), 0)
    item = lax.broadcasted_iota(jnp.int32, (1, 512), 1)
    item_g = ((item // 256) * 16 + (item % 128) // 8) * 2 + (item // 128) % 2
    item_pair = (h * 64 + item_g) * 12 + 3 * t + item % 4
    row_pair = ((row // 24) * 64 + g) * 12 + ((row // 6) % 4) * 3 + row % 3
    row_txt = (row % 6) // 3
    item_txt = jnp.where(item % 4 < 3, (item % 8) // 4, -1)
    valid = item_txt == 1 - row_txt
    return valid, row_pair, item_pair, row_txt, item_txt


def log_total(values, axis):
    largest = jnp.max(values, axis=axis, keepdims=True)
    return largest + jnp.log(jnp.sum(jnp.exp(values - largest), axis=axis, keepdims=True))


def score_kernel(place_ref, logit_ref, rows_ref, fa_ref, fb_ref, row_pos_ref, scores_ref, far_ref):
    rows = rows_ref[...]
    ends = rows[:, 1024:]
    blank = jnp.zeros_like(ends)
    ends = [[ends if k == q else blank for k in range(3)] for q in range(3)]
    ends = jnp.concatenate([jnp.concatenate(line, 1) for line in ends], 0)

    def dots(left, width):
        return jnp.concatenate(
            [
                lax.dot_general(left, ref[:, :width], ROWS_DOT, preferred_element_type=F32)
                for ref in (fa_ref, fb_ref)
            ],
            1,
        )

    scores = dots(rows[:, :1024], 1024)
    ends = dots(ends, 768)
    lane = lax.broadcasted_iota(jnp.int32, (48, 512), 1) % 4
    for q in range(3):
        moved = pltpu.roll(ends[48 * q : 48 * q + 48], 512 - (3 - q), 1)
        scores += jnp.where(lane == q, moved, 0.0)
    scores = logit_ref[0] * scores
    scores_ref[...] = scores
    valid, _, item_pair, row_txt, item_txt = tile_masks(place_ref)
    masked = jnp.where(valid, scores, LOW)
    item_part = log_total(masked, 0)
    hit = jnp.where(item_txt == 1, item_pair, -1) == jnp.where(row_txt == 0, row_pos_ref[...], -2)
    matched = jnp.sum(
        jnp.sum(jnp.where(hit, scores, 0.0), axis=1, keepdims=True), axis=0, keepdims=True
    )
    lane = lax.broadcasted_iota(jnp.int32, (1, 512), 1)
    item_part = jnp.where(lane == 3, matched, item_part)
    lines = jnp.concatenate([item_part[:, 128 * k : 128 * k + 128] for k in range(4)] * 2, 0)
    for k in range(32):
        far_ref[8 * k : 8 * k + 8, :] = lines


def in_parts(values, count):
    parts = []
    for _ in range(count):
        part = values.astype(BF).astype(F32)
        parts.append(part)
        values = values - part
    return parts


def times_items(left, fa_ref, fb_ref):
    def times(part, columns):
        return jnp.dot(part[:, :256], fa_ref[:, columns], preferred_element_type=F32) + jnp.dot(
            part[:, 256:], fb_ref[:, columns], preferred_element_type=F32
        )

    start = times(left, slice(0, 1024))
    last = lax.broadcasted_iota(jnp.int32, left.shape, 1) % 4 == 3
    wide = left.astype(F32)
    ends = jnp.zeros((left.shape[0], 256), F32)
    for q in range(3):
        moved = jnp.where(last, pltpu.roll(wide, 3 - q, 1), 0.0).astype(BF)
        ends += times(moved, slice(256 * q, 256 * q + 256))
    return jnp.concatenate([start, ends], 1)


def coef_kernel(
    place_ref, logit_ref, scores_ref, far_ref, row_pos_ref, item_pos_ref, fa_ref, fb_ref, out_ref
):
    logit = logit_ref[0]
    scores = scores_ref[...]
    seen = far_ref[...].reshape(32, 8, 128)
    largest = jnp.max(seen, axis=0)
    largest = jnp.maximum(largest[:4], largest[4:])
    both = jnp.concatenate([largest, largest], 0)
    total = jnp.sum(jnp.exp(seen - both[None]), axis=0)
    lines = largest + jnp.log(total[:4] + total[4:])
    item_lse = jnp.concatenate([lines[k : k + 1] for k in range(4)], 1)
    summed = jnp.sum(seen, axis=0)
    summed = summed[:1] + summed[4:5]
    valid, row_pair, item_pair, row_txt, item_txt = tile_masks(place_ref)
    img_hit = jnp.where(item_txt == 1, item_pair, -1) == jnp.where(
        row_txt == 0, row_pos_ref[...], -2
    )
    txt_hit = jnp.where(item_txt == 0, item_pos_ref[...], -1) == jnp.where(
        row_txt == 1, row_pair, -2
    )
    twice = jnp.where(img_hit, 2.0, jnp.where(txt_hit, 2.0, 0.0))
    lse_total = jnp.sum(jnp.where(item_txt >= 0, item_lse, 0.0), axis=1, keepdims=True)
    lane = lax.broadcasted_iota(jnp.int32, (1, 128), 1)
    matched = jnp.sum(jnp.where(lane == 3, summed, 0.0), axis=1, keepdims=True)
    value = lse_total - 2.0 * matched
    masked = jnp.where(valid, scores, LOW)
    row_part = log_total(masked, 1)
    by_row = (0.5 * logit) * jnp.exp(masked - row_part)
    by_item = (0.5 * logit) * (jnp.exp(masked - item_lse) - twice)
    coefs = [jnp.where(valid, part, 0.0).astype(BF) for part in (by_row, by_item)]
    along = [
        jnp.sum(part.astype(F32) * scores, axis=1, keepdims=True) / logit for part in coefs
    ]
    cot = times_items(jnp.concatenate(coefs, 0), fa_ref, fb_ref)
    riders = (
        in_parts(row_part, 3)
        + in_parts(along[0], 2)
        + in_parts(along[1], 2)
        + in_parts(jnp.broadcast_to(value, (48, 1)), 2)
    )
    column = lax.broadcasted_iota(jnp.int32, (48, 64), 1)
    extra = jnp.zeros((48, 64), F32)
    for k, rider in enumerate(riders):
        extra = jnp.where(column == k, rider, extra)
    width = cot.shape[1] // 8
    for k in range(8):
        first = width * (2 * (k % 4) + k // 4)
        part = cot[:, first : first + width]
        way = jnp.concatenate([part[:48], part[48:], extra], 1).astype(BF)
        out_ref[48 * k : 48 * k + 48, :] = way


def back_kernel(place_ref, got_ref, unit_ref, w_ref, other_ref, out_ref, loss_ref):
    width = unit_ref.shape[1]
    got = [got_ref[48 * k : 48 * k + 48, :].astype(F32) for k in range(8)]
    riders = [[part[:, 2 * width + k : 2 * width + k + 1] for k in range(9)] for part in got]
    parts = [r[0] + r[1] + r[2] for r in riders]
    largest = functools.reduce(jnp.maximum, parts)
    total = sum(jnp.exp(part - largest) for part in parts)
    lse = largest + jnp.log(total)
    along = jnp.zeros((48, 1), F32)
    value = jnp.zeros((48, 1), F32)
    summed = jnp.zeros((48, width), F32)
    for part, r, own in zip(got, riders, parts):
        weight = jnp.exp(own - lse)
        along += weight * (r[3] + r[4]) + (r[5] + r[6])
        value += r[7] + r[8]
        summed += weight * part[:, :width] + part[:, width : 2 * width]
    loss_ref[...] = jnp.broadcast_to(value[:8] / (2.0 * 1536), (8, 128))
    proj_cot = (summed - unit_ref[...].astype(F32) * along).astype(BF)
    is_img = slab_row((48, 768)) < 13
    first = place_ref[1] == 0

    def features(columns):
        pool = [
            lax.dot_general(proj_cot, part, ROWS_DOT, preferred_element_type=F32)
            for part in columns
        ]
        pool = jnp.concatenate(pool, 1)
        return jnp.where(is_img, pool, pltpu.roll(pool, 45, 0))

    own, other = [], []
    for a in range(2):
        quarter = weight_quarter(w_ref, a)
        columns = []
        for j in range(3):
            pair = quarter[:, 2 * width * j : 2 * width * j + 2 * width]
            columns.append(jnp.where(first, pair[:, :width], pair[:, width:]))
        own.append(features(columns))
        quarter = weight_quarter(other_ref, a)
        other.append(features([quarter[:, width * j : width * j + width] for j in range(3)]))
    mixed = [jnp.where(first, x, y) for x, y in zip(own + other, other + own)]
    blank = jnp.zeros((1, 768), F32)
    pieces = []
    for k in range(8):
        for pool in mixed:
            pieces += [pool[6 * k : 6 * k + 3], blank]
    out_ref[...] = jnp.concatenate(pieces, 0).astype(BF)


def token_kernel(pool_ref, inv_ref, img_ref, txt_ref, ig_ref, tg_ref, img_out, txt_out):
    pool = pool_ref[...]
    inv = inv_ref[...][:, :1]
    for x_ref, gain_ref, out_ref, wide, skip, at in (
        (img_ref, ig_ref, img_out, 13, 0, 0),
        (txt_ref, tg_ref, txt_out, 10, 13, 4),
    ):
        dense = lax.broadcasted_iota(jnp.int32, (1, 32 * wide), 1)
        lane = lax.broadcasted_iota(jnp.int32, (768, 32 * wide), 0)
        pick = jnp.where(lane == slab_place(dense, wide, skip), 1.0, 0.0).astype(BF)
        found = jnp.dot(pool, pick, preferred_element_type=F32)
        found = sum(found[16 * k : 16 * k + 16] for k in range(8))
        cot = jnp.concatenate([found[4 * k : 4 * k + 4] for k in range(4)], 1)
        cot = cot * inv[at : at + 4] * gain_ref[...][None]
        mean_cot = jnp.mean(cot, axis=1, keepdims=True)
        count = x_ref.shape[0] // 3
        for q in range(3):
            span = slice(count * q, count * q + count)
            values = x_ref[span, :].astype(F32)
            center = values - jnp.mean(values, axis=1, keepdims=True)
            inner = lax.rsqrt(jnp.mean(center * center, axis=1, keepdims=True) + 1e-05)
            mine = cot[q : q + 1]
            along = jnp.mean(center * mine, axis=1, keepdims=True)
            out = inner * (mine - mean_cot[q : q + 1]) - center * (inner * inner * inner * along)
            out_ref[span, :] = out.astype(BF)


def per_device(image_in, text_in, proj_img, proj_txt, img_gain, txt_gain, logit_scale, positive):
    t_index = lax.axis_index("t")
    h_index = lax.axis_index("h")
    g_index = (lax.axis_index("z") * 4 + lax.axis_index("x")) * 2 + lax.axis_index("c")
    y_index = h_index * 4 + t_index
    place = jnp.stack([y_index, h_index, t_index, g_index]).astype(jnp.int32)
    emb = proj_img.shape[1]

    width = emb // 4
    w = jnp.concatenate([proj_img, proj_txt, jnp.zeros((1, emb), BF)], 0)
    w = lax.dynamic_slice(w, (0, width * t_index), (24, width))
    w = jnp.concatenate([w[:8], w[8:16], w[16:]], 1)
    w = jnp.broadcast_to(w[None], (32, 8, 3 * width))
    w = lax.all_gather(exchange(w, ZX), "c", axis=0).reshape(512, 3 * width)

    mine, theirs = pool_call(place, image_in, text_in, img_gain, txt_gain, positive)
    theirs = lax.all_gather(theirs, Y, axis=0, axis_index_groups=[[0, 6], [1, 7], [2, 4], [3, 5]])
    row_pos = theirs[:, :12, 519].astype(F32) * 32.0 + theirs[:, :12, 527].astype(F32)
    is_mine = lax.iota(jnp.int32, 2)[:, None] == h_index
    row_pos = jnp.where(is_mine, positive.astype(F32)[None], row_pos)
    row_pos = jnp.pad(row_pos.reshape(8, 3), ((0, 0), (0, 3)), constant_values=-1.0)
    row_pos = row_pos.reshape(48, 1).astype(jnp.int32)

    (part,) = kernel_call(
        project_kernel,
        [((192, 2 * width), BF)],
        [place, mine, theirs.reshape(64, 768), w],
        smem=(0,),
    )
    parts = exchange(part.reshape(8, 24, 2 * width), Y).reshape(192, 2 * width)

    own_digits = lax.dynamic_slice(positive, (3 * t_index,), (3,))
    own_digits = jnp.concatenate([own_digits // 32, own_digits % 32]).astype(F32)
    own_digits = jnp.pad(own_digits, (0, 122))[None]
    rows, far, inv = kernel_call(
        unit_kernel,
        [((48, emb), BF), ((256, 1024), BF), ((8, 128), F32)],
        [place, parts, own_digits],
        scratch=[pltpu.VMEM((64, emb), F32), pltpu.VMEM((64, 128), F32)],
        smem=(0,),
    )
    half = width // 2
    w_held, far = lax.optimization_barrier((w, far))
    parts = w_held.reshape(512, 3, 2, half)
    w_other = jnp.where(h_index == 0, parts[:, :, 1], parts[:, :, 0]).reshape(512, 3 * half)
    w_other = lax.ppermute(w_other, "h", [(0, 1), (1, 0)])
    fa, fb = both_cores(exchange(far.reshape(32, 8, 1024), ZX))

    scores, far = kernel_call(
        score_kernel,
        [((48, 512), F32), ((256, 128), F32)],
        [place, logit_scale, rows, fa, fb, row_pos],
        smem=(0, 1),
    )
    far = exchange(far.reshape(64, 4, 128), ZXC).reshape(256, 128)
    far, w_other = lax.optimization_barrier((far, w_other))

    item_pos = jnp.concatenate([fa.reshape(32, 8, 1024)[:, 3, 768:774], fb.reshape(32, 8, 1024)[:, 3, 768:774]])
    item_pos = item_pos.astype(F32)
    item_pos = item_pos[:, :3] * 32.0 + item_pos[:, 3:]
    item_pos = jnp.pad(item_pos, ((0, 0), (0, 5)), constant_values=-1.0).reshape(1, 512)
    item_pos = item_pos.astype(jnp.int32)
    (ways,) = kernel_call(
        coef_kernel,
        [((384, 384), BF)],
        [place, logit_scale, scores, far, row_pos, item_pos, fa, fb],
        smem=(0, 1),
    )
    got = exchange(ways.reshape(8, 48, 384), Y).reshape(384, 384)
    unit_part = lax.dynamic_slice(rows, (0, half * (2 * t_index + h_index)), (48, half))
    pool, loss = kernel_call(
        back_kernel,
        [((128, 768), BF), ((8, 128), F32)],
        [place, got, unit_part, w, w_other],
        smem=(0,),
    )
    mean_loss = loss[0, :1]
    pool = exchange(pool.reshape(8, 16, 768), Y).reshape(128, 768)
    count_i, width_i = image_in.shape[1:]
    count_t, width_t = text_in.shape[1:]
    img_own = lax.dynamic_slice_in_dim(image_in, 3 * t_index, 3, 0).reshape(-1, width_i)
    txt_own = lax.dynamic_slice_in_dim(text_in, 3 * t_index, 3, 0).reshape(-1, width_t)
    img_grads, txt_grads = kernel_call(
        token_kernel,
        [(img_own.shape, BF), (txt_own.shape, BF)],
        [pool, inv, img_own, txt_own, img_gain, txt_gain],
    )
    img_grads = img_grads.reshape(3, count_i, width_i)
    txt_grads = txt_grads.reshape(3, count_t, width_t)
    return (mean_loss, img_grads[None], txt_grads[None])


def solution(mesh):
    fine = Mesh(mesh.devices.reshape(4, 2, 8, 4, 2), ("t", "h", "z", "x", "c"))
    in_specs = (
        P(DP, None, None),
        P(DP, None, None),
        P(DP, None),
        P(DP, None),
        P(),
        P(),
        P(),
        P(DP),
    )
    out_specs = (P(), P("t", DP, None, None), P("t", DP, None, None))
    return jax.shard_map(
        per_device, mesh=fine, in_specs=in_specs, out_specs=out_specs, check_vma=False
    )
```

```python
import functools

import jax
import jax.numpy as jnp
from jax import lax
from jax.experimental import pallas as pl
from jax.experimental.pallas import tpu as pltpu
from jax.sharding import Mesh, PartitionSpec as P

BF = jnp.bfloat16
F32 = jnp.float32
Y = ("h", "t")
ZX = ("z", "x")
ZXC = ("z", "x", "c")
DP = ("h", "z", "x", "c")
LOW = -1e30
ROWS_DOT = (((1,), (1,)), ((), ()))


def exchange(blocks, axes):
    return lax.all_to_all(blocks, axes, 0, 0, tiled=True)


def both_cores(blocks):
    half = blocks.shape[0] // 2
    parts = [lax.all_gather(part, "c", axis=0) for part in (blocks[:half], blocks[half:])]
    return [part.reshape(-1, blocks.shape[2]) for part in parts]


def kernel_call(body, outs, args, scratch=(), smem=()):
    vmem = pl.BlockSpec(memory_space=pltpu.VMEM)
    return pl.pallas_call(
        body,
        out_shape=[jax.ShapeDtypeStruct(shape, kind) for shape, kind in outs],
        in_specs=[
            pl.BlockSpec(memory_space=pltpu.SMEM) if k in smem else vmem for k in range(len(args))
        ],
        out_specs=[vmem] * len(outs),
        scratch_shapes=list(scratch),
        compiler_params=pltpu.CompilerParams(vmem_limit_bytes=40 * 1024 * 1024),
    )(*args)


def slab_place(dense, wide, skip):
    row = skip + dense % wide
    return (row // 8) * 256 + ((dense // wide) % 2) * 128 + (dense // (2 * wide)) * 8 + row % 8


def slab_row(shape):
    lane = lax.broadcasted_iota(jnp.int32, shape, 1)
    return (lane // 256) * 8 + lane % 8


def pool_kernel(
    h_ref,
    pos_ref,
    img_ref,
    txt_ref,
    ig_ref,
    tg_ref,
    mine_ref,
    theirs_ref,
    img_held,
    txt_held,
    img_rows,
    txt_rows,
    digits,
    sems,
):
    steps = img_ref.shape[0] // 2

    def copies(k):
        span = pl.ds(2 * k, 2)
        return (
            pltpu.make_async_copy(img_ref.at[span], img_held.at[span], sems.at[0, k]),
            pltpu.make_async_copy(txt_ref.at[span], txt_held.at[span], sems.at[1, k]),
        )

    for k in range(steps):
        for copy in copies(k):
            copy.start()
    for rows in (img_rows, txt_rows, digits):
        rows[...] = jnp.zeros_like(rows)
    spot = lax.broadcasted_iota(jnp.int32, (1, 128), 1)

    def two_pairs(k, carry):
        for copy in copies(k):
            copy.wait()
        for held, gain_ref, rows in ((img_held, ig_ref, img_rows), (txt_held, tg_ref, txt_rows)):
            values = held[pl.ds(2 * k, 2)].astype(F32)
            center = values - jnp.mean(values, axis=2, keepdims=True)
            spread = jnp.mean(center * center, axis=2, keepdims=True)
            mean = jnp.mean(center * lax.rsqrt(spread + 1e-05), axis=1)
            for b in range(2):
                rows[pl.ds(2 * k + b, 1), :] = mean[b : b + 1] * gain_ref[...][None]
        for b in range(2):
            place = pos_ref[2 * k + b]
            line = jnp.where(spot == 7, place // 32, jnp.where(spot == 15, place % 32, 0))
            digits[pl.ds(2 * k + b, 1), :] = line.astype(F32)
        return carry

    lax.fori_loop(0, steps, two_pairs, 0)
    found = jnp.zeros((64, 768), F32)
    lane = lax.broadcasted_iota(jnp.int32, (1, 768), 1)
    slab = (lane % 128) // 8 * 2 + (lane // 128) % 2
    for rows, wide, skip in ((img_rows, 13, 0), (txt_rows, 10, 13)):
        width = 32 * wide
        row = slab_row((1, 768)) - skip
        wanted = jnp.where((row >= 0) & (row < wide), slab * wide + row, -1)
        dense = lax.broadcasted_iota(jnp.int32, (width, 768), 0)
        pick = jnp.where(dense == wanted, 1.0, 0.0).astype(BF)
        held = rows[...]
        quarters = [held[:, width * k : width * k + width] for k in range(4)]
        quarters = jnp.concatenate(quarters, 0).astype(BF)
        found += jnp.dot(quarters, pick, preferred_element_type=F32)
    line = digits[...]
    blank = jnp.zeros_like(line)
    line = jnp.concatenate([line, blank, line, blank], 0)
    found = jnp.concatenate([found[:, :512], found[:, 512:640] + line, found[:, 640:]], 1)
    first = h_ref[0] == 0
    mine_ref[...] = jnp.where(first, found[:32], found[32:]).astype(BF)
    theirs_ref[...] = jnp.where(first, found[32:], found[:32]).astype(BF)


def pool_call(h_index, image_in, text_in, img_gain, txt_gain, positive):
    pairs, _, width_i = image_in.shape
    width_t = text_in.shape[2]
    vmem = pl.BlockSpec(memory_space=pltpu.VMEM)
    smem = pl.BlockSpec(memory_space=pltpu.SMEM)
    whole = pl.BlockSpec(memory_space=pl.ANY)
    return pl.pallas_call(
        pool_kernel,
        out_shape=[jax.ShapeDtypeStruct((32, 768), BF)] * 2,
        in_specs=[smem, smem, whole, whole, vmem, vmem],
        out_specs=[vmem, vmem],
        scratch_shapes=[
            pltpu.VMEM(image_in.shape, BF),
            pltpu.VMEM(text_in.shape, BF),
            pltpu.VMEM((16, width_i), F32),
            pltpu.VMEM((16, width_t), F32),
            pltpu.VMEM((16, 128), F32),
            pltpu.SemaphoreType.DMA((2, pairs // 2)),
        ],
        cost_estimate=pl.CostEstimate(
            flops=10 * (image_in.size + text_in.size),
            bytes_accessed=2 * (image_in.size + text_in.size),
            transcendentals=0,
        ),
        compiler_params=pltpu.CompilerParams(vmem_limit_bytes=60 * 1024 * 1024),
    )(h_index.astype(jnp.int32).reshape(1), positive, image_in, text_in, img_gain, txt_gain)


def weight_quarter(w_ref, a):
    return jnp.concatenate([w_ref[k + 128 * a : k + 128 * a + 128, :] for k in (0, 256)], 0)


def project_kernel(place_ref, mine_ref, theirs_ref, w_ref, out_ref):
    width = w_ref.shape[1] // 3
    part = jnp.zeros((48, width), F32)
    inside = slab_row((12, 768))
    for a in range(2):
        pieces = []
        for h in range(2):
            rows = jnp.where(
                place_ref[1] == h,
                mine_ref[16 * a : 16 * a + 16, :].astype(F32),
                theirs_ref[32 * h + 16 * a : 32 * h + 16 * a + 16, :].astype(F32),
            )[:12]
            img_rows = jnp.where(inside < 13, rows, 0.0)
            txt_rows = jnp.where((inside >= 13) & (inside < 23), rows, 0.0)
            for t in range(4):
                pieces += [img_rows[3 * t : 3 * t + 3], txt_rows[3 * t : 3 * t + 3]]
        left = jnp.concatenate(pieces, 0).astype(BF)
        quarter = weight_quarter(w_ref, a)
        for j in range(3):
            part += jnp.dot(
                left[:, 256 * j : 256 * j + 256],
                quarter[:, width * j : width * j + width],
                preferred_element_type=F32,
            )
    packed = jnp.concatenate([part[:24], part[24:]], 1)
    out_ref[...] = jnp.concatenate([packed] * 8, 0).astype(BF)


def in_blocks(values):
    blank = jnp.zeros((1, values.shape[1]), F32)
    pieces = []
    for k in range(8):
        pieces += [values[6 * k : 6 * k + 3], blank, values[6 * k + 3 : 6 * k + 6], blank]
    return jnp.concatenate(pieces, 0)


def unit_kernel(place_ref, parts_ref, digits_ref, rows_ref, far_ref, inv_ref, held, held_inv):
    spread = parts_ref[...].astype(F32)
    width = spread.shape[1] // 2
    blocks = [spread[24 * k : 24 * k + 24] + spread[96 + 24 * k : 120 + 24 * k] for k in range(4)]
    blocks = [jnp.concatenate([part[:, :width], part[:, width:]], 0) for part in blocks]
    projected = jnp.concatenate(blocks, 1)
    inv = lax.rsqrt(jnp.sum(projected * projected, axis=1, keepdims=True) + 1e-06)
    unit = projected * inv
    rows_ref[...] = unit.astype(BF)
    held[...] = in_blocks(unit)
    held_inv[...] = in_blocks(jnp.broadcast_to(inv, (48, 128)))
    own = pl.ds(pl.multiple_of(8 * place_ref[0], 8), 8)
    inv_ref[...] = held_inv[own, :]
    block = held[own, :]
    free = jnp.concatenate([digits_ref[...], jnp.zeros((1, 128), F32)], 1)
    pieces = []
    for k in (0, 4):
        ends = [block[k + q : k + q + 1, 1024:] for q in range(3)]
        pieces += [block[k : k + 3, :1024], jnp.concatenate(ends + [free], 1)]
    block = jnp.concatenate(pieces, 0)
    block = jnp.concatenate([block, block], 0).astype(BF)
    for k in range(16):
        far_ref[16 * k : 16 * k + 16, :] = block


def tile_masks(place_ref):
    h, t, g = place_ref[1], place_ref[2], place_ref[3]
    row = lax.broadcasted_iota(jnp.int32, (48, 1), 0)
    item = lax.broadcasted_iota(jnp.int32, (1, 512), 1)
    item_g = ((item // 256) * 16 + (item % 128) // 8) * 2 + (item // 128) % 2
    item_pair = (h * 64 + item_g) * 12 + 3 * t + item % 4
    row_pair = ((row // 24) * 64 + g) * 12 + ((row // 6) % 4) * 3 + row % 3
    row_txt = (row % 6) // 3
    item_txt = jnp.where(item % 4 < 3, (item % 8) // 4, -1)
    valid = item_txt == 1 - row_txt
    return valid, row_pair, item_pair, row_txt, item_txt


def log_total(values, axis):
    largest = jnp.max(values, axis=axis, keepdims=True)
    return largest + jnp.log(jnp.sum(jnp.exp(values - largest), axis=axis, keepdims=True))


def score_kernel(place_ref, logit_ref, rows_ref, fa_ref, fb_ref, row_pos_ref, scores_ref, far_ref):
    rows = rows_ref[...]
    ends = rows[:, 1024:]
    blank = jnp.zeros_like(ends)
    ends = [[ends if k == q else blank for k in range(3)] for q in range(3)]
    ends = jnp.concatenate([jnp.concatenate(line, 1) for line in ends], 0)

    def dots(left, width):
        return jnp.concatenate(
            [
                lax.dot_general(left, ref[:, :width], ROWS_DOT, preferred_element_type=F32)
                for ref in (fa_ref, fb_ref)
            ],
            1,
        )

    scores = dots(rows[:, :1024], 1024)
    ends = dots(ends, 768)
    lane = lax.broadcasted_iota(jnp.int32, (48, 512), 1) % 4
    for q in range(3):
        moved = pltpu.roll(ends[48 * q : 48 * q + 48], 512 - (3 - q), 1)
        scores += jnp.where(lane == q, moved, 0.0)
    scores = logit_ref[0] * scores
    scores_ref[...] = scores
    valid, _, item_pair, row_txt, item_txt = tile_masks(place_ref)
    masked = jnp.where(valid, scores, LOW)
    item_part = log_total(masked, 0)
    hit = jnp.where(item_txt == 1, item_pair, -1) == jnp.where(row_txt == 0, row_pos_ref[...], -2)
    matched = jnp.sum(
        jnp.sum(jnp.where(hit, scores, 0.0), axis=1, keepdims=True), axis=0, keepdims=True
    )
    lane = lax.broadcasted_iota(jnp.int32, (1, 512), 1)
    item_part = jnp.where(lane == 3, matched, item_part)
    lines = jnp.concatenate([item_part[:, 128 * k : 128 * k + 128] for k in range(4)] * 2, 0)
    for k in range(32):
        far_ref[8 * k : 8 * k + 8, :] = lines


def in_parts(values, count):
    parts = []
    for _ in range(count):
        part = values.astype(BF).astype(F32)
        parts.append(part)
        values = values - part
    return parts


def times_items(left, fa_ref, fb_ref):
    def times(part, columns):
        return jnp.dot(part[:, :256], fa_ref[:, columns], preferred_element_type=F32) + jnp.dot(
            part[:, 256:], fb_ref[:, columns], preferred_element_type=F32
        )

    start = times(left, slice(0, 1024))
    last = lax.broadcasted_iota(jnp.int32, left.shape, 1) % 4 == 3
    wide = left.astype(F32)
    ends = jnp.zeros((left.shape[0], 256), F32)
    for q in range(3):
        moved = jnp.where(last, pltpu.roll(wide, 3 - q, 1), 0.0).astype(BF)
        ends += times(moved, slice(256 * q, 256 * q + 256))
    return jnp.concatenate([start, ends], 1)


def coef_kernel(
    place_ref, logit_ref, scores_ref, far_ref, row_pos_ref, item_pos_ref, fa_ref, fb_ref, out_ref
):
    logit = logit_ref[0]
    scores = scores_ref[...]
    seen = far_ref[...].reshape(32, 8, 128)
    largest = jnp.max(seen, axis=0)
    largest = jnp.maximum(largest[:4], largest[4:])
    both = jnp.concatenate([largest, largest], 0)
    total = jnp.sum(jnp.exp(seen - both[None]), axis=0)
    lines = largest + jnp.log(total[:4] + total[4:])
    item_lse = jnp.concatenate([lines[k : k + 1] for k in range(4)], 1)
    summed = jnp.sum(seen, axis=0)
    summed = summed[:1] + summed[4:5]
    valid, row_pair, item_pair, row_txt, item_txt = tile_masks(place_ref)
    img_hit = jnp.where(item_txt == 1, item_pair, -1) == jnp.where(
        row_txt == 0, row_pos_ref[...], -2
    )
    txt_hit = jnp.where(item_txt == 0, item_pos_ref[...], -1) == jnp.where(
        row_txt == 1, row_pair, -2
    )
    twice = jnp.where(img_hit, 2.0, jnp.where(txt_hit, 2.0, 0.0))
    lse_total = jnp.sum(jnp.where(item_txt >= 0, item_lse, 0.0), axis=1, keepdims=True)
    lane = lax.broadcasted_iota(jnp.int32, (1, 128), 1)
    matched = jnp.sum(jnp.where(lane == 3, summed, 0.0), axis=1, keepdims=True)
    value = lse_total - 2.0 * matched
    masked = jnp.where(valid, scores, LOW)
    row_part = log_total(masked, 1)
    by_row = (0.5 * logit) * jnp.exp(masked - row_part)
    by_item = (0.5 * logit) * (jnp.exp(masked - item_lse) - twice)
    coefs = [jnp.where(valid, part, 0.0).astype(BF) for part in (by_row, by_item)]
    along = [
        jnp.sum(part.astype(F32) * scores, axis=1, keepdims=True) / logit for part in coefs
    ]
    cot = times_items(jnp.concatenate(coefs, 0), fa_ref, fb_ref)
    riders = (
        in_parts(row_part, 3)
        + in_parts(along[0], 2)
        + in_parts(along[1], 2)
        + in_parts(jnp.broadcast_to(value, (48, 1)), 2)
    )
    column = lax.broadcasted_iota(jnp.int32, (48, 64), 1)
    extra = jnp.zeros((48, 64), F32)
    for k, rider in enumerate(riders):
        extra = jnp.where(column == k, rider, extra)
    width = cot.shape[1] // 8
    for k in range(8):
        first = width * (2 * (k % 4) + k // 4)
        part = cot[:, first : first + width]
        way = jnp.concatenate([part[:48], part[48:], extra], 1).astype(BF)
        out_ref[48 * k : 48 * k + 48, :] = way


def back_kernel(place_ref, got_ref, unit_ref, w_ref, other_ref, out_ref, loss_ref):
    width = unit_ref.shape[1]
    got = [got_ref[48 * k : 48 * k + 48, :].astype(F32) for k in range(8)]
    riders = [[part[:, 2 * width + k : 2 * width + k + 1] for k in range(9)] for part in got]
    parts = [r[0] + r[1] + r[2] for r in riders]
    largest = functools.reduce(jnp.maximum, parts)
    total = sum(jnp.exp(part - largest) for part in parts)
    lse = largest + jnp.log(total)
    along = jnp.zeros((48, 1), F32)
    value = jnp.zeros((48, 1), F32)
    summed = jnp.zeros((48, width), F32)
    for part, r, own in zip(got, riders, parts):
        weight = jnp.exp(own - lse)
        along += weight * (r[3] + r[4]) + (r[5] + r[6])
        value += r[7] + r[8]
        summed += weight * part[:, :width] + part[:, width : 2 * width]
    loss_ref[...] = jnp.broadcast_to(value[:8] / (2.0 * 1536), (8, 128))
    proj_cot = (summed - unit_ref[...].astype(F32) * along).astype(BF)
    is_img = slab_row((48, 768)) < 13
    first = place_ref[1] == 0

    def features(columns):
        pool = [
            lax.dot_general(proj_cot, part, ROWS_DOT, preferred_element_type=F32)
            for part in columns
        ]
        pool = jnp.concatenate(pool, 1)
        return jnp.where(is_img, pool, pltpu.roll(pool, 45, 0))

    own, other = [], []
    for out, ref in ((own, w_ref), (other, other_ref)):
        for a in range(2):
            quarter = weight_quarter(ref, a)
            out.append(features([quarter[:, width * j : width * j + width] for j in range(3)]))
    mixed = [jnp.where(first, x, y) for x, y in zip(own + other, other + own)]
    blank = jnp.zeros((1, 768), F32)
    pieces = []
    for k in range(8):
        for pool in mixed:
            pieces += [pool[6 * k : 6 * k + 3], blank]
    out_ref[...] = jnp.concatenate(pieces, 0).astype(BF)


def token_kernel(pool_ref, inv_ref, img_ref, txt_ref, ig_ref, tg_ref, img_out, txt_out):
    pool = pool_ref[...]
    inv = inv_ref[...][:, :1]
    for x_ref, gain_ref, out_ref, wide, skip, at in (
        (img_ref, ig_ref, img_out, 13, 0, 0),
        (txt_ref, tg_ref, txt_out, 10, 13, 4),
    ):
        dense = lax.broadcasted_iota(jnp.int32, (1, 32 * wide), 1)
        lane = lax.broadcasted_iota(jnp.int32, (768, 32 * wide), 0)
        pick = jnp.where(lane == slab_place(dense, wide, skip), 1.0, 0.0).astype(BF)
        found = jnp.dot(pool, pick, preferred_element_type=F32)
        found = sum(found[16 * k : 16 * k + 16] for k in range(8))
        cot = jnp.concatenate([found[4 * k : 4 * k + 4] for k in range(4)], 1)
        cot = cot * inv[at : at + 4] * gain_ref[...][None]
        mean_cot = jnp.mean(cot, axis=1, keepdims=True)
        count = x_ref.shape[0] // 3
        for q in range(3):
            span = slice(count * q, count * q + count)
            values = x_ref[span, :].astype(F32)
            center = values - jnp.mean(values, axis=1, keepdims=True)
            inner = lax.rsqrt(jnp.mean(center * center, axis=1, keepdims=True) + 1e-05)
            mine = cot[q : q + 1]
            along = jnp.mean(center * mine, axis=1, keepdims=True)
            out = inner * (mine - mean_cot[q : q + 1]) - center * (inner * inner * inner * along)
            out_ref[span, :] = out.astype(BF)


def per_device(image_in, text_in, proj_img, proj_txt, img_gain, txt_gain, logit_scale, positive):
    t_index = lax.axis_index("t")
    h_index = lax.axis_index("h")
    g_index = (lax.axis_index("z") * 4 + lax.axis_index("x")) * 2 + lax.axis_index("c")
    y_index = h_index * 4 + t_index
    place = jnp.stack([y_index, h_index, t_index, g_index]).astype(jnp.int32)
    emb = proj_img.shape[1]

    width = emb // 4
    w = jnp.concatenate([proj_img, proj_txt, jnp.zeros((1, emb), BF)], 0)
    w = lax.dynamic_slice(w, (0, width * t_index), (24, width))
    w = jnp.concatenate([w[:8], w[8:16], w[16:]], 1)
    w = jnp.broadcast_to(w[None], (32, 8, 3 * width))
    w = lax.all_gather(exchange(w, ZX), "c", axis=0).reshape(512, 3 * width)

    mine, theirs = pool_call(h_index, image_in, text_in, img_gain, txt_gain, positive)
    theirs = lax.all_gather(theirs, Y, axis=0, axis_index_groups=[[0, 6], [1, 7], [2, 4], [3, 5]])
    row_pos = theirs[:, :12, 519].astype(F32) * 32.0 + theirs[:, :12, 527].astype(F32)
    is_mine = lax.iota(jnp.int32, 2)[:, None] == h_index
    row_pos = jnp.where(is_mine, positive.astype(F32)[None], row_pos)
    row_pos = jnp.pad(row_pos.reshape(8, 3), ((0, 0), (0, 3)), constant_values=-1.0)
    row_pos = row_pos.reshape(48, 1).astype(jnp.int32)

    (part,) = kernel_call(
        project_kernel,
        [((192, 2 * width), BF)],
        [place, mine, theirs.reshape(64, 768), w],
        smem=(0,),
    )
    parts = exchange(part.reshape(8, 24, 2 * width), Y).reshape(192, 2 * width)

    own_digits = lax.dynamic_slice(positive, (3 * t_index,), (3,))
    own_digits = jnp.concatenate([own_digits // 32, own_digits % 32]).astype(F32)
    own_digits = jnp.pad(own_digits, (0, 122))[None]
    rows, far, inv = kernel_call(
        unit_kernel,
        [((48, emb), BF), ((256, 1024), BF), ((8, 128), F32)],
        [place, parts, own_digits],
        scratch=[pltpu.VMEM((64, emb), F32), pltpu.VMEM((64, 128), F32)],
        smem=(0,),
    )
    half = width // 2
    w_held, far = lax.optimization_barrier((w, far))
    parts = w_held.reshape(512, 3, 2, half)
    w_other = jnp.where(h_index == 0, parts[:, :, 1], parts[:, :, 0]).reshape(512, 3 * half)
    w_own = jnp.where(h_index == 0, parts[:, :, 0], parts[:, :, 1]).reshape(512, 3 * half)
    w_other = lax.ppermute(w_other, "h", [(0, 1), (1, 0)])
    fa, fb = both_cores(exchange(far.reshape(32, 8, 1024), ZX))

    scores, far = kernel_call(
        score_kernel,
        [((48, 512), F32), ((256, 128), F32)],
        [place, logit_scale, rows, fa, fb, row_pos],
        smem=(0, 1),
    )
    far = exchange(far.reshape(64, 4, 128), ZXC).reshape(256, 128)
    far, w_other = lax.optimization_barrier((far, w_other))

    item_pos = jnp.concatenate([fa.reshape(32, 8, 1024)[:, 3, 768:774], fb.reshape(32, 8, 1024)[:, 3, 768:774]])
    item_pos = item_pos.astype(F32)
    item_pos = item_pos[:, :3] * 32.0 + item_pos[:, 3:]
    item_pos = jnp.pad(item_pos, ((0, 0), (0, 5)), constant_values=-1.0).reshape(1, 512)
    item_pos = item_pos.astype(jnp.int32)
    (ways,) = kernel_call(
        coef_kernel,
        [((384, 384), BF)],
        [place, logit_scale, scores, far, row_pos, item_pos, fa, fb],
        smem=(0, 1),
    )
    got = exchange(ways.reshape(8, 48, 384), Y).reshape(384, 384)
    unit_part = lax.dynamic_slice(rows, (0, half * (2 * t_index + h_index)), (48, half))
    pool, loss = kernel_call(
        back_kernel,
        [((128, 768), BF), ((8, 128), F32)],
        [place, got, unit_part, w_own, w_other],
        smem=(0,),
    )
    mean_loss = loss[0, :1]
    pool = exchange(pool.reshape(8, 16, 768), Y).reshape(128, 768)
    count_i, width_i = image_in.shape[1:]
    count_t, width_t = text_in.shape[1:]
    img_own = lax.dynamic_slice_in_dim(image_in, 3 * t_index, 3, 0).reshape(-1, width_i)
    txt_own = lax.dynamic_slice_in_dim(text_in, 3 * t_index, 3, 0).reshape(-1, width_t)
    img_grads, txt_grads = kernel_call(
        token_kernel,
        [(img_own.shape, BF), (txt_own.shape, BF)],
        [pool, inv, img_own, txt_own, img_gain, txt_gain],
    )
    img_grads = img_grads.reshape(3, count_i, width_i)
    txt_grads = txt_grads.reshape(3, count_t, width_t)
    return (mean_loss, img_grads[None], txt_grads[None])


def solution(mesh):
    fine = Mesh(mesh.devices.reshape(4, 2, 8, 4, 2), ("t", "h", "z", "x", "c"))
    in_specs = (
        P(DP, None, None),
        P(DP, None, None),
        P(DP, None),
        P(DP, None),
        P(),
        P(),
        P(),
        P(DP),
    )
    out_specs = (P(), P("t", DP, None, None), P("t", DP, None, None))
    return jax.shard_map(
        per_device, mesh=fine, in_specs=in_specs, out_specs=out_specs, check_vma=False
    )
```
